32 devices in a mesh: dp: 16 (over z, y, x), hid: 2 (over core).
Axes of the slice: x: 2, y: 2, z: 4, core: 2. Of those that a mesh axis runs over, the one named last changes fastest.
Arguments:
- field_ids: int32 [32768, 26, 4], P('dp'), may hold values from 0 to 255
- bag_lengths: int32 [32768, 26], P('dp'), may hold values from 1 to 4
- dense_values: float32 [32768, 13], P('dp'), may hold values from -12 to 12
- labels: int32 [32768, 2], P('dp'), may hold values from 0 to 1
- tables: float32 [26, 256, 16], replicated, may hold values from -1.5 to 1.5
- tables_momentum: float32 [26, 256, 16], replicated, may hold values from -0.625 to 0.625
- tables_average: float32 [26, 256, 16], replicated, may hold values from -1.5 to 1.5
- in_weight: float32 [429, 512], replicated, may hold values from -0.3125 to 0.3125
- in_weight_momentum: float32 [429, 512], replicated, may hold values from -0.625 to 0.625
- in_weight_average: float32 [429, 512], replicated, may hold values from -0.3125 to 0.3125
- expert_up: float32 [4, 512, 256], P(None, None, 'hid'), may hold values from -0.25 to 0.25
- expert_up_momentum: float32 [4, 512, 256], P(None, None, 'hid'), may hold values from -0.625 to 0.625
- expert_up_average: float32 [4, 512, 256], P(None, None, 'hid'), may hold values from -0.25 to 0.25
- expert_down: float32 [4, 256, 128], P(None, 'hid'), may hold values from -0.375 to 0.375
- expert_down_momentum: float32 [4, 256, 128], P(None, 'hid'), may hold values from -0.625 to 0.625
- expert_down_average: float32 [4, 256, 128], P(None, 'hid'), may hold values from -0.375 to 0.375
- expert_up_bias: float32 [4, 256], P(None, 'hid'), may hold values from -0.625 to 0.625
- expert_up_bias_momentum: float32 [4, 256], P(None, 'hid'), may hold values from -0.625 to 0.625
- expert_up_bias_average: float32 [4, 256], P(None, 'hid'), may hold values from -0.625 to 0.625
- gate_weight: float32 [2, 512, 4], replicated, may hold values from -0.125 to 0.125
- gate_weight_momentum: float32 [2, 512, 4], replicated, may hold values from -0.625 to 0.625
- gate_weight_average: float32 [2, 512, 4], replicated, may hold values from -0.125 to 0.125
- tower_up: float32 [2, 128, 64], replicated, may hold values from -0.5 to 0.5
- tower_up_momentum: float32 [2, 128, 64], replicated, may hold values from -0.625 to 0.625
- tower_up_average: float32 [2, 128, 64], replicated, may hold values from -0.5 to 0.5
- tower_out: float32 [2, 64], replicated, may hold values from -0.75 to 0.75
- tower_out_momentum: float32 [2, 64], replicated, may hold values from -0.625 to 0.625
- tower_out_average: float32 [2, 64], replicated, may hold values from -0.75 to 0.75
- biases: float32 [1162], replicated, may hold values from -0.625 to 0.625
- biases_momentum: float32 [1162], replicated, may hold values from -0.625 to 0.625
- biases_average: float32 [1162], replicated, may hold values from -0.625 to 0.625
Outputs:
- new_tables: float32 [26, 256, 16], replicated
- new_tables_momentum: float32 [26, 256, 16], replicated
- new_tables_average: float32 [26, 256, 16], replicated
- tables_rounded: bfloat16 [26, 256, 16], replicated
- new_in_weight: float32 [429, 512], replicated
- new_in_weight_momentum: float32 [429, 512], replicated
- new_in_weight_average: float32 [429, 512], replicated
- in_weight_rounded: bfloat16 [429, 512], replicated
- new_expert_up: float32 [4, 512, 256], P(None, None, 'hid')
- new_expert_up_momentum: float32 [4, 512, 256], P(None, None, 'hid')
- new_expert_up_average: float32 [4, 512, 256], P(None, None, 'hid')
- expert_up_rounded: bfloat16 [4, 512, 256], P(None, None, 'hid')
- new_expert_down: float32 [4, 256, 128], P(None, 'hid')
- new_expert_down_momentum: float32 [4, 256, 128], P(None, 'hid')
- new_expert_down_average: float32 [4, 256, 128], P(None, 'hid')
- expert_down_rounded: bfloat16 [4, 256, 128], P(None, 'hid')
- new_expert_up_bias: float32 [4, 256], P(None, 'hid')
- new_expert_up_bias_momentum: float32 [4, 256], P(None, 'hid')
- new_expert_up_bias_average: float32 [4, 256], P(None, 'hid')
- expert_up_bias_rounded: bfloat16 [4, 256], P(None, 'hid')
- new_gate_weight: float32 [2, 512, 4], replicated
- new_gate_weight_momentum: float32 [2, 512, 4], replicated
- new_gate_weight_average: float32 [2, 512, 4], replicated
- gate_weight_rounded: bfloat16 [2, 512, 4], replicated
- new_tower_up: float32 [2, 128, 64], replicated
- new_tower_up_momentum: float32 [2, 128, 64], replicated
- new_tower_up_average: float32 [2, 128, 64], replicated
- tower_up_rounded: bfloat16 [2, 128, 64], replicated
- new_tower_out: float32 [2, 64], replicated
- new_tower_out_momentum: float32 [2, 64], replicated
- new_tower_out_average: float32 [2, 64], replicated
- tower_out_rounded: bfloat16 [2, 64], replicated
- new_biases: float32 [1162], replicated
- new_biases_momentum: float32 [1162], replicated
- new_biases_average: float32 [1162], replicated
- biases_rounded: bfloat16 [1162], replicated
- layer_rms: float32 [4], replicated
The draws below stay inside these ranges and needn't reach their ends.
All inputs are finite; a program needn't handle non-finite values.
Results may differ from the reference program's by a relative error of at most 0.001.
Values sent between devices are 32-bit elements; how exact they have to be, the bound alone decides.
A program may use at most 128 MiB of HBM per device.

```python
import math
import jax
import jax.numpy as jnp
import numpy as np
from jax import lax

D = 512
HID = 256
OUT = 128
TH = 64
EMB = 16
FIELDS = 26
DENSE = 13
TASKS = 2
VOCAB = 256
EXPERTS = 4
BAG = 4
TOTAL = 32768
IN_ROWS = 429
NB = 1162


def draw_dense_values(key, part):
    key = jax.random.fold_in(key, 11)
    position = jnp.arange(TOTAL, dtype=jnp.float32) / max(TOTAL - 1, 1)
    values = jnp.clip(jax.random.normal(key, (TOTAL, DENSE), jnp.float32), -4.0, 4.0)
    scales = 1.0 + 2.0 * position
    return (values * scales[:, None]).astype(jnp.float32)


def plant(drawn, stream_key, low, high):
    shape = drawn.shape
    place = [jax.random.randint(jax.random.fold_in(stream_key, axis), (), 0, shape[axis]) for axis in range(len(shape))]
    drawn = drawn.at[tuple(place)].set(low)
    longest = shape.index(max(shape))
    place[longest] = (place[longest] + 1) % shape[longest]
    return drawn.at[tuple(place)].set(high)


def shard_levels(key, shape, split, smallest, high):
    def one(dim, blocks):
        heights = jax.random.uniform(jax.random.fold_in(jax.random.fold_in(key, 6), dim), (blocks,), jnp.float32, smallest / len(split), high / len(split))
        return jnp.repeat(jnp.exp(heights), shape[dim] // blocks).reshape((-1,) + (1,) * (len(shape) - dim - 1))

    gain = one(*split[0])
    for cut in split[1:]:
        gain = gain * one(*cut)
    return gain


def rank_table(amount, lean):
    loads = [(1 << 20) // math.isqrt(grade ** lean) + 1 for grade in range(1, amount + 1)]
    spread = 1 + sum(loads) // (1 << 30)
    return np.cumsum(np.array([max(1, weight // spread) for weight in loads]))


def ranked(own_key, dims, number_of, lean):
    listing = rank_table(number_of, lean)
    lot = jax.random.randint(jax.random.fold_in(own_key, 1), dims, 0, int(listing[number_of - 1]))
    standing = jnp.searchsorted(jnp.asarray(listing, jnp.int32), lot, side="right")
    return jax.random.permutation(jax.random.fold_in(own_key, 2), number_of)[standing].astype(jnp.int32)


def centred(own_key, dims, width, reach, cuts=(), kind=jnp.bfloat16):
    values = width * jax.random.normal(own_key, dims, jnp.float32)
    if cuts:
        values = values * shard_levels(own_key, dims, cuts, -0.22, 0.18)
    return jnp.clip(values, -reach, reach).astype(kind)


def setup_inputs(seed: int = 0) -> dict:
    key_of = jax.random.split(jax.random.key(seed), 32)
    return {
        "field_ids": plant(ranked(key_of[0], (TOTAL, FIELDS, BAG), VOCAB, 2), jax.random.fold_in(key_of[0], 3), 0, VOCAB - 1).astype(jnp.int32),
        "bag_lengths": plant(jax.random.randint(key_of[1], (TOTAL, FIELDS), 1, BAG + 1), jax.random.fold_in(key_of[1], 1), 1, BAG).astype(jnp.int32),
        "dense_values": draw_dense_values(jax.random.fold_in(key_of[31], 71), 0),
        "labels": plant(jax.random.randint(key_of[3], (TOTAL, TASKS), 0, 2), jax.random.fold_in(key_of[3], 1), 0, 1).astype(jnp.int32),
        "tables": centred(key_of[4], (FIELDS, VOCAB, EMB), 0.25, 1.5, (), jnp.float32),
        "tables_momentum": centred(key_of[5], (FIELDS, VOCAB, EMB), 0.1, 0.625, (), jnp.float32),
        "tables_average": centred(key_of[6], (FIELDS, VOCAB, EMB), 0.25, 1.5, (), jnp.float32),
        "in_weight": centred(key_of[7], (IN_ROWS, D), IN_ROWS ** -0.5, 0.3125, (), jnp.float32),
        "in_weight_momentum": centred(key_of[8], (IN_ROWS, D), 0.1, 0.625, (), jnp.float32),
        "in_weight_average": centred(key_of[9], (IN_ROWS, D), IN_ROWS ** -0.5, 0.3125, (), jnp.float32),
        "expert_up": centred(key_of[10], (EXPERTS, D, HID), D ** -0.5, 0.25, ((2, 2),), jnp.float32),
        "expert_up_momentum": centred(key_of[11], (EXPERTS, D, HID), 0.1, 0.625, ((2, 2),), jnp.float32),
        "expert_up_average": centred(key_of[12], (EXPERTS, D, HID), D ** -0.5, 0.25, ((2, 2),), jnp.float32),
        "expert_down": centred(key_of[13], (EXPERTS, HID, OUT), HID ** -0.5, 0.375, ((1, 2),), jnp.float32),
        "expert_down_momentum": centred(key_of[14], (EXPERTS, HID, OUT), 0.1, 0.625, ((1, 2),), jnp.float32),
        "expert_down_average": centred(key_of[15], (EXPERTS, HID, OUT), HID ** -0.5, 0.375, ((1, 2),), jnp.float32),
        "expert_up_bias": centred(key_of[16], (EXPERTS, HID), 0.1, 0.625, ((1, 2),), jnp.float32),
        "expert_up_bias_momentum": centred(key_of[17], (EXPERTS, HID), 0.1, 0.625, ((1, 2),), jnp.float32),
        "expert_up_bias_average": centred(key_of[18], (EXPERTS, HID), 0.1, 0.625, ((1, 2),), jnp.float32),
        "gate_weight": centred(key_of[19], (TASKS, D, EXPERTS), (4 * D) ** -0.5, 0.125, (), jnp.float32),
        "gate_weight_momentum": centred(key_of[20], (TASKS, D, EXPERTS), 0.1, 0.625, (), jnp.float32),
        "gate_weight_average": centred(key_of[21], (TASKS, D, EXPERTS), (4 * D) ** -0.5, 0.125, (), jnp.float32),
        "tower_up": centred(key_of[22], (TASKS, OUT, TH), OUT ** -0.5, 0.5, (), jnp.float32),
        "tower_up_momentum": centred(key_of[23], (TASKS, OUT, TH), 0.1, 0.625, (), jnp.float32),
        "tower_up_average": centred(key_of[24], (TASKS, OUT, TH), OUT ** -0.5, 0.5, (), jnp.float32),
        "tower_out": centred(key_of[25], (TASKS, TH), TH ** -0.5, 0.75, (), jnp.float32),
        "tower_out_momentum": centred(key_of[26], (TASKS, TH), 0.1, 0.625, (), jnp.float32),
        "tower_out_average": centred(key_of[27], (TASKS, TH), TH ** -0.5, 0.75, (), jnp.float32),
        "biases": centred(key_of[28], (NB,), 0.1, 0.625, (), jnp.float32),
        "biases_momentum": centred(key_of[29], (NB,), 0.1, 0.625, (), jnp.float32),
        "biases_average": centred(key_of[30], (NB,), 0.1, 0.625, (), jnp.float32),
    }


HIGH = lax.Precision.HIGHEST
MOMENTUM_RATE = 0.9
LEARN_RATE = 0.3
AVERAGE_RATE = 0.9

@jax.custom_vjp
def low(v):
    return lax.optimization_barrier(v.astype(jnp.bfloat16)).astype(jnp.float32)

@jax.custom_vjp
def low_back(v):
    return v

def low_keep(v):
    return (low(v), None)

def low_pass(kept, grad):
    return (grad,)

def back_keep(v):
    return (v, None)

def back_low(kept, grad):
    return (low(grad),)
low.defvjp(low_keep, low_pass)
low_back.defvjp(back_keep, back_low)

def split_biases(biases):
    in_end = D
    down_end = in_end + EXPERTS * OUT
    gate_end = down_end + TASKS * EXPERTS
    tower_end = gate_end + TASKS * TH
    return (biases[:in_end], biases[in_end:down_end].reshape(EXPERTS, OUT), biases[down_end:gate_end].reshape(TASKS, EXPERTS), biases[gate_end:tower_end].reshape(TASKS, TH), biases[tower_end:])

def bag_counts(field_ids, bag_lengths, vocab_size):
    vocab_index = lax.broadcasted_iota(jnp.int32, (1, 1, vocab_size), 2)
    counts = jnp.zeros(field_ids.shape[:2] + (vocab_size,), jnp.float32)
    for position in range(field_ids.shape[2]):
        active = (bag_lengths > position)[:, :, None]
        matched = field_ids[:, :, position:position + 1] == vocab_index
        counts = counts + jnp.where(active & matched, 1.0, 0.0).astype(jnp.float32)
    return counts

def block_terms(params, operands):
    tables, in_weight, expert_up, expert_down, expert_up_bias, gate_weight, tower_up, tower_out, biases = params
    field_ids, bag_lengths, dense_values, labels = operands
    in_bias, down_bias, gate_bias, tower_up_bias, tower_out_bias = split_biases(biases)
    counts = bag_counts(field_ids, bag_lengths, tables.shape[1])
    pooled = jnp.einsum('bfv,fve->bfe', counts, tables, precision=HIGH).reshape(field_ids.shape[0], -1)
    features = jnp.concatenate([pooled, dense_values], axis=1)
    inputs = jnp.dot(features, in_weight, precision=HIGH) + in_bias
    pre_up = jnp.einsum('bd,edh->beh', inputs, expert_up, precision=HIGH) + expert_up_bias[None]
    hidden = jax.nn.silu(pre_up)
    pre_down = jnp.einsum('beh,eho->beo', hidden, expert_down, precision=HIGH) + down_bias[None]
    expert_out = jax.nn.silu(pre_down)
    gate_logits = jnp.einsum('bd,tde->bte', inputs, gate_weight, precision=HIGH) + gate_bias[None]
    gates = jax.nn.softmax(gate_logits, axis=-1)
    mixed = jnp.einsum('bte,beo->bto', gates, expert_out, precision=HIGH)
    pre_tower = jnp.einsum('bto,toz->btz', mixed, tower_up, precision=HIGH) + tower_up_bias[None]
    tower_hidden = jax.nn.silu(pre_tower)
    logits = jnp.einsum('btz,tz->bt', tower_hidden, tower_out, precision=HIGH) + tower_out_bias[None]
    targets = labels.astype(jnp.float32)
    losses = jnp.sum(jax.nn.softplus(logits) - targets * logits)
    squares = jnp.stack([jnp.sum(inputs * inputs), jnp.sum(hidden * hidden), jnp.sum(expert_out * expert_out), jnp.sum(tower_hidden * tower_hidden)])
    return (losses, squares)

def update(weight, gradient, momentum, average):
    new_momentum = MOMENTUM_RATE * momentum + gradient
    new_weight = weight - LEARN_RATE * (gradient + MOMENTUM_RATE * new_momentum)
    new_average = AVERAGE_RATE * average + (1.0 - AVERAGE_RATE) * new_weight
    return (new_weight, new_momentum, new_average, new_weight.astype(jnp.bfloat16))

def reference(field_ids, bag_lengths, dense_values, labels, tables, tables_momentum, tables_average, in_weight, in_weight_momentum, in_weight_average, expert_up, expert_up_momentum, expert_up_average, expert_down, expert_down_momentum, expert_down_average, expert_up_bias, expert_up_bias_momentum, expert_up_bias_average, gate_weight, gate_weight_momentum, gate_weight_average, tower_up, tower_up_momentum, tower_up_average, tower_out, tower_out_momentum, tower_out_average, biases, biases_momentum, biases_average):
    params = (tables, in_weight, expert_up, expert_down, expert_up_bias, gate_weight, tower_up, tower_out, biases)
    momenta = (tables_momentum, in_weight_momentum, expert_up_momentum, expert_down_momentum, expert_up_bias_momentum, gate_weight_momentum, tower_up_momentum, tower_out_momentum, biases_momentum)
    averages = (tables_average, in_weight_average, expert_up_average, expert_down_average, expert_up_bias_average, gate_weight_average, tower_up_average, tower_out_average, biases_average)
    block_rows = math.gcd(TOTAL, 4096)
    block_count = TOTAL // block_rows
    operands = (field_ids.reshape(block_count, block_rows, FIELDS, BAG), bag_lengths.reshape(block_count, block_rows, FIELDS), dense_values.reshape(block_count, block_rows, DENSE), labels.reshape(block_count, block_rows, TASKS))

    def objective(weights):

        def one_block(pieces):
            return block_terms(weights, pieces)
        losses, squares = lax.map(jax.checkpoint(one_block), operands)
        return (jnp.sum(losses) * TOTAL ** (-0.5), lax.optimization_barrier(jnp.sum(squares, axis=0)))
    loss_value, pullback, squares = jax.vjp(objective, params, has_aux=True)
    gradients = pullback(jnp.ones_like(loss_value))[0]
    results = []
    for weight, gradient, momentum, average in zip(params, gradients, momenta, averages):
        results.extend(update(weight, gradient, momentum, average))
    sizes_list = jnp.array([TOTAL * D, TOTAL * EXPERTS * HID, TOTAL * EXPERTS * OUT, TOTAL * TASKS * TH], jnp.float32)
    layer_rms = jnp.sqrt(squares / sizes_list + 1e-06)
    return (results[0], results[1], results[2], results[3], results[4], results[5], results[6], results[7], results[8], results[9], results[10], results[11], results[12], results[13], results[14], results[15], results[16], results[17], results[18], results[19], results[20], results[21], results[22], results[23], results[24], results[25], results[26], results[27], results[28], results[29], results[30], results[31], results[32], results[33], results[34], results[35], layer_rms)
```

```python
import functools

import jax
import jax.numpy as jnp
from jax import lax
from jax.experimental import pallas as pl
from jax.experimental.pallas import tpu as pltpu
from jax.sharding import PartitionSpec as P

D = 512
HID = 256
OUT = 128
TH = 64
TASKS = 2
EXPERTS = 4
FIELDS = 26
VOCAB = 256
EMB = 16
POOLED = 416
IN_ROWS = 429
NB = 1162

MOMENTUM_RATE = 0.9
LEARN_RATE = 0.3
AVERAGE_RATE = 0.9

BF = jnp.bfloat16
F32 = jnp.float32
NN = (((1,), (0,)), ((), ()))
NT = (((1,), (1,)), ((), ()))
MESH = pl.DeviceIdType.MESH

E_ROWS = 640
I_BASE = EXPERTS * E_ROWS
I_ROWS = 864
GATE_AT = 416
TOWER_AT = 432
MISC_AT = 496
UPB_AT = 504
T_ROWS = 512


def split(v):
    hi = v.astype(BF)
    return hi, (v - hi.astype(F32)).astype(BF)


def dot(a, b, dims):
    return lax.dot_general(a, b, dims, preferred_element_type=F32)


def mm(a, b, dims=NN):
    return dot(a[0], b[0], dims) + (dot(a[1], b[0], dims) + dot(a[0], b[1], dims))


def sigmoid(v):
    return 1.0 / (1.0 + jnp.exp(-v))


def padded(rows, n):
    unit = 8 * n
    return (rows + unit - 1) // unit * unit


def step_kernel(
    n,
    chunks,
    total_rows,
    block,
    ids_hbm,
    len_hbm,
    dense_hbm,
    lab_hbm,
    tab_ref,
    inw_ref,
    upo_ref,
    dno_ref,
    upbo_ref,
    gate_ref,
    tw_ref,
    tout_ref,
    bias_ref,
    gexp_ref,
    grep_ref,
    ids_ref,
    len_ref,
    dense_ref,
    lab_ref,
    upx_ref,
    dnx_ref,
    upbx_ref,
    w_in,
    w_in_t,
    w_in_b,
    up_b,
    up_t,
    dn_b,
    dn_t,
    tw_b,
    gate_b,
    gate_t,
    cols,
    bcol,
    feat32,
    feat,
    x,
    h,
    bpd,
    bpu,
    dsu,
    mixed,
    bpt,
    bgl,
    thbl,
    bi,
    bp,
    sq,
    grads,
    r_core,
    r_one,
    r_two,
    r_z,
    in_sem,
    w_send,
    w_recv,
    s_sem,
    v_sem,
    zs_sem,
    zv_sem,
):
    dp = lax.axis_index("dp")
    hid = lax.axis_index("hid")
    nz = n // 4
    bx = dp % 2
    by = (dp // 2) % 2
    mz = dp // 4
    core_peer = (dp, 1 - hid)
    x_peer = (dp + 1 - 2 * bx, hid)
    y_peer = (dp + 2 - 4 * by, hid)
    z_peers = [((mz + k) % nz * 4 + dp % 4, hid) for k in range(1, nz)]

    rows = ids_ref.shape[2]
    lanes = pl.ds(pl.multiple_of(hid * rows, rows), rows)
    loads = [
        pltpu.make_async_copy(src, dst, in_sem.at[k])
        for k, (src, dst) in enumerate(
            (
                (ids_hbm.at[:, :, lanes], ids_ref),
                (len_hbm.at[:, lanes], len_ref),
                (dense_hbm.at[:, lanes], dense_ref),
                (lab_hbm.at[:, lanes], lab_ref),
            )
        )
    ]
    for load in loads:
        load.start()

    barrier = pltpu.get_barrier_semaphore()
    peers = [core_peer, x_peer, y_peer] + z_peers
    for peer in peers:
        pl.semaphore_signal(barrier, inc=1, device_id=peer, device_id_type=MESH)
    pl.semaphore_wait(barrier, len(peers))

    def remote(src, dst, send, recv, peer):
        return pltpu.make_async_remote_copy(
            src_ref=src, dst_ref=dst, send_sem=send, recv_sem=recv, device_id=peer, device_id_type=MESH
        )

    weights = [
        remote(src, dst, w_send.at[k], w_recv.at[k], core_peer)
        for k, (src, dst) in enumerate(((upo_ref, upx_ref), (dno_ref, dnx_ref), (upbo_ref, upbx_ref)))
    ]
    for copy in weights:
        copy.start()

    w_in[0:IN_ROWS, :] = inw_ref[...]
    row = lax.broadcasted_iota(jnp.int32, (8, D), 0)
    in_bias = jnp.broadcast_to(bias_ref[0:1, 0:D], (8, D))
    w_in[424:432, :] = jnp.where(row == 5, in_bias, jnp.where(row < 5, w_in[424:432, :], 0.0))
    w_in[432:512, :] = jnp.zeros((80, D), F32)
    for i in range(4):
        hi, lo = split(w_in[128 * i : 128 * (i + 1), :].T)
        w_in_t[0, :, 128 * i : 128 * (i + 1)] = hi
        w_in_t[1, :, 128 * i : 128 * (i + 1)] = lo
    hi, lo = split(w_in[0:POOLED, :])
    w_in_b[0] = hi
    w_in_b[1] = lo

    def expert_weights(k, up, down):
        for e in range(EXPERTS):
            c = 256 * e + 128 * k
            hi, lo = split(up[e])
            up_b[0, :, c : c + 128] = hi
            up_b[1, :, c : c + 128] = lo
            hi, lo = split(up[e].T)
            up_t[0, c : c + 128, :] = hi
            up_t[1, c : c + 128, :] = lo
            hi, lo = split(down[e])
            dn_b[0, c : c + 128, :] = hi
            dn_b[1, c : c + 128, :] = lo
            hi, lo = split(down[e].T)
            dn_t[0, e, :, 128 * k : 128 * k + 128] = hi
            dn_t[1, e, :, 128 * k : 128 * k + 128] = lo

    expert_weights(0, upo_ref, dno_ref)
    gate8 = jnp.concatenate([gate_ref[0], gate_ref[1]], 0)
    hi, lo = split(jnp.concatenate([gate8, jnp.zeros((8, D), F32)], 0))
    gate_b[0] = hi
    gate_b[1] = lo
    for i in range(4):
        tile = jnp.concatenate([gate8[:, 128 * i : 128 * (i + 1)], jnp.zeros((120, 128), F32)], 0).T
        hi, lo = split(tile)
        gate_t[0, 128 * i : 128 * (i + 1), :] = hi
        gate_t[1, 128 * i : 128 * (i + 1), :] = lo
    for t in range(TASKS):
        hi, lo = split(tw_ref[t])
        tw_b[0, TH * t : TH * t + TH, :] = hi
        tw_b[1, TH * t : TH * t + TH, :] = lo
    tw_t = split(jnp.concatenate([tw_ref[0], tw_ref[1]], 0).T)
    x[0, D : D + 16, :] = jnp.ones((16, rows), BF)
    x[1, D : D + 16, :] = jnp.zeros((16, rows), BF)
    sq[...] = jnp.zeros(sq.shape, F32)
    feat32[...] = jnp.zeros(feat32.shape, F32)

    for copy in weights:
        copy.wait()
    expert_weights(1, upx_ref, dnx_ref)
    biases = bias_ref[0:1, :]
    bcol[...] = jnp.zeros((128, 128), F32)
    bcol[0:4, :] = upbo_ref[...]
    bcol[4:8, :] = upbx_ref[...]
    for e in range(EXPERTS):
        bcol[8 + e : 9 + e, :] = biases[:, 512 + 128 * e : 640 + 128 * e]
    bcol[12:13, :] = biases[:, 1032:1160]
    bcol[13:14, 0:64] = tout_ref[0:1, :]
    bcol[13:14, 64:128] = tout_ref[1:2, :]
    bcol[14:15, 0:8] = biases[:, 1024:1032]
    cols[...] = bcol[...].T

    for load in loads:
        load.wait()

    scale = float(total_rows) ** -0.5

    def examples(i, carry):
        off = pl.multiple_of(i * block, block)
        here = pl.ds(off, block)

        def field(f, carry):
            lengths = len_ref[pl.ds(f, 1), here]
            table = [[tab_ref[f, 8 * a : 8 * a + 8, 128 * k : 128 * k + 128] for k in range(2)] for a in range(2)]
            for j in range(block // 128):
                length = jnp.broadcast_to(lengths[:, 128 * j : 128 * j + 128], (8, 128))
                sums = [jnp.zeros((8, 128), F32) for _ in range(2)]
                for s in range(4):
                    at = pl.ds(pl.multiple_of(off + 128 * j, 128), 128)
                    ident = jnp.broadcast_to(ids_ref[f, s : s + 1, at], (8, 128))
                    low = jnp.bitwise_and(ident, 127)
                    for a in range(2):
                        first = jnp.take_along_axis(table[a][0], low, axis=1, mode="promise_in_bounds")
                        second = jnp.take_along_axis(table[a][1], low, axis=1, mode="promise_in_bounds")
                        found = jnp.where(ident < 128, first, second)
                        sums[a] = sums[a] + jnp.where(length > s, found, 0.0)
                for a in range(2):
                    at = pl.ds(pl.multiple_of(16 * f + 8 * a, 8), 8)
                    feat32[at, 128 * j : 128 * j + 128] = sums[a]
            return carry

        lax.fori_loop(0, FIELDS, field, 0)
        feat32[POOLED:IN_ROWS, :] = dense_ref[:, here]
        feat32[IN_ROWS : IN_ROWS + 1, :] = jnp.ones((1, block), F32)
        fs = split(feat32[...])
        feat[0, :, here] = fs[0]
        feat[1, :, here] = fs[1]
        xv = mm((w_in_t[0], w_in_t[1]), fs)
        sq[0] += jnp.sum((xv * xv).reshape(D // 8, 8, block), axis=0)
        xs = split(xv)
        x[0, 0:D, here] = xs[0]
        x[1, 0:D, here] = xs[1]
        gate_logits = mm((gate_b[0], gate_b[1]), xs)[0:8] + cols[0:8, 14:15]
        gates = []
        for t in range(TASKS):
            r = [gate_logits[4 * t + e : 4 * t + e + 1] for e in range(EXPERTS)]
            top = jnp.maximum(jnp.maximum(r[0], r[1]), jnp.maximum(r[2], r[3]))
            ex = [jnp.exp(v - top) for v in r]
            inv = 1.0 / ((ex[0] + ex[1]) + (ex[2] + ex[3]))
            gates.append([v * inv for v in ex])
        outs = []
        slopes = []
        for e in range(EXPERTS):
            c = 256 * e
            pre = mm((up_t[0, c : c + 256, :], up_t[1, c : c + 256, :]), xs)
            pre = pre + jnp.concatenate([cols[:, e : e + 1], cols[:, 4 + e : 5 + e]], 0)
            s = sigmoid(pre)
            hv = pre * s
            dsu[c : c + 256, :] = s * (1.0 + pre * (1.0 - s))
            sq[1] += jnp.sum((hv * hv).reshape(HID // 8, 8, block), axis=0)
            hs = split(hv)
            h[0, c : c + 256, here] = hs[0]
            h[1, c : c + 256, here] = hs[1]
            pre = mm((dn_t[0, e], dn_t[1, e]), hs) + cols[:, 8 + e : 9 + e]
            s = sigmoid(pre)
            out = pre * s
            sq[2] += jnp.sum((out * out).reshape(OUT // 8, 8, block), axis=0)
            outs.append(out)
            slopes.append(s * (1.0 + pre * (1.0 - s)))
        back_mixed = []
        back_logit = []
        for t in range(TASKS):
            z = slice(TH * t, TH * t + TH)
            o = slice(OUT * t, OUT * t + OUT)
            g = gates[t]
            ms = split(g[0] * outs[0] + g[1] * outs[1] + g[2] * outs[2] + g[3] * outs[3])
            mixed[0, o, here] = ms[0]
            mixed[1, o, here] = ms[1]
            pre = mm((tw_b[0, z, :], tw_b[1, z, :]), ms) + cols[z, 12:13]
            s = sigmoid(pre)
            th = pre * s
            sq[3] += jnp.sum((th * th).reshape(TH // 8, 8, block), axis=0)
            wo = cols[z, 13:14]
            logit = jnp.sum(th * wo, axis=0, keepdims=True) + bias_ref[0:1, 1160 + t : 1161 + t]
            back = (sigmoid(logit) - lab_ref[t : t + 1, here].astype(F32)) * scale
            ths = split(th)
            thbl[0, z, here] = ths[0]
            thbl[1, z, here] = ths[1]
            bs = split(jnp.broadcast_to(back, (16, block)))
            thbl[0, 128 + 16 * t : 144 + 16 * t, here] = bs[0]
            thbl[1, 128 + 16 * t : 144 + 16 * t, here] = bs[1]
            bs = split(back * wo * (s * (1.0 + pre * (1.0 - s))))
            bpt[0, z, here] = bs[0]
            bpt[1, z, here] = bs[1]
            bm = mm((tw_t[0][:, z], tw_t[1][:, z]), bs)
            back_mixed.append(bm)
            bg = [jnp.sum(bm * outs[e], axis=0, keepdims=True) for e in range(EXPERTS)]
            mean = g[0] * bg[0] + g[1] * bg[1] + g[2] * bg[2] + g[3] * bg[3]
            back_logit += [g[e] * (bg[e] - mean) for e in range(EXPERTS)]
        bs = split(jnp.concatenate(back_logit + [jnp.zeros((8, block), F32)], 0))
        bgl[0, :, here] = bs[0]
        bgl[1, :, here] = bs[1]
        for e in range(EXPERTS):
            c = 256 * e
            bs = split((gates[0][e] * back_mixed[0] + gates[1][e] * back_mixed[1]) * slopes[e])
            bpd[0, OUT * e : OUT * e + OUT, here] = bs[0]
            bpd[1, OUT * e : OUT * e + OUT, here] = bs[1]
            bs = split(mm((dn_b[0, c : c + 256, :], dn_b[1, c : c + 256, :]), bs) * dsu[c : c + 256, :])
            bpu[0, c : c + 256, here] = bs[0]
            bpu[1, c : c + 256, here] = bs[1]
        return carry

    lax.fori_loop(0, rows // block, examples, 0)

    class Chunk:
        def __init__(self, c, base, size, expert):
            self.c, self.base, self.size, self.expert = c, base, size, expert
            one, two = ((bx, x_peer), (by, y_peer)) if c % 2 == 0 else ((by, y_peer), (bx, x_peer))
            self.b1, self.p1 = one
            self.b2, self.p2 = two
            self.o2 = base + self.b1 * (size // 2)
            self.o3 = self.o2 + self.b2 * (size // 4)
            self.piece = size // 4 // nz
            self.o4 = self.o3 + mz * self.piece

        def at(self, start, size):
            return pl.ds(pl.multiple_of(start, 8), size)

        def res(self, start, size):
            if self.expert:
                return gexp_ref.at[self.at(start, size)]
            return grep_ref.at[hid, self.at(start - I_PAD, size)]

        def sems(self, k):
            return s_sem.at[8 * self.c + k], v_sem.at[8 * self.c + k]

        def core_start(self):
            rng = self.at(self.base, self.size)
            self.core = remote(grads.at[1, rng], r_core.at[rng], *self.sems(0), core_peer)
            self.core.start()

        def one_start(self):
            self.core.wait()
            rng = self.at(self.base, self.size)
            grads[0, rng, :] += r_core[rng, :]
            half = self.size // 2
            src = self.at(self.base + (1 - self.b1) * half, half)
            self.one = remote(
                grads.at[0, src], r_one.at[self.at(self.base // 2, half)], *self.sems(1), self.p1
            )
            self.one.start()

        def two_start(self):
            self.one.wait()
            half = self.size // 2
            grads[0, self.at(self.o2, half), :] += r_one[self.at(self.base // 2, half), :]
            quarter = self.size // 4
            src = self.at(self.o2 + (1 - self.b2) * quarter, quarter)
            self.two = remote(
                grads.at[0, src], r_two.at[self.at(self.base // 4, quarter)], *self.sems(2), self.p2
            )
            self.two.start()

        def z_start(self):
            self.two.wait()
            quarter = self.size // 4
            grads[0, self.at(self.o3, quarter), :] += r_two[self.at(self.base // 4, quarter), :]
            self.z = []
            for k in range(1, nz):
                src = self.at(self.o3 + (mz + k) % nz * self.piece, self.piece)
                dst = r_z.at[nz - k - 1, self.at(self.base // (4 * nz), self.piece)]
                q = self.c * (nz - 1)
                self.z.append(
                    remote(
                        grads.at[0, src], dst, zs_sem.at[0, q + k - 1], zv_sem.at[0, q + nz - k - 1], z_peers[k - 1]
                    )
                )
            for copy in self.z:
                copy.start()

        def z_gather(self):
            for copy in self.z:
                copy.wait()
            mine = self.at(self.o4, self.piece)
            total = grads[0, mine, :]
            for k in range(nz - 1):
                total = total + r_z[k, self.at(self.base // (4 * nz), self.piece), :]
            out = self.res(self.o4, self.piece)
            out[...] = total
            self.z = []
            for k in range(1, nz):
                q = self.c * (nz - 1)
                self.z.append(
                    remote(out, out, zs_sem.at[1, q + k - 1], zv_sem.at[1, q + nz - k - 1], z_peers[k - 1])
                )
            for copy in self.z:
                copy.start()

        def two_gather(self):
            for copy in self.z:
                copy.wait()
            out = self.res(self.o3, self.size // 4)
            self.two = remote(out, out, *self.sems(3), self.p2)
            self.two.start()

        def one_gather(self):
            self.two.wait()
            out = self.res(self.o2, self.size // 2)
            self.one = remote(out, out, *self.sems(4), self.p1)
            self.one.start()

        def core_gather(self):
            self.one.wait()
            if not self.expert:
                out = self.res(self.base, self.size)
                self.core = remote(out, out, *self.sems(5), core_peer)
                self.core.start()

        def finish(self):
            if not self.expert:
                self.core.wait()

    I_PAD = chunks[EXPERTS][0]
    parts = [Chunk(c, base, size, c < EXPERTS) for c, (base, size) in enumerate(chunks)]

    t_base, t_size = chunks[EXPERTS + 1]
    misc = t_base + MISC_AT
    grads[:, misc : t_base + t_size, :] = jnp.zeros((2, t_size - MISC_AT, 128), F32)
    for e in range(EXPERTS):
        c, o = 256 * e, 128 * e
        base = chunks[e][0]
        g = mm((x[0], x[1]), (bpu[0, c : c + 256, :], bpu[1, c : c + 256, :]), NT)
        grads[0, base : base + D, :] = g[0:D, 0:128]
        grads[1, base : base + D, :] = g[0:D, 128:256]
        upb = chunks[5][0] + UPB_AT + e
        grads[0, upb : upb + 1, :] = g[D : D + 1, 0:128]
        grads[1, upb : upb + 1, :] = g[D : D + 1, 128:256]
        g = mm((h[0, c : c + 256, :], h[1, c : c + 256, :]), (bpd[0, o : o + 128, :], bpd[1, o : o + 128, :]), NT)
        grads[0, base + D : base + E_ROWS, :] = g[0:128]
        grads[1, base + D : base + E_ROWS, :] = g[128:256]
        if chunks[e][1] > E_ROWS:
            grads[:, base + E_ROWS : base + chunks[e][1], :] = jnp.zeros((2, chunks[e][1] - E_ROWS, 128), F32)
        parts[e].core_start()

    def inputs_back(i, carry):
        here = pl.ds(pl.multiple_of(i * block, block), block)
        b = mm((up_b[0], up_b[1]), (bpu[0, :, here], bpu[1, :, here]))
        b = b + mm((gate_t[0, :, 0:16], gate_t[1, :, 0:16]), (bgl[0, :, here], bgl[1, :, here]))
        bs = split(b)
        bi[0, :, here] = bs[0]
        bi[1, :, here] = bs[1]
        ps = split(mm((w_in_b[0], w_in_b[1]), bs))
        bp[0, :, here] = ps[0]
        bp[1, :, here] = ps[1]
        return carry

    lax.fori_loop(0, rows // block, inputs_back, 0)

    def owner(k):
        return (k + hid) % 2

    i_base, i_size = chunks[EXPERTS]
    for k in range(4):
        g = mm((feat[0], feat[1]), (bi[0, 128 * k : 128 * k + 128, :], bi[1, 128 * k : 128 * k + 128, :]), NT)
        at = i_base + 432 * (k % 2)
        grads[owner(k // 2), at : at + 432, :] = g[0:432]
    if i_size > I_ROWS:
        grads[:, i_base + I_ROWS : i_base + i_size, :] = jnp.zeros((2, i_size - I_ROWS, 128), F32)
    parts[4].core_start()

    one16 = jnp.ones((16, rows), BF)
    g = mm((bgl[0], bgl[1]), (x[0], x[1]), NT)
    for k in range(4):
        at = t_base + GATE_AT + 8 * (k % 2)
        grads[owner(k // 2), at : at + 8, :] = g[0:8, 128 * k : 128 * k + 128]
    for t in range(TASKS):
        z = slice(TH * t, TH * t + TH)
        o = slice(OUT * t, OUT * t + OUT)
        g = mm((bpt[0, z, :], bpt[1, z, :]), (mixed[0, o, :], mixed[1, o, :]), NT)
        grads[owner(t), t_base + TOWER_AT : t_base + TOWER_AT + TH, :] = g
    lane = lax.broadcasted_iota(jnp.int32, (1, 128), 1)
    g = dot(one16, bpd[0], NT) + dot(one16, bpd[1], NT)
    m = owner(0)
    for e in range(EXPERTS):
        grads[m, misc + e : misc + e + 1, :] = g[0:1, 128 * e : 128 * e + 128]
    g = dot(one16, bpt[0], NT) + dot(one16, bpt[1], NT)
    grads[m, misc + 4 : misc + 5, :] = g[0:1]
    g = mm((thbl[0, 128:160, :], thbl[1, 128:160, :]), (thbl[0, 0:128, :], thbl[1, 0:128, :]), NT)
    grads[m, misc + 5 : misc + 6, :] = jnp.where(lane < TH, g[0:1], g[16:17])
    g = dot(one16, bgl[0], NT) + dot(one16, bgl[1], NT)
    grads[m, misc + 6 : misc + 7, 0:8] = g[0:1, 0:8]
    g = dot(one16, thbl[0, 128:160, :], NT) + dot(one16, thbl[1, 128:160, :], NT)
    grads[m, misc + 6 : misc + 7, 8:9] = g[0:1, 0:1]
    grads[m, misc + 6 : misc + 7, 9:10] = g[0:1, 16:17]
    sums = jnp.sum(sq[...], axis=(1, 2), keepdims=True).reshape(4, 1)
    squares = jnp.zeros((1, 128), F32)
    for k in range(4):
        squares = jnp.where(lane == k, sums[k : k + 1, :], squares)
    grads[m, misc + 7 : misc + 8, :] = squares

    def table_field(f, carry):
        lengths = len_ref[pl.ds(f, 1), :]
        ident = [jnp.where(lengths > s, ids_ref[f, s : s + 1, :], 512).astype(F32).astype(BF) for s in range(4)]
        at = pl.ds(pl.multiple_of(EMB * f, EMB), EMB)
        total = jnp.zeros((2 * EMB, VOCAB), F32)
        vocab = lax.broadcasted_iota(jnp.int32, (VOCAB, block), 0).astype(F32).astype(BF)
        one, zero = jnp.ones((VOCAB, block), BF), jnp.zeros((VOCAB, block), BF)
        for j in range(rows // block):
            here = slice(block * j, block * (j + 1))
            counts = zero
            for s in range(4):
                counts = counts + jnp.where(jnp.broadcast_to(ident[s][:, here], (VOCAB, block)) == vocab, one, zero)
            total = total + dot(jnp.concatenate([bp[0, at, here], bp[1, at, here]], 0), counts, NT)
        g = total[0:EMB] + total[EMB : 2 * EMB]
        at = pl.ds(pl.multiple_of(t_base + EMB * f, EMB), EMB)
        grads[owner(0), at, :] = g[:, 0:128]
        grads[owner(1), at, :] = g[:, 128:256]
        return carry

    lax.fori_loop(0, FIELDS, table_field, 0)
    parts[5].core_start()

    for stage in ("one_start", "two_start", "z_start", "z_gather", "two_gather", "one_gather", "core_gather", "finish"):
        for part in parts:
            getattr(part, stage)()


def step(ids, lengths, dense, labels, tables, in_weight, up, down, up_bias, gate, tower, tower_out, biases, n, total_rows):
    rows = ids.shape[2] // 2
    block = 256
    sizes = [padded(E_ROWS, n)] * EXPERTS + [padded(I_ROWS, n), padded(T_ROWS, n)]
    chunks = []
    base = 0
    for size in sizes:
        chunks.append((base, size))
        base += size
    e_all = chunks[EXPERTS][0]
    nz = n // 4
    vm = pltpu.VMEM
    scratch = [
        vm((FIELDS, 4, rows), jnp.int32),
        vm((FIELDS, rows), jnp.int32),
        vm((13, rows), F32),
        vm((TASKS, rows), jnp.int32),
        vm((EXPERTS, D, 128), F32),
        vm((EXPERTS, 128, OUT), F32),
        vm((EXPERTS, 128), F32),
        vm((512, D), F32),
        vm((2, D, 512), BF),
        vm((2, POOLED, D), BF),
        vm((2, D, EXPERTS * HID), BF),
        vm((2, EXPERTS * HID, D), BF),
        vm((2, EXPERTS * HID, OUT), BF),
        vm((2, EXPERTS, OUT, HID), BF),
        vm((2, TASKS * TH, OUT), BF),
        vm((2, 16, D), BF),
        vm((2, D, 128), BF),
        vm((128, 128), F32),
        vm((128, 128), F32),
        vm((512, block), F32),
        vm((2, 512, rows), BF),
        vm((2, D + 16, rows), BF),
        vm((2, EXPERTS * HID, rows), BF),
        vm((2, EXPERTS * OUT, rows), BF),
        vm((2, EXPERTS * HID, rows), BF),
        vm((EXPERTS * HID, block), F32),
        vm((2, TASKS * OUT, rows), BF),
        vm((2, TASKS * TH, rows), BF),
        vm((2, 16, rows), BF),
        vm((2, 160, rows), BF),
        vm((2, D, rows), BF),
        vm((2, POOLED, rows), BF),
        vm((4, 8, block), F32),
        vm((2, base, 128), F32),
        vm((base, 128), F32),
        vm((base // 2, 128), F32),
        vm((base // 4, 128), F32),
        vm((nz - 1, base // n, 128), F32),
        pltpu.SemaphoreType.DMA((4,)),
        pltpu.SemaphoreType.DMA((3,)),
        pltpu.SemaphoreType.DMA((3,)),
        pltpu.SemaphoreType.DMA((8 * len(chunks),)),
        pltpu.SemaphoreType.DMA((8 * len(chunks),)),
        pltpu.SemaphoreType.DMA((2, len(chunks) * (nz - 1))),
        pltpu.SemaphoreType.DMA((2, len(chunks) * (nz - 1))),
    ]
    anywhere = pl.BlockSpec(memory_space=pl.ANY)
    local = pl.BlockSpec(memory_space=pltpu.VMEM)
    return pl.pallas_call(
        functools.partial(step_kernel, n, chunks, total_rows, block),
        out_shape=[
            jax.ShapeDtypeStruct((e_all, 128), F32),
            jax.ShapeDtypeStruct((2, base - e_all, 128), F32),
        ],
        in_specs=[anywhere] * 4 + [local] * 9,
        out_specs=[local] * 2,
        scratch_shapes=scratch,
        compiler_params=pltpu.CompilerParams(collective_id=0, has_side_effects=True, vmem_limit_bytes=62 << 20),
        name="step",
    )(ids, lengths, dense, labels, tables, in_weight, up, down, up_bias, gate, tower, tower_out, biases)


def update_kernel(e_size, i_size, counts, gexp_ref, grep_ref, *refs):
    hid = lax.axis_index("hid")
    params = [refs[3 * k : 3 * k + 3] for k in range(9)]
    results = [refs[27 + 4 * k : 31 + 4 * k] for k in range(9)]
    rms_ref = refs[63]

    def update(k, at, g):
        w_ref, m_ref, a_ref = params[k]
        new_m = MOMENTUM_RATE * m_ref[at] + g
        new_w = w_ref[at] - LEARN_RATE * (g + MOMENTUM_RATE * new_m)
        ow, om, oa, orr = results[k]
        ow[at] = new_w
        om[at] = new_m
        oa[at] = AVERAGE_RATE * a_ref[at] + (1.0 - AVERAGE_RATE) * new_w
        orr[at] = new_w.astype(BF)

    t = i_size
    everything = slice(None)
    for f in range(FIELDS):
        for k in range(2):
            update(0, (f, everything, slice(128 * k, 128 * k + 128)), grep_ref[k, t + EMB * f : t + EMB * f + EMB, :])
    for k in range(4):
        at = 432 * (k % 2)
        update(1, (everything, slice(128 * k, 128 * k + 128)), grep_ref[k // 2, at : at + IN_ROWS, :])
    for e in range(EXPERTS):
        at = e_size * e
        update(2, (e,), gexp_ref[at : at + D, :])
        update(3, (e,), gexp_ref[at + D : at + E_ROWS, :])
    update(4, (everything,), grep_ref[hid, t + UPB_AT : t + UPB_AT + 4, :])
    for k in range(4):
        at = t + GATE_AT + 8 * (k % 2)
        for s in range(TASKS):
            g = grep_ref[k // 2, at + 4 * s : at + 4 * s + 4, :]
            update(5, (s, everything, slice(128 * k, 128 * k + 128)), g)
    for s in range(TASKS):
        update(6, (s,), grep_ref[s, t + TOWER_AT : t + TOWER_AT + TH, :])
    misc = t + MISC_AT
    tout = grep_ref[0, misc + 5 : misc + 6, :]
    for s in range(TASKS):
        update(7, (slice(s, s + 1), everything), tout[:, TH * s : TH * s + TH])
    pieces = [grep_ref[k // 2, 432 * (k % 2) + IN_ROWS : 432 * (k % 2) + IN_ROWS + 1, :] for k in range(4)]
    pieces += [grep_ref[0, misc + e : misc + e + 1, :] for e in range(EXPERTS)]
    last = grep_ref[0, misc + 6 : misc + 7, :]
    pieces += [last[:, 0:8], grep_ref[0, misc + 4 : misc + 5, :], last[:, 8:10]]
    update(8, (everything,), jnp.concatenate(pieces, 1))
    squares = grep_ref[0, misc + 7 : misc + 8, 0:4]
    lane = lax.broadcasted_iota(jnp.int32, (1, 4), 1)
    inverse = jnp.zeros((1, 4), F32)
    for k, count in enumerate(counts):
        inverse = jnp.where(lane == k, 1.0 / count, inverse)
    rms_ref[...] = jnp.sqrt(squares * inverse + 1e-06)


def local(*args):
    n = lax.axis_size("dp")
    ids, lengths, dense, labels = args[:4]
    total_rows = ids.shape[0] * n
    params = [list(args[4 + 3 * k : 7 + 3 * k]) for k in range(9)]
    for k in (0, 5, 6):
        params[k] = [v.transpose(0, 2, 1) for v in params[k]]
    params[8] = [v.reshape(1, NB) for v in params[8]]
    gexp, grep = step(
        ids.transpose(1, 2, 0),
        lengths.T,
        dense.T,
        labels.T,
        *[p[0] for p in params],
        n=n,
        total_rows=total_rows,
    )
    counts = [float(total_rows * c) for c in (D, EXPERTS * HID, EXPERTS * OUT, TASKS * TH)]
    shapes = []
    for p in params:
        shapes += [jax.ShapeDtypeStruct(p[0].shape, F32)] * 3 + [jax.ShapeDtypeStruct(p[0].shape, BF)]
    shapes.append(jax.ShapeDtypeStruct((1, 4), F32))
    flat = [v for p in params for v in p]
    vmem = pl.BlockSpec(memory_space=pltpu.VMEM)
    outs = pl.pallas_call(
        functools.partial(update_kernel, padded(E_ROWS, n), padded(I_ROWS, n), counts),
        out_shape=shapes,
        in_specs=[vmem] * (2 + len(flat)),
        out_specs=[vmem] * len(shapes),
        compiler_params=pltpu.CompilerParams(vmem_limit_bytes=62 << 20),
        name="update",
    )(gexp, grep, *flat)
    outs = list(outs)
    for k in (0, 5, 6):
        outs[4 * k : 4 * k + 4] = [v.transpose(0, 2, 1) for v in outs[4 * k : 4 * k + 4]]
    outs[32:36] = [v.reshape(NB) for v in outs[32:36]]
    outs[36] = outs[36].reshape(4)
    return tuple(outs)


def solution(mesh):
    up, down, bias = P(None, None, "hid"), P(None, "hid", None), P(None, "hid")
    rep = P()
    return jax.shard_map(
        local,
        mesh=mesh,
        in_specs=(P("dp", None, None), P("dp", None), P("dp", None), P("dp", None))
        + (rep,) * 6
        + (up,) * 3
        + (down,) * 3
        + (bias,) * 3
        + (rep,) * 12,
        out_specs=(rep,) * 8 + (up,) * 4 + (down,) * 4 + (bias,) * 4 + (rep,) * 17,
        check_vma=False,
    )
```

```python
import functools

import jax
import jax.numpy as jnp
from jax import lax
from jax.experimental import pallas as pl
from jax.experimental.pallas import tpu as pltpu
from jax.sharding import PartitionSpec as P

D = 512
HID = 256
OUT = 128
TH = 64
TASKS = 2
EXPERTS = 4
FIELDS = 26
VOCAB = 256
EMB = 16
POOLED = 416
IN_ROWS = 429
NB = 1162

MOMENTUM_RATE = 0.9
LEARN_RATE = 0.3
AVERAGE_RATE = 0.9

BF = jnp.bfloat16
F32 = jnp.float32
NN = (((1,), (0,)), ((), ()))
NT = (((1,), (1,)), ((), ()))
MESH = pl.DeviceIdType.MESH

E_ROWS = 640
I_BASE = EXPERTS * E_ROWS
I_ROWS = 864
GATE_AT = 416
TOWER_AT = 432
MISC_AT = 496
UPB_AT = 504
T_ROWS = 512


def split(v):
    hi = v.astype(BF)
    return hi, (v - hi.astype(F32)).astype(BF)


def dot(a, b, dims):
    return lax.dot_general(a, b, dims, preferred_element_type=F32)


def mm(a, b, dims=NN):
    return dot(a[0], b[0], dims) + (dot(a[1], b[0], dims) + dot(a[0], b[1], dims))


def bag_counts(part_ref, f, here, width):
    row = lax.broadcasted_iota(jnp.int32, (16, width), 0).astype(F32).astype(BF)
    zero = jnp.zeros((16, width), BF)
    weights = [jnp.broadcast_to(part_ref[0, f, s : s + 1, here], (16, width)).astype(BF) for s in range(4)]
    offsets = [jnp.broadcast_to(part_ref[1, f, s : s + 1, here], (16, width)).astype(BF) - row for s in range(4)]
    low, high = [], []
    for t in range(8):
        start = jnp.full((16, width), 16 * t, BF)
        hit = [jnp.where(offsets[s] == start, weights[s], zero) for s in range(4)]
        both = (hit[0] + hit[1]) + (hit[2] + hit[3])
        whole = (both + 128.0) - 128.0
        low.append(both - whole)
        high.append(whole)
    return jnp.concatenate(low + high, 0)


def step_kernel(
    n,
    chunks,
    total_rows,
    ids_hbm,
    len_hbm,
    dense_hbm,
    lab_hbm,
    tab_hbm,
    inw_hbm,
    up_hbm,
    dn_hbm,
    upbo_ref,
    gate_ref,
    tw_ref,
    tout_ref,
    bias_ref,
    gexp_ref,
    grep_ref,
    ids_ref,
    len_ref,
    dense_ref,
    lab_ref,
    tab_ref,
    up_ref,
    dn_ref,
    upbx_ref,
    brow,
    part,
    w_raw,
    w_in,
    w_in_t,
    w_in_b,
    up_b,
    up_t,
    dn_b,
    dn_t,
    tw_b,
    gate_t,
    cols,
    bcol,
    feat,
    x,
    h,
    bpd,
    bpu,
    dsu,
    mixed,
    bpt,
    bgl,
    thbl,
    bi,
    bp,
    grads,
    r_core,
    r_one,
    r_two,
    r_z,
    in_sem,
    w_send,
    w_recv,
    s_sem,
    v_sem,
    zs_sem,
    zv_sem,
):
    dp = lax.axis_index("dp")
    hid = lax.axis_index("hid")
    nz = n // 4
    bx = dp % 2
    by = (dp // 2) % 2
    mz = dp // 4
    core_peer = (dp, 1 - hid)
    x_peer = (dp + 1 - 2 * bx, hid)
    y_peer = (dp + 2 - 4 * by, hid)
    z_peers = [((mz + k) % nz * 4 + dp % 4, hid) for k in range(1, nz)]

    barrier = pltpu.get_barrier_semaphore()
    peers = [core_peer, x_peer, y_peer] + z_peers
    for peer in peers:
        pl.semaphore_signal(barrier, inc=1, device_id=peer, device_id_type=MESH)

    rows = ids_ref.shape[2]
    lanes = pl.ds(pl.multiple_of(hid * rows, rows), rows)
    loads = [
        pltpu.make_async_copy(src, dst, in_sem.at[k])
        for k, (src, dst) in enumerate(
            (
                (ids_hbm.at[:, :, lanes], ids_ref),
                (len_hbm.at[:, lanes], len_ref),
                (tab_hbm, tab_ref),
                (inw_hbm, w_raw),
                (up_hbm, up_ref.at[0]),
                (dn_hbm, dn_ref.at[0]),
                (dense_hbm.at[:, lanes], dense_ref),
                (lab_hbm.at[:, lanes], lab_ref),
            )
        )
    ]
    for load in loads:
        load.start()

    def remote(src, dst, send, recv, peer):
        return pltpu.make_async_remote_copy(
            src_ref=src, dst_ref=dst, send_sem=send, recv_sem=recv, device_id=peer, device_id_type=MESH
        )

    loads[0].wait()
    loads[1].wait()
    slot = lax.broadcasted_iota(jnp.int32, (4, rows), 0)
    for f in range(FIELDS):
        used = jnp.broadcast_to(len_ref[f : f + 1, :], (4, rows)) > slot
        ident = ids_ref[f]
        part[0, f] = jnp.where(used, jnp.where(ident < 128, 0.0625, 1.0), 0.0)
        part[1, f] = jnp.bitwise_and(ident, 127).astype(F32)

    pl.semaphore_wait(barrier, len(peers))
    weights = [
        remote(src, dst, w_send.at[k], w_recv.at[k], core_peer)
        for k, (src, dst) in enumerate(((up_hbm, up_ref.at[1]), (dn_hbm, dn_ref.at[1]), (upbo_ref, upbx_ref)))
    ]
    for copy in weights:
        copy.start()

    loads[2].wait()
    sixteen = jnp.where(lax.broadcasted_iota(jnp.int32, (EMB, VOCAB), 1) < 128, 16.0, 1.0)
    width = 256

    def pool_fields(i, carry):
        for u in range(2):
            f = 2 * i + u
            table = jnp.concatenate(split(tab_ref[f] * sixteen), 0)
            at = pl.ds(pl.multiple_of(EMB * f, EMB), EMB)
            for j in range(rows // width):
                here = slice(width * j, width * (j + 1))
                both = dot(table, bag_counts(part, f, here, width), NN)
                hi, lo = split(both[0:EMB] + both[EMB : 2 * EMB])
                feat[0, at, here] = hi
                feat[1, at, here] = lo
        return carry

    lax.fori_loop(0, FIELDS // 2, pool_fields, 0)

    brow[0:1, 0:1024] = bias_ref[0:1024].reshape(1, 1024)
    brow[0:1, 1024:NB] = bias_ref[1024:NB].reshape(1, NB - 1024)
    biases = brow[0:1, 0:NB]
    loads[3].wait()
    row = lax.broadcasted_iota(jnp.int32, (8, D), 0)
    in_bias = jnp.broadcast_to(biases[:, 0:D], (8, D))
    w_in[0:IN_ROWS, :] = w_raw[...]
    w_in[424:432, :] = jnp.where(row == 5, in_bias, jnp.where(row < 5, w_in[424:432, :], 0.0))
    w_in[432:512, :] = jnp.zeros((80, D), F32)
    for i in range(4):
        hi, lo = split(w_in[128 * i : 128 * (i + 1), :].T)
        w_in_t[0, :, 128 * i : 128 * (i + 1)] = hi
        w_in_t[1, :, 128 * i : 128 * (i + 1)] = lo
    hi, lo = split(w_in[0:POOLED, :])
    w_in_b[0] = hi
    w_in_b[1] = lo

    def expert_weights(k):
        for e in range(EXPERTS):
            c = 256 * e + 128 * k
            up, down = up_ref[k, e], dn_ref[k, e]
            hi, lo = split(up)
            up_b[0, :, c : c + 128] = hi
            up_b[1, :, c : c + 128] = lo
            hi, lo = split(up.T)
            up_t[0, c : c + 128, :] = hi
            up_t[1, c : c + 128, :] = lo
            hi, lo = split(down)
            dn_b[c : c + 128, 0:128] = hi
            dn_b[c : c + 128, 128:256] = lo
            hi, lo = split(down.T)
            dn_t[0, e, :, 128 * k : 128 * k + 128] = hi
            dn_t[1, e, :, 128 * k : 128 * k + 128] = lo

    loads[4].wait()
    loads[5].wait()
    expert_weights(0)
    gate8 = jnp.concatenate([gate_ref[0], gate_ref[1]], 0)
    hi, lo = split(jnp.concatenate([gate8, jnp.zeros((8, D), F32)], 0))
    up_t[0, 1024:1040, :] = hi
    up_t[1, 1024:1040, :] = lo
    for i in range(4):
        tile = jnp.concatenate([gate8[:, 128 * i : 128 * (i + 1)], jnp.zeros((120, 128), F32)], 0).T
        hi, lo = split(tile)
        gate_t[0, 128 * i : 128 * (i + 1), :] = hi
        gate_t[1, 128 * i : 128 * (i + 1), :] = lo
    for t in range(TASKS):
        hi, lo = split(tw_ref[t])
        tw_b[TH * t : TH * t + TH, 0:128] = hi
        tw_b[TH * t : TH * t + TH, 128:256] = lo
    tw_t = split(jnp.concatenate([tw_ref[0], tw_ref[1]], 0).T)
    x[0, D : D + 16, :] = jnp.ones((16, rows), BF)
    x[1, D : D + 16, :] = jnp.zeros((16, rows), BF)
    loads[6].wait()
    loads[7].wait()
    hi, lo = split(jnp.concatenate([dense_ref[...], jnp.ones((1, rows), F32), jnp.zeros((2, rows), F32)], 0))
    feat[0, POOLED:432, :] = hi
    feat[1, POOLED:432, :] = lo

    for copy in weights:
        copy.wait()
    expert_weights(1)
    bcol[...] = jnp.zeros((128, 128), F32)
    bcol[0:4, :] = upbo_ref[...]
    bcol[4:8, :] = upbx_ref[...]
    for e in range(EXPERTS):
        bcol[8 + e : 9 + e, :] = biases[:, 512 + 128 * e : 640 + 128 * e]
    bcol[12:13, :] = biases[:, 1032:1160]
    bcol[13:14, 0:64] = tout_ref[0:1, :]
    bcol[13:14, 64:128] = tout_ref[1:2, :]
    bcol[14:15, 0:8] = biases[:, 1024:1032]
    cols[...] = bcol[...].T

    scale = float(total_rows) ** -0.5
    fs = (feat[0], feat[1])
    xv = mm((w_in_t[0, :, 0:432], w_in_t[1, :, 0:432]), fs)
    squares = [jnp.sum(xv * xv, keepdims=True)]
    xs = split(xv)
    x[0, 0:D, :] = xs[0]
    x[1, 0:D, :] = xs[1]
    gate_logits = mm((up_t[0, 1024:1040], up_t[1, 1024:1040]), xs)[0:8] + cols[0:8, 14:15]
    gates = []
    for t in range(TASKS):
        r = [gate_logits[4 * t + e : 4 * t + e + 1] for e in range(EXPERTS)]
        top = jnp.maximum(jnp.maximum(r[0], r[1]), jnp.maximum(r[2], r[3]))
        ex = [jnp.exp(v - top) for v in r]
        inv = 1.0 / ((ex[0] + ex[1]) + (ex[2] + ex[3]))
        gates.append([v * inv for v in ex])
    outs, slopes = [], []
    sums = [0.0, 0.0, 0.0]
    for e in range(EXPERTS):
        c = 256 * e
        pre = mm((up_t[0, c : c + 256, :], up_t[1, c : c + 256, :]), xs)
        pre = pre + jnp.concatenate([cols[:, e : e + 1], cols[:, 4 + e : 5 + e]], 0)
        s = jax.nn.sigmoid(pre)
        hv = pre * s
        dsu[c : c + 256, :] = s + hv * (1.0 - s)
        sums[0] = sums[0] + jnp.sum(hv * hv, keepdims=True)
        hs = split(hv)
        h[0, c : c + 256, :] = hs[0]
        h[1, c : c + 256, :] = hs[1]
        pre = mm((dn_t[0, e], dn_t[1, e]), hs) + cols[:, 8 + e : 9 + e]
        s = jax.nn.sigmoid(pre)
        out = pre * s
        sums[1] = sums[1] + jnp.sum(out * out, keepdims=True)
        outs.append(out)
        slopes.append(s + out * (1.0 - s))
    back_mixed, back_logit = [], []
    for t in range(TASKS):
        z = slice(TH * t, TH * t + TH)
        o = slice(OUT * t, OUT * t + OUT)
        g = gates[t]
        ms = split(g[0] * outs[0] + g[1] * outs[1] + g[2] * outs[2] + g[3] * outs[3])
        mixed[0, o, :] = ms[0]
        mixed[1, o, :] = ms[1]
        w = tw_b[z, :]
        pre = dot(w, jnp.concatenate([ms[0], ms[0]], 0), NN) + dot(w[:, 0:128], ms[1], NN) + cols[z, 12:13]
        s = jax.nn.sigmoid(pre)
        th = pre * s
        sums[2] = sums[2] + jnp.sum(th * th, keepdims=True)
        wo = cols[z, 13:14]
        logit = jnp.sum(th * wo, axis=0, keepdims=True) + biases[:, 1160 + t : 1161 + t]
        back = (jax.nn.sigmoid(logit) - lab_ref[t : t + 1, :].astype(F32)) * scale
        ths = split(th)
        thbl[0, z, :] = ths[0]
        thbl[1, z, :] = ths[1]
        bs = split(jnp.broadcast_to(back, (16, rows)))
        thbl[0, 128 + 16 * t : 144 + 16 * t, :] = bs[0]
        thbl[1, 128 + 16 * t : 144 + 16 * t, :] = bs[1]
        bs = split(back * wo * (s + th * (1.0 - s)))
        bpt[0, z, :] = bs[0]
        bpt[1, z, :] = bs[1]
        w = [v[:, z] for v in tw_t]
        bm = dot(jnp.concatenate([w[0], w[1], w[0]], 1), jnp.concatenate([bs[0], bs[0], bs[1]], 0), NN)
        back_mixed.append(bm)
        bg = [jnp.sum(bm * outs[e], axis=0, keepdims=True) for e in range(EXPERTS)]
        mean = g[0] * bg[0] + g[1] * bg[1] + g[2] * bg[2] + g[3] * bg[3]
        back_logit += [g[e] * (bg[e] - mean) for e in range(EXPERTS)]
    bs = split(jnp.concatenate(back_logit + [jnp.zeros((8, rows), F32)], 0))
    bgl[0] = bs[0]
    bgl[1] = bs[1]
    for e in range(EXPERTS):
        c = 256 * e
        bs = split((gates[0][e] * back_mixed[0] + gates[1][e] * back_mixed[1]) * slopes[e])
        bpd[0, OUT * e : OUT * e + OUT, :] = bs[0]
        bpd[1, OUT * e : OUT * e + OUT, :] = bs[1]
        w = dn_b[c : c + 256, :]
        back = dot(w, jnp.concatenate([bs[0], bs[0]], 0), NN) + dot(w[:, 0:128], bs[1], NN)
        bs = split(back * dsu[c : c + 256, :])
        bpu[0, c : c + 256, :] = bs[0]
        bpu[1, c : c + 256, :] = bs[1]
    squares += sums

    class Piece:
        def __init__(self, c, base, size, expert):
            self.c, self.base, self.size, self.expert = c, base, size, expert
            one, two = ((bx, x_peer), (by, y_peer)) if c % 2 == 0 else ((by, y_peer), (bx, x_peer))
            self.b1, self.p1 = one
            self.b2, self.p2 = two
            self.o2 = base + self.b1 * (size // 2)
            self.o3 = self.o2 + self.b2 * (size // 4)
            self.part = size // 4 // nz
            self.o4 = self.o3 + mz * self.part

        def at(self, start, size):
            return pl.ds(pl.multiple_of(start, 8), size)

        def res(self, start, size):
            if self.expert:
                return gexp_ref.at[self.at(start, size)]
            return grep_ref.at[hid, self.at(start - rep_base, size)]

        def sems(self, k):
            return s_sem.at[6 * self.c + k], v_sem.at[6 * self.c + k]

        def core(self):
            rng = self.at(self.base, self.size)
            self.core_copy = remote(grads.at[1, rng], r_core.at[rng], *self.sems(0), core_peer)
            self.core_copy.start()

        def one(self):
            self.core_copy.wait()
            rng = self.at(self.base, self.size)
            grads[0, rng, :] += r_core[rng, :]
            half = self.size // 2
            src = self.at(self.base + (1 - self.b1) * half, half)
            self.copy = remote(grads.at[0, src], r_one.at[self.at(self.base // 2, half)], *self.sems(1), self.p1)
            self.copy.start()

        def two(self):
            self.copy.wait()
            half = self.size // 2
            grads[0, self.at(self.o2, half), :] += r_one[self.at(self.base // 2, half), :]
            quarter = self.size // 4
            src = self.at(self.o2 + (1 - self.b2) * quarter, quarter)
            self.copy = remote(grads.at[0, src], r_two.at[self.at(self.base // 4, quarter)], *self.sems(2), self.p2)
            self.copy.start()

        def z(self):
            self.copy.wait()
            quarter = self.size // 4
            grads[0, self.at(self.o3, quarter), :] += r_two[self.at(self.base // 4, quarter), :]
            self.z_copies = []
            q = self.c * (nz - 1)
            for k in range(1, nz):
                src = self.at(self.o3 + (mz + k) % nz * self.part, self.part)
                dst = r_z.at[nz - k - 1, self.at(self.base // (4 * nz), self.part)]
                sems = zs_sem.at[0, q + k - 1], zv_sem.at[0, q + nz - k - 1]
                self.z_copies.append(remote(grads.at[0, src], dst, *sems, z_peers[k - 1]))
            for copy in self.z_copies:
                copy.start()

        def zg(self):
            for copy in self.z_copies:
                copy.wait()
            total = grads[0, self.at(self.o4, self.part), :]
            for k in range(nz - 1):
                total = total + r_z[k, self.at(self.base // (4 * nz), self.part), :]
            out = self.res(self.o4, self.part)
            out[...] = total
            self.z_copies = []
            q = self.c * (nz - 1)
            for k in range(1, nz):
                sems = zs_sem.at[1, q + k - 1], zv_sem.at[1, q + nz - k - 1]
                self.z_copies.append(remote(out, out, *sems, z_peers[k - 1]))
            for copy in self.z_copies:
                copy.start()

        def twog(self):
            for copy in self.z_copies:
                copy.wait()
            out = self.res(self.o3, self.size // 4)
            self.copy = remote(out, out, *self.sems(3), self.p2)
            self.copy.start()

        def oneg(self):
            self.copy.wait()
            out = self.res(self.o2, self.size // 2)
            self.copy = remote(out, out, *self.sems(4), self.p1)
            self.copy.start()

        def coreg(self):
            self.copy.wait()
            if not self.expert:
                out = self.res(self.base, self.size)
                self.copy = remote(out, out, *self.sems(5), core_peer)
                self.copy.start()

        def end(self):
            if not self.expert:
                self.copy.wait()

    rep_base = chunks[EXPERTS][0][0]
    pieces = {}
    c = 0
    for k, (name, parts) in enumerate(zip(("e0", "e1", "e2", "e3", "i", "t"), chunks)):
        pieces[name] = []
        for base, size in parts:
            pieces[name].append(Piece(c, base, size, k < EXPERTS))
            c += 1

    def run(*steps):
        for step in steps:
            name, stage = step.split(".")
            for piece in pieces[name]:
                getattr(piece, stage)()

    def owner(k):
        return (k + hid) % 2

    e_base = [chunks[e][0][0] for e in range(EXPERTS)]
    e_size = chunks[1][0][0] - chunks[0][0][0]
    i_base, t_base = chunks[EXPERTS][0][0], chunks[EXPERTS + 1][0][0]
    t_size = grads.shape[1] - t_base
    misc = t_base + MISC_AT
    grads[:, misc : t_base + t_size, :] = jnp.zeros((2, t_size - MISC_AT, 128), F32)

    def expert_gradients(e):
        c, o, base = 256 * e, 128 * e, e_base[e]
        g = mm((x[0], x[1]), (bpu[0, c : c + 256, :], bpu[1, c : c + 256, :]), NT)
        grads[0, base : base + D, :] = g[0:D, 0:128]
        grads[1, base : base + D, :] = g[0:D, 128:256]
        upb = t_base + UPB_AT + e
        grads[0, upb : upb + 1, :] = g[D : D + 1, 0:128]
        grads[1, upb : upb + 1, :] = g[D : D + 1, 128:256]
        hi, lo = bpd[0, o : o + 128, :], bpd[1, o : o + 128, :]
        g = dot(h[0, c : c + 256, :], jnp.concatenate([hi, lo], 0), NT)
        g = (g[:, 0:128] + g[:, 128:256]) + dot(h[1, c : c + 256, :], hi, NT)
        grads[0, base + D : base + E_ROWS, :] = g[0:128]
        grads[1, base + D : base + E_ROWS, :] = g[128:256]
        if e_size > E_ROWS:
            grads[:, base + E_ROWS : base + e_size, :] = jnp.zeros((2, e_size - E_ROWS, 128), F32)
        run(f"e{e}.core")

    expert_gradients(0)
    expert_gradients(1)
    run("e0.one")
    expert_gradients(2)
    run("e1.one")
    expert_gradients(3)
    run("e2.one")

    def inputs_back(here):
        b = mm((up_b[0], up_b[1]), (bpu[0, :, here], bpu[1, :, here]))
        b = b + mm((gate_t[0, :, 0:16], gate_t[1, :, 0:16]), (bgl[0, :, here], bgl[1, :, here]))
        bs = split(b)
        bi[0, :, here] = bs[0]
        bi[1, :, here] = bs[1]
        ps = split(mm((w_in_b[0], w_in_b[1]), bs))
        bp[0, :, here] = ps[0]
        bp[1, :, here] = ps[1]

    inputs_back(slice(0, rows // 2))
    run("e3.one", "e0.two")
    inputs_back(slice(rows // 2, rows))
    run("e1.two")
    for k in range(2):
        g = mm((feat[0], feat[1]), (bi[0, 256 * k : 256 * k + 256, :], bi[1, 256 * k : 256 * k + 256, :]), NT)
        grads[owner(k), i_base : i_base + 432, :] = g[:, 0:128]
        grads[owner(k), i_base + 432 : i_base + I_ROWS, :] = g[:, 128:256]
    if t_base - i_base > I_ROWS:
        grads[:, i_base + I_ROWS : t_base, :] = jnp.zeros((2, t_base - i_base - I_ROWS, 128), F32)
    run("i.core", "e2.two", "e0.z")

    one16 = jnp.ones((16, rows), BF)
    g = mm((bgl[0], bgl[1]), (x[0], x[1]), NT)
    for k in range(4):
        at = t_base + GATE_AT + 8 * (k % 2)
        grads[owner(k // 2), at : at + 8, :] = g[0:8, 128 * k : 128 * k + 128]
    for t in range(TASKS):
        z = slice(TH * t, TH * t + TH)
        o = slice(OUT * t, OUT * t + OUT)
        g = mm((bpt[0, z, :], bpt[1, z, :]), (mixed[0, o, :], mixed[1, o, :]), NT)
        grads[owner(t), t_base + TOWER_AT : t_base + TOWER_AT + TH, :] = g
    lane = lax.broadcasted_iota(jnp.int32, (1, 128), 1)
    g = dot(one16, bpd[0], NT) + dot(one16, bpd[1], NT)
    m = owner(0)
    for e in range(EXPERTS):
        grads[m, misc + e : misc + e + 1, :] = g[0:1, 128 * e : 128 * e + 128]
    g = dot(one16, bpt[0], NT) + dot(one16, bpt[1], NT)
    grads[m, misc + 4 : misc + 5, :] = g[0:1]
    g = mm((thbl[0, 128:160, :], thbl[1, 128:160, :]), (thbl[0, 0:128, :], thbl[1, 0:128, :]), NT)
    grads[m, misc + 5 : misc + 6, :] = jnp.where(lane < TH, g[0:1], g[16:17])
    g = dot(one16, bgl[0], NT) + dot(one16, bgl[1], NT)
    grads[m, misc + 6 : misc + 7, 0:8] = g[0:1, 0:8]
    g = dot(one16, thbl[0, 128:160, :], NT) + dot(one16, thbl[1, 128:160, :], NT)
    grads[m, misc + 6 : misc + 7, 8:9] = g[0:1, 0:1]
    grads[m, misc + 6 : misc + 7, 9:10] = g[0:1, 16:17]
    total = jnp.zeros((1, 128), F32)
    for k in range(4):
        total = jnp.where(lane == k, squares[k], total)
    grads[m, misc + 7 : misc + 8, :] = total
    run("i.one", "e3.two", "e1.z")

    def table_fields(i, carry):
        for u in range(2):
            f = 2 * i + u
            at = pl.ds(pl.multiple_of(EMB * f, EMB), EMB)
            total = jnp.zeros((2 * EMB, VOCAB), F32)
            for j in range(rows // width):
                here = slice(width * j, width * (j + 1))
                back = jnp.concatenate([bp[0, at, here], bp[1, at, here]], 0)
                total = total + dot(back, bag_counts(part, f, here, width), NT)
            g = (total[0:EMB] + total[EMB : 2 * EMB]) * sixteen
            at = pl.ds(pl.multiple_of(t_base + EMB * f, EMB), EMB)
            grads[owner(0), at, :] = g[:, 0:128]
            grads[owner(1), at, :] = g[:, 128:256]
        return carry

    lax.fori_loop(0, 4, table_fields, 0)
    run("e2.z", "e0.zg")
    lax.fori_loop(4, 8, table_fields, 0)
    run("e3.z", "e1.zg", "i.two")
    lax.fori_loop(8, 13, table_fields, 0)
    run("t.core", "e0.twog", "e2.zg")
    run("t.one", "e1.twog", "e3.zg", "i.z", "e0.oneg", "e2.twog", "t.two", "e1.oneg", "e3.twog", "i.zg")
    run("t.z", "e2.oneg", "e3.oneg", "i.twog", "t.zg", "e0.coreg", "e1.coreg", "i.oneg", "t.twog", "e2.coreg")
    run("i.coreg", "t.oneg", "e3.coreg", "t.coreg", "i.end", "t.end")


def layout(n):
    unit = 8 * n
    chunks, base = [], 0
    for k, size in enumerate([E_ROWS] * EXPERTS + [I_ROWS, T_ROWS]):
        units = -(-size // unit)
        first = units if k < EXPERTS else (units + 1) // 2
        parts = [(base, first * unit)]
        if units > first:
            parts.append((base + first * unit, (units - first) * unit))
        chunks.append(parts)
        base += units * unit
    return chunks, base


def step(ids, lengths, dense, labels, tables, in_weight, up, down, up_bias, gate, tower, tower_out, biases, n, total_rows):
    rows = ids.shape[2] // 2
    chunks, size = layout(n)
    count = sum(len(parts) for parts in chunks)
    e_all = chunks[EXPERTS][0][0]
    nz = n // 4
    vm = pltpu.VMEM
    scratch = [
        vm((FIELDS, 4, rows), jnp.int32),
        vm((FIELDS, rows), jnp.int32),
        vm((13, rows), F32),
        vm((TASKS, rows), jnp.int32),
        vm((FIELDS, EMB, VOCAB), F32),
        vm((2, EXPERTS, D, 128), F32),
        vm((2, EXPERTS, 128, OUT), F32),
        vm((EXPERTS, 128), F32),
        vm((8, 1280), F32),
        vm((2, FIELDS, 4, rows), F32),
        vm((IN_ROWS, D), F32),
        vm((512, D), F32),
        vm((2, D, 512), BF),
        vm((2, POOLED, D), BF),
        vm((2, D, EXPERTS * HID), BF),
        vm((2, EXPERTS * HID + 16, D), BF),
        vm((EXPERTS * HID, 2 * OUT), BF),
        vm((2, EXPERTS, OUT, HID), BF),
        vm((TASKS * TH, 2 * OUT), BF),
        vm((2, D, 128), BF),
        vm((128, 128), F32),
        vm((128, 128), F32),
        vm((2, 432, rows), BF),
        vm((2, D + 16, rows), BF),
        vm((2, EXPERTS * HID, rows), BF),
        vm((2, EXPERTS * OUT, rows), BF),
        vm((2, EXPERTS * HID, rows), BF),
        vm((EXPERTS * HID, rows), F32),
        vm((2, TASKS * OUT, rows), BF),
        vm((2, TASKS * TH, rows), BF),
        vm((2, 16, rows), BF),
        vm((2, 160, rows), BF),
        vm((2, D, rows), BF),
        vm((2, POOLED, rows), BF),
        vm((2, size, 128), F32),
        vm((size, 128), F32),
        vm((size // 2, 128), F32),
        vm((size // 4, 128), F32),
        vm((nz - 1, size // n, 128), F32),
        pltpu.SemaphoreType.DMA((8,)),
        pltpu.SemaphoreType.DMA((3,)),
        pltpu.SemaphoreType.DMA((3,)),
        pltpu.SemaphoreType.DMA((6 * count,)),
        pltpu.SemaphoreType.DMA((6 * count,)),
        pltpu.SemaphoreType.DMA((2, count * (nz - 1))),
        pltpu.SemaphoreType.DMA((2, count * (nz - 1))),
    ]
    anywhere = pl.BlockSpec(memory_space=pl.ANY)
    local = pl.BlockSpec(memory_space=pltpu.VMEM)
    return pl.pallas_call(
        functools.partial(step_kernel, n, chunks, total_rows),
        out_shape=[
            jax.ShapeDtypeStruct((e_all, 128), F32),
            jax.ShapeDtypeStruct((2, size - e_all, 128), F32),
        ],
        in_specs=[anywhere] * 8 + [local] * 5,
        out_specs=[local] * 2,
        scratch_shapes=scratch,
        compiler_params=pltpu.CompilerParams(collective_id=0, has_side_effects=True, vmem_limit_bytes=62 << 20),
        name="step",
    )(ids, lengths, dense, labels, tables, in_weight, up, down, up_bias, gate, tower, tower_out, biases)


def update_kernel(e_size, i_size, counts, gexp_ref, grep_ref, *refs):
    *refs, row_ref = refs
    hid = lax.axis_index("hid")
    params = [refs[3 * k : 3 * k + 3] for k in range(9)]
    results = [refs[27 + 4 * k : 31 + 4 * k] for k in range(9)]
    rms_ref = refs[63]

    def update(k, at, g):
        w_ref, m_ref, a_ref = params[k]
        new_m = MOMENTUM_RATE * m_ref[at] + g
        new_w = w_ref[at] - LEARN_RATE * (g + MOMENTUM_RATE * new_m)
        ow, om, oa, orr = results[k]
        ow[at] = new_w
        om[at] = new_m
        oa[at] = AVERAGE_RATE * a_ref[at] + (1.0 - AVERAGE_RATE) * new_w
        orr[at] = new_w.astype(BF)

    t = i_size
    everything = slice(None)
    for f in range(FIELDS):
        for k in range(2):
            update(0, (f, everything, slice(128 * k, 128 * k + 128)), grep_ref[k, t + EMB * f : t + EMB * f + EMB, :])
    for k in range(4):
        at = 432 * (k % 2)
        update(1, (everything, slice(128 * k, 128 * k + 128)), grep_ref[k // 2, at : at + IN_ROWS, :])
    for e in range(EXPERTS):
        at = e_size * e
        update(2, (e,), gexp_ref[at : at + D, :])
        update(3, (e,), gexp_ref[at + D : at + E_ROWS, :])
    update(4, (everything,), grep_ref[hid, t + UPB_AT : t + UPB_AT + 4, :])
    for k in range(4):
        at = t + GATE_AT + 8 * (k % 2)
        for s in range(TASKS):
            g = grep_ref[k // 2, at + 4 * s : at + 4 * s + 4, :]
            update(5, (s, everything, slice(128 * k, 128 * k + 128)), g)
    for s in range(TASKS):
        update(6, (s,), grep_ref[s, t + TOWER_AT : t + TOWER_AT + TH, :])
    misc = t + MISC_AT
    tout = grep_ref[0, misc + 5 : misc + 6, :]
    for s in range(TASKS):
        update(7, (slice(s, s + 1), everything), tout[:, TH * s : TH * s + TH])
    for k in range(4):
        at = 432 * (k % 2) + IN_ROWS
        row_ref[0:1, 128 * k : 128 * k + 128] = grep_ref[k // 2, at : at + 1, :]
        row_ref[0:1, D + 128 * k : D + 128 * k + 128] = grep_ref[0, misc + k : misc + k + 1, :]
    row_ref[0:1, 1024:1032] = grep_ref[0, misc + 6 : misc + 7, 0:8]
    row_ref[0:1, 1032:1160] = grep_ref[0, misc + 4 : misc + 5, :]
    row_ref[0:1, 1160:1162] = grep_ref[0, misc + 6 : misc + 7, 8:10]
    update(8, (everything,), row_ref[0, 0:NB])
    squares = grep_ref[0, misc + 7 : misc + 8, :]
    lane = lax.broadcasted_iota(jnp.int32, (1, 128), 1)
    inverse = jnp.zeros((1, 128), F32)
    for k, count in enumerate(counts):
        inverse = jnp.where(lane == k, 1.0 / count, inverse)
    row_ref[1:2, 0:128] = jnp.sqrt(squares * inverse + 1e-06)
    rms_ref[...] = row_ref[1, 0:4]


def local(*args):
    n = lax.axis_size("dp")
    ids, lengths, dense, labels = args[:4]
    total_rows = ids.shape[0] * n
    params = [list(args[4 + 3 * k : 7 + 3 * k]) for k in range(9)]
    for k in (0, 5, 6):
        params[k] = [v.transpose(0, 2, 1) for v in params[k]]
    gexp, grep = step(
        ids.transpose(1, 2, 0),
        lengths.T,
        dense.T,
        labels.T,
        *[p[0] for p in params],
        n=n,
        total_rows=total_rows,
    )
    chunks, _ = layout(n)
    counts = [float(total_rows * c) for c in (D, EXPERTS * HID, EXPERTS * OUT, TASKS * TH)]
    shapes = []
    for p in params:
        shapes += [jax.ShapeDtypeStruct(p[0].shape, F32)] * 3 + [jax.ShapeDtypeStruct(p[0].shape, BF)]
    shapes.append(jax.ShapeDtypeStruct((4,), F32))
    flat = [v for p in params for v in p]
    vmem = pl.BlockSpec(memory_space=pltpu.VMEM)
    outs = pl.pallas_call(
        functools.partial(update_kernel, chunks[1][0][0], chunks[5][0][0] - chunks[4][0][0], counts),
        out_shape=shapes,
        in_specs=[vmem] * (2 + len(flat)),
        out_specs=[vmem] * len(shapes),
        scratch_shapes=[pltpu.VMEM((8, 1280), F32)],
        compiler_params=pltpu.CompilerParams(vmem_limit_bytes=62 << 20),
        name="update",
    )(gexp, grep, *flat)
    outs = list(outs)
    for k in (0, 5, 6):
        outs[4 * k : 4 * k + 4] = [v.transpose(0, 2, 1) for v in outs[4 * k : 4 * k + 4]]
    return tuple(outs)


def solution(mesh):
    up, down, bias = P(None, None, "hid"), P(None, "hid", None), P(None, "hid")
    rep = P()
    return jax.shard_map(
        local,
        mesh=mesh,
        in_specs=(P("dp", None, None), P("dp", None), P("dp", None), P("dp", None))
        + (rep,) * 6
        + (up,) * 3
        + (down,) * 3
        + (bias,) * 3
        + (rep,) * 12,
        out_specs=(rep,) * 8 + (up,) * 4 + (down,) * 4 + (bias,) * 4 + (rep,) * 17,
        check_vma=False,
    )
```

```python
import functools

import jax
import jax.numpy as jnp
from jax import lax
from jax.experimental import pallas as pl
from jax.experimental.pallas import tpu as pltpu
from jax.sharding import PartitionSpec as P

D = 512
HID = 256
OUT = 128
TH = 64
TASKS = 2
EXPERTS = 4
FIELDS = 26
VOCAB = 256
EMB = 16
POOLED = 416
IN_ROWS = 429
NB = 1162

MOMENTUM_RATE = 0.9
LEARN_RATE = 0.3
AVERAGE_RATE = 0.9

BF = jnp.bfloat16
F32 = jnp.float32
NN = (((1,), (0,)), ((), ()))
NT = (((1,), (1,)), ((), ()))
MESH = pl.DeviceIdType.MESH

E_ROWS = 640
I_BASE = EXPERTS * E_ROWS
I_ROWS = 864
GATE_AT = 416
TOWER_AT = 432
MISC_AT = 496
UPB_AT = 504
T_ROWS = 512


PARTS = (
    ((640, "xyz"),),
    ((640, "yxz"),),
    ((640, "pz"),),
    ((640, "pz"),),
    ((512, "pz"), (384, "zxy"),),
    ((512, "pz"),),
)
SCHEDULE = (
    "!b2",
    "!b3",
    "!G2",
    "!D2",
    "e2a",
    "!G3",
    "e2a",
    "!D3",
    "e3a",
    "!b0",
    "!b1",
    "!G0",
    "e3a",
    "!D0",
    "e0a",
    "!G1",
    "e0a",
    "!D1",
    "e1a",
    "!s0",
    "e2a e1a",
    "!h0",
    "e3a",
    "!i0",
    "e2a",
    "!i1",
    "ib e1a ia e0a",
    "!h1",
    "ia ib",
    "!j0-7",
    "e1a e0a e2a",
    "!j7-13",
    "e3a ia ta ib",
    "ta e1a e2a u2",
    "ib e0a e3a ib",
    "ia ta e1a e0a",
    "ib ia e3a u3",
    "ta e1a e0a ib",
    "ia ta ia e1a",
    "e0a u1 u0 ib",
    "ib ui ta ta",
    "ur",
)


def split(v):
    hi = v.astype(BF)
    return hi, (v - hi.astype(F32)).astype(BF)


def dot(a, b, dims):
    return lax.dot_general(a, b, dims, preferred_element_type=F32)


def mm(a, b, dims=NN):
    return dot(a[0], b[0], dims) + (dot(a[1], b[0], dims) + dot(a[0], b[1], dims))


def bag_counts(part_ref, f, here, width):
    row = lax.broadcasted_iota(jnp.int32, (16, width), 0).astype(F32).astype(BF)
    zero = jnp.zeros((16, width), BF)
    weights = [jnp.broadcast_to(part_ref[0, f, s : s + 1, here], (16, width)).astype(BF) for s in range(4)]
    offsets = [jnp.broadcast_to(part_ref[1, f, s : s + 1, here], (16, width)).astype(BF) - row for s in range(4)]
    low, high = [], []
    for t in range(8):
        start = jnp.full((16, width), 16 * t, BF)
        hit = [jnp.where(offsets[s] == start, weights[s], zero) for s in range(4)]
        both = (hit[0] + hit[1]) + (hit[2] + hit[3])
        whole = (both + 128.0) - 128.0
        low.append(both - whole)
        high.append(whole)
    return jnp.concatenate(low + high, 0)


def step_kernel(n, chunks, total_rows, counts, *refs):
    hbm, refs = refs[:31], refs[31:]
    outs, refs = refs[:37], refs[37:]
    ids_hbm, len_hbm, dense_hbm, lab_hbm = hbm[:4]
    up_hbm, dn_hbm, upb_hbm = hbm[10], hbm[13], hbm[16]
    params = [outs[4 * k : 4 * k + 4] for k in range(9)]
    rms_ref = outs[36]
    tab_ref, w_raw, upo_ref, dno_ref, upbo_ref, gate_ref, tw_ref, tout_ref, bias_ref = [p[0] for p in params]
    (
        ids_ref,
        len_ref,
        dense_ref,
        lab_ref,
        upx_ref,
        dnx_ref,
        upbx_ref,
        brow,
        part,
        w_in,
        w_in_t,
        w_in_b,
        up_b,
        up_t,
        dn_b,
        dn_t,
        tw_b,
        gate_t,
        cols,
        bcol,
        feat,
        x,
        h,
        bpd,
        bpu,
        dsu,
        mixed,
        bpt,
        bgl,
        row_sums,
        bi,
        bp,
        grads,
        total_e,
        total_r,
        r_core,
        r_sum,
        in_sem,
        w_send,
        w_recv,
        s_sem,
        v_sem,
    ) = refs
    dp = lax.axis_index("dp")
    hid = lax.axis_index("hid")
    core_peer = (dp, 1 - hid)

    def group(stride, size):
        me = dp // stride % size
        others = [(me + k) % size for k in range(1, size)]
        return me, [(q, (dp + (q - me) * stride, hid)) for q in others]

    groups = {"x": group(1, 2), "y": group(2, 2), "z": group(4, n // 4), "p": group(1, 4), "a": group(1, n)}

    barrier = pltpu.get_barrier_semaphore()
    everyone = [core_peer] + [peer for _, peer in groups["a"][1]]
    for peer in everyone:
        pl.semaphore_signal(barrier, inc=1, device_id=peer, device_id_type=MESH)

    rows = ids_ref.shape[2]
    lanes = pl.ds(pl.multiple_of(hid * rows, rows), rows)
    order = (0, 1, 2, 3, 4, 5, 6, 7, 8)
    pairs = [(ids_hbm.at[:, :, lanes], ids_ref), (len_hbm.at[:, lanes], len_ref)]
    pairs += [(hbm[4 + 3 * k], params[k][0]) for k in order]
    pairs += [(dense_hbm.at[:, lanes], dense_ref), (lab_hbm.at[:, lanes], lab_ref)]
    for j in (1, 2):
        pairs += [(hbm[4 + 3 * k + j], params[k][j]) for k in order]
    loads = [pltpu.make_async_copy(src, dst, in_sem.at[k]) for k, (src, dst) in enumerate(pairs)]
    for load in loads[:13]:
        load.start()

    def remote(src, dst, send, recv, peer):
        return pltpu.make_async_remote_copy(
            src_ref=src, dst_ref=dst, send_sem=send, recv_sem=recv, device_id=peer, device_id_type=MESH
        )

    pl.semaphore_wait(barrier, len(everyone))
    weights = [
        remote(src, dst, w_send.at[k], w_recv.at[k], core_peer)
        for k, (src, dst) in enumerate(((up_hbm, upx_ref), (dn_hbm, dnx_ref), (upb_hbm, upbx_ref)))
    ]
    for copy in weights:
        copy.start()

    loads[0].wait()
    loads[1].wait()
    slot = lax.broadcasted_iota(jnp.int32, (4, rows), 0)
    for f in range(FIELDS):
        used = jnp.broadcast_to(len_ref[f : f + 1, :], (4, rows)) > slot
        ident = ids_ref[f]
        part[0, f] = jnp.where(used, jnp.where(ident < 128, 0.0625, 1.0), 0.0)
        part[1, f] = jnp.bitwise_and(ident, 127).astype(F32)
    for load in loads[2:13]:
        load.wait()

    sixteen = jnp.where(lax.broadcasted_iota(jnp.int32, (EMB, VOCAB), 1) < 128, 16.0, 1.0)
    width = 256

    def pool_fields(i, carry):
        for u in range(2):
            f = 2 * i + u
            table = jnp.concatenate(split(tab_ref[f] * sixteen), 0)
            at = pl.ds(pl.multiple_of(EMB * f, EMB), EMB)
            for j in range(rows // width):
                here = slice(width * j, width * (j + 1))
                both = dot(table, bag_counts(part, f, here, width), NN)
                hi, lo = split(both[0:EMB] + both[EMB : 2 * EMB])
                feat[0, at, here] = hi
                feat[1, at, here] = lo
        return carry

    lax.fori_loop(0, FIELDS // 2, pool_fields, 0)
    for load in loads[13:]:
        load.start()

    brow[0:1, 0:1024] = bias_ref[0:1024].reshape(1, 1024)
    brow[0:1, 1024:NB] = bias_ref[1024:NB].reshape(1, NB - 1024)
    biases = brow[0:1, 0:NB]
    row = lax.broadcasted_iota(jnp.int32, (8, D), 0)
    in_bias = jnp.broadcast_to(biases[:, 0:D], (8, D))
    w_in[0:IN_ROWS, :] = w_raw[...]
    w_in[424:432, :] = jnp.where(row == 5, in_bias, jnp.where(row < 5, w_in[424:432, :], 0.0))
    w_in[432:512, :] = jnp.zeros((80, D), F32)
    for i in range(4):
        hi, lo = split(w_in[128 * i : 128 * (i + 1), :].T)
        w_in_t[0, :, 128 * i : 128 * (i + 1)] = hi
        w_in_t[1, :, 128 * i : 128 * (i + 1)] = lo
    hi, lo = split(w_in[0:POOLED, :])
    w_in_b[0] = hi
    w_in_b[1] = lo

    def expert_weights(k, up_ref, dn_ref):
        for e in range(EXPERTS):
            c = 256 * e + 128 * k
            up, down = up_ref[e], dn_ref[e]
            hi, lo = split(up)
            up_b[0, :, c : c + 128] = hi
            up_b[1, :, c : c + 128] = lo
            hi, lo = split(up.T)
            up_t[0, c : c + 128, :] = hi
            up_t[1, c : c + 128, :] = lo
            hi, lo = split(down)
            dn_b[c : c + 128, 0:128] = hi
            dn_b[c : c + 128, 128:256] = lo
            hi, lo = split(down.T)
            dn_t[0, e, :, 128 * k : 128 * k + 128] = hi
            dn_t[1, e, :, 128 * k : 128 * k + 128] = lo

    expert_weights(0, upo_ref, dno_ref)
    gate8 = jnp.concatenate([gate_ref[0], gate_ref[1]], 0)
    hi, lo = split(jnp.concatenate([gate8, jnp.zeros((8, D), F32)], 0))
    up_t[0, 1024:1040, :] = hi
    up_t[1, 1024:1040, :] = lo
    for i in range(4):
        tile = jnp.concatenate([gate8[:, 128 * i : 128 * (i + 1)], jnp.zeros((120, 128), F32)], 0).T
        hi, lo = split(tile)
        at = slice(128 * i, 128 * (i + 1))
        gate_t[at, 0:16] = hi[:, 0:16]
        gate_t[at, 16:32] = hi[:, 0:16]
        gate_t[at, 32:48] = lo[:, 0:16]
    for t in range(TASKS):
        hi, lo = split(tw_ref[t])
        tw_b[TH * t : TH * t + TH, 0:128] = hi
        tw_b[TH * t : TH * t + TH, 128:256] = lo
    tw_t = split(jnp.concatenate([tw_ref[0], tw_ref[1]], 0).T)
    x[0, D : D + 16, :] = jnp.ones((16, rows), BF)
    x[1, D : D + 16, :] = jnp.zeros((16, rows), BF)
    hi, lo = split(jnp.concatenate([dense_ref[...], jnp.ones((1, rows), F32), jnp.zeros((2, rows), F32)], 0))
    feat[0, POOLED:432, :] = hi
    feat[1, POOLED:432, :] = lo

    for copy in weights:
        copy.wait_recv()
    expert_weights(1, upx_ref, dnx_ref)
    bcol[...] = jnp.zeros((128, 128), F32)
    bcol[0:4, :] = upbo_ref[...]
    bcol[4:8, :] = upbx_ref[...]
    for e in range(EXPERTS):
        bcol[8 + e : 9 + e, :] = biases[:, 512 + 128 * e : 640 + 128 * e]
    bcol[12:13, :] = biases[:, 1032:1160]
    bcol[13:14, 0:64] = tout_ref[0:1, :]
    bcol[13:14, 64:128] = tout_ref[1:2, :]
    bcol[14:15, 0:8] = biases[:, 1024:1032]
    cols[...] = bcol[...].T
    row_sums[...] = jnp.zeros((128, 128), F32)

    scale = float(total_rows) ** -0.5
    fs = (feat[0], feat[1])
    xv = mm((w_in_t[0, :, 0:432], w_in_t[1, :, 0:432]), fs)
    squares = [jnp.sum(xv * xv, keepdims=True)]
    xs = split(xv)
    x[0, 0:D, :] = xs[0]
    x[1, 0:D, :] = xs[1]
    eouts, slopes = [], []
    sums = [0.0, 0.0, 0.0]
    for e in range(EXPERTS):
        c = 256 * e
        end = c + 256 if e < EXPERTS - 1 else c + 272
        pre = mm((up_t[0, c:end, :], up_t[1, c:end, :]), xs)
        gate_logits = pre[256:264] + cols[0:8, 14:15] if e == EXPERTS - 1 else None
        pre = pre[0:256] + jnp.concatenate([cols[:, e : e + 1], cols[:, 4 + e : 5 + e]], 0)
        s = jax.nn.sigmoid(pre)
        hv = pre * s
        dsu[c : c + 256, :] = s + hv * (1.0 - s)
        sums[0] = sums[0] + jnp.sum(hv * hv, keepdims=True)
        hs = split(hv)
        h[0, c : c + 256, :] = hs[0]
        h[1, c : c + 256, :] = hs[1]
        pre = mm((dn_t[0, e], dn_t[1, e]), hs) + cols[:, 8 + e : 9 + e]
        s = jax.nn.sigmoid(pre)
        out = pre * s
        sums[1] = sums[1] + jnp.sum(out * out, keepdims=True)
        eouts.append(out)
        slopes.append(s + out * (1.0 - s))
    gates = []
    for t in range(TASKS):
        r = [gate_logits[4 * t + e : 4 * t + e + 1] for e in range(EXPERTS)]
        top = jnp.maximum(jnp.maximum(r[0], r[1]), jnp.maximum(r[2], r[3]))
        ex = [jnp.exp(v - top) for v in r]
        inv = 1.0 / ((ex[0] + ex[1]) + (ex[2] + ex[3]))
        gates.append([v * inv for v in ex])
    back_mixed, back_logit = [], []
    for t in range(TASKS):
        z = slice(TH * t, TH * t + TH)
        o = slice(OUT * t, OUT * t + OUT)
        g = gates[t]
        ms = split(g[0] * eouts[0] + g[1] * eouts[1] + g[2] * eouts[2] + g[3] * eouts[3])
        mixed[t, 0:OUT, :] = ms[0]
        mixed[t, OUT : 2 * OUT, :] = ms[1]
        w = tw_b[z, :]
        pre = dot(w, jnp.concatenate([ms[0], ms[0]], 0), NN) + dot(w[:, 0:128], ms[1], NN) + cols[z, 12:13]
        s = jax.nn.sigmoid(pre)
        th = pre * s
        sums[2] = sums[2] + jnp.sum(th * th, keepdims=True)
        wo = cols[z, 13:14]
        logit = jnp.sum(th * wo, axis=0, keepdims=True) + biases[:, 1160 + t : 1161 + t]
        back = (jax.nn.sigmoid(logit) - lab_ref[t : t + 1, :].astype(F32)) * scale
        row_sums[z, 5:6] = jnp.sum(back * th, axis=1, keepdims=True)
        row_sums[8 + t : 9 + t, 6:7] = jnp.sum(back, axis=1, keepdims=True)
        back = back * wo * (s + th * (1.0 - s))
        row_sums[z, 4:5] = jnp.sum(back, axis=1, keepdims=True)
        bs = split(back)
        bpt[t, 0:TH, :] = bs[0]
        bpt[t, TH : 2 * TH, :] = bs[1]
        w = [v[:, z] for v in tw_t]
        bm = dot(jnp.concatenate([w[0], w[1], w[0]], 1), jnp.concatenate([bs[0], bs[0], bs[1]], 0), NN)
        back_mixed.append(bm)
        bg = [jnp.sum(bm * eouts[e], axis=0, keepdims=True) for e in range(EXPERTS)]
        mean = g[0] * bg[0] + g[1] * bg[1] + g[2] * bg[2] + g[3] * bg[3]
        back_logit += [g[e] * (bg[e] - mean) for e in range(EXPERTS)]
    back_logit = jnp.concatenate(back_logit, 0)
    row_sums[0:8, 6:7] = jnp.sum(back_logit, axis=1, keepdims=True)
    bs = split(jnp.concatenate([back_logit, jnp.zeros((8, rows), F32)], 0))
    bgl[0:16] = bs[0]
    bgl[16:32] = bs[1]
    bgl[32:48] = bs[0]
    squares += sums

    def expert_back(e):
        c = 256 * e
        back = (gates[0][e] * back_mixed[0] + gates[1][e] * back_mixed[1]) * slopes[e]
        row_sums[:, e : e + 1] = jnp.sum(back, axis=1, keepdims=True)
        bs = split(back)
        bpd[0, OUT * e : OUT * e + OUT, :] = bs[0]
        bpd[1, OUT * e : OUT * e + OUT, :] = bs[1]
        w = dn_b[c : c + 256, :]
        back = dot(w, jnp.concatenate([bs[0], bs[0]], 0), NN) + dot(w[:, 0:128], bs[1], NN)
        bs = split(back * dsu[c : c + 256, :])
        bpu[0, c : c + 256, :] = bs[0]
        bpu[1, c : c + 256, :] = bs[1]

    rep_base = chunks[EXPERTS][0][0]
    sent = []
    used = {"sem": 0, "row": 0}

    def sems(count):
        first = used["sem"]
        used["sem"] += count
        return first

    class Piece:
        def __init__(self, base, size, steps, expert):
            self.base, self.size, self.expert = base, size, expert
            self.steps = [groups[k] for k in steps]
            self.plan = self.stages()

        def at(self, start, size):
            return pl.ds(pl.multiple_of(start, 8), size)

        def total(self, start, size):
            if self.expert:
                return total_e.at[self.at(start, size)]
            return total_r.at[hid, self.at(start - rep_base, size)]

        def start(self, copies):
            for copy in copies:
                copy.start()
            sent.extend(copies)
            return copies

        def stages(self):
            rng = self.at(self.base, self.size)
            k = sems(1)
            yield self.start([remote(grads.at[1, rng], r_core.at[rng], s_sem.at[k], v_sem.at[k], core_peer)])
            grads[0, rng, :] += r_core[rng, :]
            start, size, held = self.base, self.size, []
            for me, others in self.steps:
                m = len(others) + 1
                held.append((start, size))
                size //= m
                k, row = sems(m - 1), used["row"]
                used["row"] += (m - 1) * size
                copies = []
                for j, (q, peer) in enumerate(others):
                    slot = m - 2 - j
                    src, dst = self.at(start + q * size, size), self.at(row + slot * size, size)
                    copies.append(remote(grads.at[0, src], r_sum.at[dst], s_sem.at[k + j], v_sem.at[k + slot], peer))
                yield self.start(copies)
                start = start + me * size
                mine = self.at(start, size)
                total = grads[0, mine, :]
                for slot in range(m - 1):
                    total = total + r_sum[row + slot * size : row + slot * size + size, :]
                if len(held) < len(self.steps):
                    grads[0, mine, :] = total
                else:
                    self.total(start, size)[...] = total
            for me, others in reversed(self.steps):
                m = len(others) + 1
                out = self.total(start, size)
                k = sems(m - 1)
                yield self.start(
                    [remote(out, out, s_sem.at[k + j], v_sem.at[k + m - 2 - j], peer) for j, (_, peer) in enumerate(others)]
                )
                start, size = held.pop()
            if not self.expert:
                out = self.total(self.base, self.size)
                k = sems(1)
                yield self.start([remote(out, out, s_sem.at[k], v_sem.at[k], core_peer)])

        def advance(self):
            for copy in getattr(self, "copies", []):
                copy.wait_recv()
            self.copies = next(self.plan, [])

    names = ("e0", "e1", "e2", "e3", "i", "t")
    pieces = {}
    for k, (name, parts) in enumerate(zip(names, chunks)):
        for j, (base, size, steps) in enumerate(parts):
            pieces[name + "abcd"[j]] = Piece(base, size, steps, k < EXPERTS)

    def owner(k):
        return (k + hid) % 2

    e_base = [chunks[e][0][0] for e in range(EXPERTS)]
    e_size = chunks[1][0][0] - chunks[0][0][0]
    i_base, t_base = chunks[EXPERTS][0][0], chunks[EXPERTS + 1][0][0]
    t_size = grads.shape[1] - t_base
    misc = t_base + MISC_AT
    grads[:, misc : t_base + t_size, :] = jnp.zeros((2, t_size - MISC_AT, 128), F32)

    def update(k, at, g):
        w_ref, m_ref, a_ref, r_ref = params[k]
        new_m = MOMENTUM_RATE * m_ref[at] + g
        new_w = w_ref[at] - LEARN_RATE * (g + MOMENTUM_RATE * new_m)
        w_ref[at] = new_w
        m_ref[at] = new_m
        a_ref[at] = AVERAGE_RATE * a_ref[at] + (1.0 - AVERAGE_RATE) * new_w
        r_ref[at] = new_w.astype(BF)

    everything = slice(None)
    to = t_base - rep_base

    def update_expert(e):
        update(2, (e,), total_e[e_base[e] : e_base[e] + D, :])
        update(3, (e,), total_e[e_base[e] + D : e_base[e] + E_ROWS, :])

    def update_inputs():
        for k in range(4):
            at = 432 * (k % 2)
            update(1, (everything, slice(128 * k, 128 * k + 128)), total_r[k // 2, at : at + IN_ROWS, :])

    def update_tables(first, last):
        for f in range(first, last):
            for k in range(2):
                g = total_r[k, to + EMB * f : to + EMB * f + EMB, :]
                update(0, (f, everything, slice(128 * k, 128 * k + 128)), g)

    def update_rest():
        update(4, (everything,), total_r[hid, to + UPB_AT : to + UPB_AT + 4, :])
        for k in range(4):
            at = to + GATE_AT + 8 * (k % 2)
            for s in range(TASKS):
                g = total_r[k // 2, at + 4 * s : at + 4 * s + 4, :]
                update(5, (s, everything, slice(128 * k, 128 * k + 128)), g)
        for s in range(TASKS):
            update(6, (s,), total_r[s, to + TOWER_AT : to + TOWER_AT + TH, :])
        at = to + MISC_AT
        g = total_r[0, at + 5 : at + 6, :]
        for s in range(TASKS):
            update(7, (slice(s, s + 1), everything), g[:, TH * s : TH * s + TH])
        for k in range(4):
            r = 432 * (k % 2) + IN_ROWS
            brow[0:1, 128 * k : 128 * k + 128] = total_r[k // 2, r : r + 1, :]
            brow[0:1, D + 128 * k : D + 128 * k + 128] = total_r[0, at + k : at + k + 1, :]
        brow[0:1, 1024:1032] = total_r[0, at + 6 : at + 7, 0:8]
        brow[0:1, 1032:1160] = total_r[0, at + 4 : at + 5, :]
        brow[0:1, 1160:1162] = total_r[0, at + 6 : at + 7, 8:10]
        update(8, (everything,), brow[0, 0:NB])
        lane = lax.broadcasted_iota(jnp.int32, (1, 128), 1)
        inverse = jnp.zeros((1, 128), F32)
        for k, count in enumerate(counts):
            inverse = jnp.where(lane == k, 1.0 / count, inverse)
        brow[1:2, 0:128] = jnp.sqrt(total_r[0, at + 7 : at + 8, :] * inverse + 1e-06)
        rms_ref[...] = brow[1, 0:4]

    updates = {f"u{e}": functools.partial(update_expert, e) for e in range(EXPERTS)}
    table_split = FIELDS if len(chunks[5]) == 1 else min(FIELDS, sum(part[1] for part in chunks[5][:-1]) // EMB)
    updates["ui"] = update_inputs
    updates["ut"] = functools.partial(update_tables, 0, table_split)
    updates["ur"] = lambda: (update_tables(table_split, FIELDS), update_rest())

    done = set()

    def run(*steps):
        for name in steps:
            if name in updates:
                if not done:
                    for load in loads[13:]:
                        load.wait()
                done.add(name)
                updates[name]()
            elif name in pieces:
                pieces[name].advance()

    def first_gradients(e):
        c, base = 256 * e, e_base[e]
        g = mm((x[0], x[1]), (bpu[0, c : c + 256, :], bpu[1, c : c + 256, :]), NT)
        grads[0, base : base + D, :] = g[0:D, 0:128]
        grads[1, base : base + D, :] = g[0:D, 128:256]
        upb = t_base + UPB_AT + e
        grads[0, upb : upb + 1, :] = g[D : D + 1, 0:128]
        grads[1, upb : upb + 1, :] = g[D : D + 1, 128:256]

    def second_gradients(e):
        c, o, base = 256 * e, 128 * e, e_base[e]
        hi, lo = bpd[0, o : o + 128, :], bpd[1, o : o + 128, :]
        g = dot(h[0, c : c + 256, :], jnp.concatenate([hi, lo], 0), NT)
        g = (g[:, 0:128] + g[:, 128:256]) + dot(h[1, c : c + 256, :], hi, NT)
        grads[0, base + D : base + E_ROWS, :] = g[0:128]
        grads[1, base + D : base + E_ROWS, :] = g[128:256]
        if e_size > E_ROWS:
            grads[:, base + E_ROWS : base + e_size, :] = jnp.zeros((2, e_size - E_ROWS, 128), F32)

    def inputs_back(k):
        if k == 0:
            b = mm((up_b[0], up_b[1]), (bpu[0], bpu[1])) + dot(gate_t[...], bgl[...], NN)
            bs = split(b)
            bi[0] = bs[0]
            bi[1] = bs[1]
        else:
            ps = split(mm((w_in_b[0], w_in_b[1]), (bi[0], bi[1])))
            bp[0] = ps[0]
            bp[1] = ps[1]

    def input_gradients(k):
        g = mm((feat[0], feat[1]), (bi[0, 256 * k : 256 * k + 256, :], bi[1, 256 * k : 256 * k + 256, :]), NT)
        grads[owner(k), i_base : i_base + 432, :] = g[:, 0:128]
        grads[owner(k), i_base + 432 : i_base + I_ROWS, :] = g[:, 128:256]
        if t_base - i_base > I_ROWS:
            grads[:, i_base + I_ROWS : t_base, :] = jnp.zeros((2, t_base - i_base - I_ROWS, 128), F32)

    def small_gradients():
        g = dot(x[0], bgl[0:32], NT)
        g = g[0:D, 0:8] + g[0:D, 16:24] + dot(x[1], bgl[0:16], NT)[0:D, 0:8]
        for k in range(4):
            tile = jnp.concatenate([g[128 * k : 128 * k + 128], jnp.zeros((128, 120), F32)], 1).T
            at = t_base + GATE_AT + 8 * (k % 2)
            grads[owner(k // 2), at : at + 8, :] = tile[0:8]
        for t in range(TASKS):
            g = dot(bpt[t], mixed[t], NT)
            g = (g[0:TH, 0:OUT] + g[0:TH, OUT : 2 * OUT]) + g[TH : 2 * TH, 0:OUT]
            grads[owner(t), t_base + TOWER_AT : t_base + TOWER_AT + TH, :] = g
        lane = lax.broadcasted_iota(jnp.int32, (1, 128), 1)
        m = owner(0)
        grads[m, misc : misc + 8, :] = row_sums[...].T[0:8]
        total = jnp.zeros((1, 128), F32)
        for k in range(4):
            total = jnp.where(lane == k, squares[k], total)
        grads[m, misc + 7 : misc + 8, :] = total

    def table_fields(i, carry):
        for u in range(2):
            f = 2 * i + u
            at = pl.ds(pl.multiple_of(EMB * f, EMB), EMB)
            total = jnp.zeros((2 * EMB, VOCAB), F32)
            for j in range(rows // width):
                here = slice(width * j, width * (j + 1))
                back = jnp.concatenate([bp[0, at, here], bp[1, at, here]], 0)
                total = total + dot(back, bag_counts(part, f, here, width), NT)
            g = (total[0:EMB] + total[EMB : 2 * EMB]) * sixteen
            at = pl.ds(pl.multiple_of(t_base + EMB * f, EMB), EMB)
            grads[owner(0), at, :] = g[:, 0:128]
            grads[owner(1), at, :] = g[:, 128:256]
        return carry

    def tables(first, last):
        lax.fori_loop(first, last, table_fields, 0)

    work = {
        "b": expert_back,
        "G": first_gradients,
        "D": second_gradients,
        "h": inputs_back,
        "i": input_gradients,
        "s": lambda k: small_gradients(),
    }
    for item in SCHEDULE:
        if item[0:2] == "!j":
            tables(*[int(v) for v in item[2:].split("-")])
        elif item[0] == "!":
            work[item[1]](int(item[2]))
        else:
            run(*item.split())
    while any(piece.copies for piece in pieces.values()):
        run(*[name for name in pieces if pieces[name].copies])
    run(*[name for name in updates if name not in done])
    for copy in sent + weights:
        copy.wait_send()


def layout(n):
    unit = 8 * n
    chunks, base = [], 0
    for size, parts in zip([E_ROWS] * EXPERTS + [I_ROWS, T_ROWS], PARTS):
        left = -(-size // unit) * unit
        pieces = []
        for j, (rows, steps) in enumerate(parts):
            take = left if j == len(parts) - 1 else min(left, -(-rows // unit) * unit)
            if take:
                pieces.append((base, take, steps))
            base += take
            left -= take
        chunks.append(pieces)
    return chunks, base


def step(args, shapes, n, total_rows):
    rows = args[0].shape[2] // 2
    chunks, size = layout(n)
    e_all = chunks[EXPERTS][0][0]
    count = 0
    for parts in chunks:
        for _, _, steps in parts:
            count += 2 + 2 * sum({"x": 1, "y": 1, "p": 3, "z": n // 4 - 1, "a": n - 1}[k] for k in steps)
    vm = pltpu.VMEM
    scratch = [
        vm((FIELDS, 4, rows), jnp.int32),
        vm((FIELDS, rows), jnp.int32),
        vm((13, rows), F32),
        vm((TASKS, rows), jnp.int32),
        vm((EXPERTS, D, 128), F32),
        vm((EXPERTS, 128, OUT), F32),
        vm((EXPERTS, 128), F32),
        vm((8, 1280), F32),
        vm((2, FIELDS, 4, rows), F32),
        vm((512, D), F32),
        vm((2, D, 512), BF),
        vm((2, POOLED, D), BF),
        vm((2, D, EXPERTS * HID), BF),
        vm((2, EXPERTS * HID + 16, D), BF),
        vm((EXPERTS * HID, 2 * OUT), BF),
        vm((2, EXPERTS, OUT, HID), BF),
        vm((TASKS * TH, 2 * OUT), BF),
        vm((D, 48), BF),
        vm((128, 128), F32),
        vm((128, 128), F32),
        vm((2, 432, rows), BF),
        vm((2, D + 16, rows), BF),
        vm((2, EXPERTS * HID, rows), BF),
        vm((2, EXPERTS * OUT, rows), BF),
        vm((2, EXPERTS * HID, rows), BF),
        vm((EXPERTS * HID, rows), F32),
        vm((TASKS, 2 * OUT, rows), BF),
        vm((TASKS, 2 * TH, rows), BF),
        vm((48, rows), BF),
        vm((128, 128), F32),
        vm((2, D, rows), BF),
        vm((2, POOLED, rows), BF),
        vm((2, size, 128), F32),
        vm((e_all, 128), F32),
        vm((2, size - e_all, 128), F32),
        vm((size, 128), F32),
        vm((size, 128), F32),
        pltpu.SemaphoreType.DMA((31,)),
        pltpu.SemaphoreType.DMA((3,)),
        pltpu.SemaphoreType.DMA((3,)),
        pltpu.SemaphoreType.DMA((count,)),
        pltpu.SemaphoreType.DMA((count,)),
    ]
    counts = [float(total_rows * c) for c in (D, EXPERTS * HID, EXPERTS * OUT, TASKS * TH)]
    return pl.pallas_call(
        functools.partial(step_kernel, n, chunks, total_rows, counts),
        out_shape=[pltpu.VMEM(shape, dtype) for shape, dtype in shapes],
        in_specs=[pl.BlockSpec(memory_space=pl.ANY)] * len(args),
        out_specs=[pl.BlockSpec(memory_space=pltpu.VMEM)] * len(shapes),
        scratch_shapes=scratch,
        compiler_params=pltpu.CompilerParams(collective_id=0, has_side_effects=True, vmem_limit_bytes=50 << 20),
        name="step",
    )(*args)


def write_kernel(*refs):
    sems = refs[-1]
    k = (len(refs) - 1) // 2
    copies = [pltpu.make_async_copy(refs[i], refs[k + i], sems.at[i]) for i in range(k)]
    for copy in copies:
        copy.start()
    for copy in copies:
        copy.wait()


def local(*args):
    n = lax.axis_size("dp")
    ids, lengths, dense, labels = args[:4]
    total_rows = ids.shape[0] * n
    params = [list(args[4 + 3 * k : 7 + 3 * k]) for k in range(9)]
    for k in (0, 5, 6):
        params[k] = [v.transpose(0, 2, 1) for v in params[k]]
    shapes = []
    for p in params:
        shapes += [(p[0].shape, F32)] * 3 + [(p[0].shape, BF)]
    shapes.append(((4,), F32))
    flat = [ids.transpose(1, 2, 0), lengths.T, dense.T, labels.T] + [v for p in params for v in p]
    results = step(flat, shapes, n, total_rows)
    results = [pltpu.with_memory_space_constraint(v, pltpu.VMEM) for v in results]
    outs = pl.pallas_call(
        write_kernel,
        out_shape=[jax.ShapeDtypeStruct(shape, dtype) for shape, dtype in shapes],
        in_specs=[pl.BlockSpec(memory_space=pltpu.VMEM)] * len(shapes),
        out_specs=[pl.BlockSpec(memory_space=pl.ANY)] * len(shapes),
        scratch_shapes=[pltpu.SemaphoreType.DMA((len(shapes),))],
        compiler_params=pltpu.CompilerParams(vmem_limit_bytes=1 << 20),
        name="write",
    )(*results)
    outs = list(outs)
    for k in (0, 5, 6):
        outs[4 * k : 4 * k + 4] = [v.transpose(0, 2, 1) for v in outs[4 * k : 4 * k + 4]]
    return tuple(outs)


def solution(mesh):
    up, down, bias = P(None, None, "hid"), P(None, "hid", None), P(None, "hid")
    rep = P()
    return jax.shard_map(
        local,
        mesh=mesh,
        in_specs=(P("dp", None, None), P("dp", None), P("dp", None), P("dp", None))
        + (rep,) * 6
        + (up,) * 3
        + (down,) * 3
        + (bias,) * 3
        + (rep,) * 12,
        out_specs=(rep,) * 8 + (up,) * 4 + (down,) * 4 + (bias,) * 4 + (rep,) * 17,
        check_vma=False,
    )
```

```python
import functools

import jax
import jax.numpy as jnp
from jax import lax
from jax.experimental import pallas as pl
from jax.experimental.pallas import tpu as pltpu
from jax.sharding import PartitionSpec as P

D = 512
HID = 256
OUT = 128
TH = 64
TASKS = 2
EXPERTS = 4
FIELDS = 26
VOCAB = 256
EMB = 16
POOLED = 416
IN_ROWS = 429
NB = 1162

MOMENTUM_RATE = 0.9
LEARN_RATE = 0.3
AVERAGE_RATE = 0.9

BF = jnp.bfloat16
F32 = jnp.float32
NN = (((1,), (0,)), ((), ()))
NT = (((1,), (1,)), ((), ()))
MESH = pl.DeviceIdType.MESH

E_ROWS = 640
I_BASE = EXPERTS * E_ROWS
I_ROWS = 864
GATE_AT = 416
TOWER_AT = 432
MISC_AT = 496
UPB_AT = 504
T_ROWS = 512


PARTS = (
    ((640, "pz"),),
    ((256, "zyx"), (256, "zyx"), (128, "pz"),),
    ((640, "pz"),),
    ((256, "xyz"), (384, "yxz"),),
    ((256, "zp"), (640, "pz"),),
    ((256, "pz"), (256, "pz"),),
)
SCHEDULE = (
    "!b0",
    "!b3",
    "!D0",
    "!G0",
    "e0a",
    "!b1",
    "!G1",
    "e0a e1a e1b",
    "!b2",
    "!D1",
    "e1c e1a",
    "!D2",
    "!G2",
    "e2a e1c",
    "!G3",
    "e1b e3a",
    "!D3",
    "e2a e3b",
    "!h0",
    "e0a e3b e3a",
    "!i0",
    "e2a",
    "!i1",
    "ib e1b e1a ia",
    "!s0",
    "ib ia",
    "!j0-8",
    "e0a ta e3b e3a",
    "!j8-10",
    "e2a ta",
    "!j10-13",
    "tb e1b e1a e1c",
    "ia ib e3a tb",
    "e3b e0a e1b e1a",
    "ta ia e2a e1c",
    "tb ib e3a e3b",
    "ta e1b e1a e0a",
    "e1c u0 ia tb",
    "ib e3a e1b e1a",
    "e2a e3b u2 ta",
    "e1c ia tb ia",
    "ib e3a e3b ib",
    "ui e1b ta ta",
    "tb ut e3a e1a",
    "tb u1 e3b u3",
    "ur",
)


def split(v):
    hi = v.astype(BF)
    return hi, (v - hi.astype(F32)).astype(BF)


def dot(a, b, dims):
    return lax.dot_general(a, b, dims, preferred_element_type=F32)


def blocks(size, step=128):
    return [slice(k, min(size, k + step)) for k in range(0, size, step)]


def mm(a, b, dims=NN):
    return dot(a[0], b[0], dims) + (dot(a[1], b[0], dims) + dot(a[0], b[1], dims))


def bag_counts(part_ref, f, here, width):
    row = lax.broadcasted_iota(jnp.int32, (16, width), 0).astype(F32).astype(BF)
    zero = jnp.zeros((16, width), BF)
    weights = [jnp.broadcast_to(part_ref[0, f, s : s + 1, here], (16, width)).astype(BF) for s in range(4)]
    offsets = [jnp.broadcast_to(part_ref[1, f, s : s + 1, here], (16, width)).astype(BF) - row for s in range(4)]
    low, high = [], []
    for t in range(8):
        start = jnp.full((16, width), 16 * t, BF)
        hit = [jnp.where(offsets[s] == start, weights[s], zero) for s in range(4)]
        both = (hit[0] + hit[1]) + (hit[2] + hit[3])
        whole = (both + 128.0) - 128.0
        low.append(both - whole)
        high.append(whole)
    return jnp.concatenate(low + high, 0)


def step_kernel(n, chunks, total_rows, counts, *refs):
    hbm, refs = refs[:31], refs[31:]
    outs, refs = refs[:37], refs[37:]
    ids_hbm, len_hbm, dense_hbm, lab_hbm = hbm[:4]
    up_hbm, dn_hbm, upb_hbm = hbm[10], hbm[13], hbm[16]
    params = [outs[4 * k : 4 * k + 4] for k in range(9)]
    rms_ref = outs[36]
    tab_ref, w_raw, upo_ref, dno_ref, upbo_ref, gate_ref, tw_ref, tout_ref, bias_ref = [p[0] for p in params]
    (
        ids_ref,
        len_ref,
        dense_ref,
        lab_ref,
        upx_ref,
        dnx_ref,
        upbx_ref,
        brow,
        part,
        w_in,
        w_in_t,
        w_in_b,
        up_b,
        up_t,
        dn_b,
        dn_t,
        tw_b,
        gate_t,
        cols,
        bcol,
        feat,
        x,
        h,
        bpd,
        bpu,
        dsu,
        mixed,
        bpt,
        bgl,
        row_sums,
        bi,
        bp,
        grads,
        total_e,
        total_r,
        r_core,
        r_sum,
        in_sem,
        w_send,
        w_recv,
        s_sem,
        v_sem,
    ) = refs
    dp = lax.axis_index("dp")
    hid = lax.axis_index("hid")
    core_peer = (dp, 1 - hid)

    def group(stride, size):
        me = dp // stride % size
        others = [(me + k) % size for k in range(1, size)]
        return me, [(q, (dp + (q - me) * stride, hid)) for q in others]

    groups = {"x": group(1, 2), "y": group(2, 2), "z": group(4, n // 4), "p": group(1, 4), "a": group(1, n)}

    barrier = pltpu.get_barrier_semaphore()
    everyone = [core_peer] + [peer for _, peer in groups["a"][1]]
    for peer in everyone:
        pl.semaphore_signal(barrier, inc=1, device_id=peer, device_id_type=MESH)

    rows = ids_ref.shape[2]
    lanes = pl.ds(pl.multiple_of(hid * rows, rows), rows)
    order = (0, 1, 2, 3, 4, 5, 6, 7, 8)
    pairs = [(ids_hbm.at[:, :, lanes], ids_ref), (len_hbm.at[:, lanes], len_ref)]
    pairs += [(hbm[4 + 3 * k], params[k][0]) for k in order]
    pairs += [(dense_hbm.at[:, lanes], dense_ref), (lab_hbm.at[:, lanes], lab_ref)]
    for j in (1, 2):
        pairs += [(hbm[4 + 3 * k + j], params[k][j]) for k in order]
    loads = [pltpu.make_async_copy(src, dst, in_sem.at[k]) for k, (src, dst) in enumerate(pairs)]
    for load in loads[:13]:
        load.start()

    def remote(src, dst, send, recv, peer):
        return pltpu.make_async_remote_copy(
            src_ref=src, dst_ref=dst, send_sem=send, recv_sem=recv, device_id=peer, device_id_type=MESH
        )

    pl.semaphore_wait(barrier, len(everyone))
    weights = [
        remote(src, dst, w_send.at[k], w_recv.at[k], core_peer)
        for k, (src, dst) in enumerate(((up_hbm, upx_ref), (dn_hbm, dnx_ref), (upb_hbm, upbx_ref)))
    ]
    for copy in weights:
        copy.start()

    loads[0].wait()
    loads[1].wait()
    slot = lax.broadcasted_iota(jnp.int32, (4, rows), 0)
    for f in range(FIELDS):
        used = jnp.broadcast_to(len_ref[f : f + 1, :], (4, rows)) > slot
        ident = ids_ref[f]
        part[0, f] = jnp.where(used, jnp.where(ident < 128, 0.0625, 1.0), 0.0)
        part[1, f] = jnp.bitwise_and(ident, 127).astype(F32)
    for load in loads[2:13]:
        load.wait()

    sixteen = jnp.where(lax.broadcasted_iota(jnp.int32, (EMB, VOCAB), 1) < 128, 16.0, 1.0)
    width = 256

    for f in range(FIELDS):
        table = jnp.concatenate(split(tab_ref[f] * sixteen), 0)
        at = slice(EMB * f, EMB * f + EMB)
        for j in range(rows // width):
            here = slice(width * j, width * (j + 1))
            both = dot(table, bag_counts(part, f, here, width), NN)
            hi, lo = split(both[0:EMB] + both[EMB : 2 * EMB])
            feat[0, at, here] = hi
            feat[1, at, here] = lo
    for load in loads[13:]:
        load.start()

    brow[0:1, 0:1024] = bias_ref[0:1024].reshape(1, 1024)
    brow[0:1, 1024:NB] = bias_ref[1024:NB].reshape(1, NB - 1024)
    biases = brow[0:1, 0:NB]
    row = lax.broadcasted_iota(jnp.int32, (8, D), 0)
    in_bias = jnp.broadcast_to(biases[:, 0:D], (8, D))
    w_in[0:IN_ROWS, :] = w_raw[...]
    w_in[424:432, :] = jnp.where(row == 5, in_bias, jnp.where(row < 5, w_in[424:432, :], 0.0))
    w_in[432:512, :] = jnp.zeros((80, D), F32)
    for i in range(4):
        hi, lo = split(w_in[128 * i : 128 * (i + 1), :].T)
        w_in_t[0, :, 128 * i : 128 * (i + 1)] = hi
        w_in_t[1, :, 128 * i : 128 * (i + 1)] = lo
    hi, lo = split(w_in[0:POOLED, :])
    w_in_b[0] = hi
    w_in_b[1] = lo

    def expert_weights(k, up_ref, dn_ref):
        for e in range(EXPERTS):
            c = 256 * e + 128 * k
            up, down = up_ref[e], dn_ref[e]
            hi, lo = split(up)
            up_b[0, :, c : c + 128] = hi
            up_b[1, :, c : c + 128] = lo
            hi, lo = split(up.T)
            up_t[0, c : c + 128, :] = hi
            up_t[1, c : c + 128, :] = lo
            hi, lo = split(down)
            dn_b[c : c + 128, 0:128] = hi
            dn_b[c : c + 128, 128:256] = lo
            hi, lo = split(down.T)
            dn_t[0, e, :, 128 * k : 128 * k + 128] = hi
            dn_t[1, e, :, 128 * k : 128 * k + 128] = lo

    expert_weights(0, upo_ref, dno_ref)
    gate8 = jnp.concatenate([gate_ref[0], gate_ref[1]], 0)
    hi, lo = split(jnp.concatenate([gate8, jnp.zeros((8, D), F32)], 0))
    up_t[0, 1024:1040, :] = hi
    up_t[1, 1024:1040, :] = lo
    for i in range(4):
        tile = jnp.concatenate([gate8[:, 128 * i : 128 * (i + 1)], jnp.zeros((120, 128), F32)], 0).T
        hi, lo = split(tile)
        at = slice(128 * i, 128 * (i + 1))
        gate_t[at, 0:16] = hi[:, 0:16]
        gate_t[at, 16:32] = hi[:, 0:16]
        gate_t[at, 32:48] = lo[:, 0:16]
    for t in range(TASKS):
        hi, lo = split(tw_ref[t])
        tw_b[TH * t : TH * t + TH, 0:128] = hi
        tw_b[TH * t : TH * t + TH, 128:256] = lo
    tw_t = split(jnp.concatenate([tw_ref[0], tw_ref[1]], 0).T)
    x[0, D : D + 16, :] = jnp.ones((16, rows), BF)
    x[1, D : D + 16, :] = jnp.zeros((16, rows), BF)
    hi, lo = split(jnp.concatenate([dense_ref[...], jnp.ones((1, rows), F32), jnp.zeros((2, rows), F32)], 0))
    feat[0, POOLED:432, :] = hi
    feat[1, POOLED:432, :] = lo

    scale = float(total_rows) ** -0.5
    fs = (feat[0], feat[1])
    xv = mm((w_in_t[0, :, 0:432], w_in_t[1, :, 0:432]), fs)
    squares = [jnp.sum(xv * xv, keepdims=True)]
    xs = split(xv)
    x[0, 0:D, :] = xs[0]
    x[1, 0:D, :] = xs[1]
    for copy in weights:
        copy.wait_recv()
    expert_weights(1, upx_ref, dnx_ref)
    bcol[...] = jnp.zeros((128, 128), F32)
    bcol[0:4, :] = upbo_ref[...]
    bcol[4:8, :] = upbx_ref[...]
    for e in range(EXPERTS):
        bcol[8 + e : 9 + e, :] = biases[:, 512 + 128 * e : 640 + 128 * e]
    bcol[12:13, :] = biases[:, 1032:1160]
    bcol[13:14, 0:64] = tout_ref[0:1, :]
    bcol[13:14, 64:128] = tout_ref[1:2, :]
    bcol[14:15, 0:8] = biases[:, 1024:1032]
    cols[...] = bcol[...].T
    row_sums[...] = jnp.zeros((128, 128), F32)

    eouts, slopes = [], []
    sums = [0.0, 0.0, 0.0]
    for e in range(EXPERTS):
        c = 256 * e
        end = c + 256 if e < EXPERTS - 1 else c + 272
        pre = mm((up_t[0, c:end, :], up_t[1, c:end, :]), xs)
        gate_logits = pre[256:264] + cols[0:8, 14:15] if e == EXPERTS - 1 else None
        pre = pre[0:256] + jnp.concatenate([cols[:, e : e + 1], cols[:, 4 + e : 5 + e]], 0)
        s = jax.nn.sigmoid(pre)
        hv = pre * s
        dsu[c : c + 256, :] = s + hv * (1.0 - s)
        sums[0] = sums[0] + jnp.sum(hv * hv, keepdims=True)
        hs = split(hv)
        h[0, c : c + 256, :] = hs[0]
        h[1, c : c + 256, :] = hs[1]
        pre = mm((dn_t[0, e], dn_t[1, e]), hs) + cols[:, 8 + e : 9 + e]
        s = jax.nn.sigmoid(pre)
        out = pre * s
        sums[1] = sums[1] + jnp.sum(out * out, keepdims=True)
        eouts.append(out)
        slopes.append(s + out * (1.0 - s))
    gates = []
    for t in range(TASKS):
        r = [gate_logits[4 * t + e : 4 * t + e + 1] for e in range(EXPERTS)]
        top = jnp.maximum(jnp.maximum(r[0], r[1]), jnp.maximum(r[2], r[3]))
        ex = [jnp.exp(v - top) for v in r]
        inv = 1.0 / ((ex[0] + ex[1]) + (ex[2] + ex[3]))
        gates.append([v * inv for v in ex])
    back_mixed, back_logit = [], []
    for t in range(TASKS):
        z = slice(TH * t, TH * t + TH)
        o = slice(OUT * t, OUT * t + OUT)
        g = gates[t]
        ms = split(g[0] * eouts[0] + g[1] * eouts[1] + g[2] * eouts[2] + g[3] * eouts[3])
        mixed[t, 0:OUT, :] = ms[0]
        mixed[t, OUT : 2 * OUT, :] = ms[1]
        w = tw_b[z, :]
        pre = dot(w, jnp.concatenate([ms[0], ms[0]], 0), NN) + dot(w[:, 0:128], ms[1], NN) + cols[z, 12:13]
        s = jax.nn.sigmoid(pre)
        th = pre * s
        sums[2] = sums[2] + jnp.sum(th * th, keepdims=True)
        wo = cols[z, 13:14]
        logit = jnp.sum(th * wo, axis=0, keepdims=True) + biases[:, 1160 + t : 1161 + t]
        back = (jax.nn.sigmoid(logit) - lab_ref[t : t + 1, :].astype(F32)) * scale
        row_sums[z, 5:6] = jnp.sum(back * th, axis=1, keepdims=True)
        row_sums[8 + t : 9 + t, 6:7] = jnp.sum(back, axis=1, keepdims=True)
        back = back * wo * (s + th * (1.0 - s))
        row_sums[z, 4:5] = jnp.sum(back, axis=1, keepdims=True)
        bs = split(back)
        bpt[t, 0:TH, :] = bs[0]
        bpt[t, TH : 2 * TH, :] = bs[1]
        w = [v[:, z] for v in tw_t]
        bm = dot(jnp.concatenate([w[0], w[1], w[0]], 1), jnp.concatenate([bs[0], bs[0], bs[1]], 0), NN)
        back_mixed.append(bm)
        bg = [jnp.sum(bm * eouts[e], axis=0, keepdims=True) for e in range(EXPERTS)]
        mean = g[0] * bg[0] + g[1] * bg[1] + g[2] * bg[2] + g[3] * bg[3]
        back_logit += [g[e] * (bg[e] - mean) for e in range(EXPERTS)]
    back_logit = jnp.concatenate(back_logit, 0)
    row_sums[0:8, 6:7] = jnp.sum(back_logit, axis=1, keepdims=True)
    bs = split(jnp.concatenate([back_logit, jnp.zeros((8, rows), F32)], 0))
    bgl[0:16] = bs[0]
    bgl[16:32] = bs[1]
    bgl[32:48] = bs[0]
    squares += sums

    def expert_back(e):
        c = 256 * e
        back = (gates[0][e] * back_mixed[0] + gates[1][e] * back_mixed[1]) * slopes[e]
        row_sums[:, e : e + 1] = jnp.sum(back, axis=1, keepdims=True)
        bs = split(back)
        bpd[0, OUT * e : OUT * e + OUT, :] = bs[0]
        bpd[1, OUT * e : OUT * e + OUT, :] = bs[1]
        w = dn_b[c : c + 256, :]
        back = dot(w, jnp.concatenate([bs[0], bs[0]], 0), NN) + dot(w[:, 0:128], bs[1], NN)
        bs = split(back * dsu[c : c + 256, :])
        bpu[0, c : c + 256, :] = bs[0]
        bpu[1, c : c + 256, :] = bs[1]

    rep_base = chunks[EXPERTS][0][0]
    used = {"sem": 0, "row": 0}

    def sems(count):
        first = used["sem"]
        used["sem"] += count
        return first

    class Piece:
        def __init__(self, place, base, size, steps, expert):
            self.place, self.base, self.size, self.expert = place, base, size, expert
            self.steps = [groups[k] for k in steps]
            self.sent = 0
            self.plan = self.stages()

        def at(self, start, size):
            return pl.ds(pl.multiple_of(start, 8), size)

        def total(self, start, size):
            if self.expert:
                return total_e.at[self.at(start, size)]
            return total_r.at[hid, self.at(start - rep_base, size)]

        def start(self, copies, rows):
            k = sems(1)
            for src, dst, peer in copies:
                remote(src, dst, s_sem.at[self.place], v_sem.at[k], peer).start()
            self.sent += rows
            return remote(r_core.at[pl.ds(0, rows)], r_core.at[pl.ds(0, rows)], s_sem.at[self.place], v_sem.at[k], core_peer)

        def stages(self):
            rng = self.at(self.base, self.size)
            yield self.start([(grads.at[1, rng], r_core.at[rng], core_peer)], self.size)
            grads[0, rng, :] += r_core[rng, :]
            start, size, held = self.base, self.size, []
            for me, others in self.steps:
                m = len(others) + 1
                held.append((start, size))
                size //= m
                row = used["row"]
                used["row"] += (m - 1) * size
                copies = []
                for j, (q, peer) in enumerate(others):
                    src, dst = self.at(start + q * size, size), self.at(row + (m - 2 - j) * size, size)
                    copies.append((grads.at[0, src], r_sum.at[dst], peer))
                yield self.start(copies, (m - 1) * size)
                start = start + me * size
                mine = self.at(start, size)
                total = grads[0, mine, :]
                for slot in range(m - 1):
                    total = total + r_sum[row + slot * size : row + slot * size + size, :]
                if len(held) < len(self.steps):
                    grads[0, mine, :] = total
                else:
                    self.total(start, size)[...] = total
            for me, others in reversed(self.steps):
                out = self.total(start, size)
                yield self.start([(out, out, peer) for _, peer in others], len(others) * size)
                start, size = held.pop()
            if not self.expert:
                out = self.total(self.base, self.size)
                yield self.start([(out, out, core_peer)], self.size)

        def advance(self):
            if self.step is not None:
                self.step.wait_recv()
            self.step = next(self.plan, None)

        step = None

        def end(self):
            rows = pl.ds(0, self.sent)
            remote(r_sum.at[rows], r_sum.at[rows], s_sem.at[self.place], v_sem.at[0], core_peer).wait_send()

    names = ("e0", "e1", "e2", "e3", "i", "t")
    pieces = {}
    for k, (name, parts) in enumerate(zip(names, chunks)):
        for j, (base, size, steps) in enumerate(parts):
            pieces[name + "abcd"[j]] = Piece(len(pieces), base, size, steps, k < EXPERTS)

    def owner(k):
        return (k + hid) % 2

    e_base = [chunks[e][0][0] for e in range(EXPERTS)]
    e_size = chunks[1][0][0] - chunks[0][0][0]
    i_base, t_base = chunks[EXPERTS][0][0], chunks[EXPERTS + 1][0][0]
    t_size = grads.shape[1] - t_base
    misc = t_base + MISC_AT
    grads[:, misc : t_base + t_size, :] = jnp.zeros((2, t_size - MISC_AT, 128), F32)

    def update(k, at, g):
        w_ref, m_ref, a_ref, r_ref = params[k]
        new_m = MOMENTUM_RATE * m_ref[at] + g
        new_w = w_ref[at] - LEARN_RATE * (g + MOMENTUM_RATE * new_m)
        w_ref[at] = new_w
        m_ref[at] = new_m
        a_ref[at] = AVERAGE_RATE * a_ref[at] + (1.0 - AVERAGE_RATE) * new_w
        r_ref[at] = new_w.astype(BF)

    everything = slice(None)
    to = t_base - rep_base

    def update_expert(e):
        update(2, (e,), total_e[e_base[e] : e_base[e] + D, :])
        update(3, (e,), total_e[e_base[e] + D : e_base[e] + E_ROWS, :])

    def update_inputs():
        for k in range(4):
            at = 432 * (k % 2)
            update(1, (everything, slice(128 * k, 128 * k + 128)), total_r[k // 2, at : at + IN_ROWS, :])

    def update_tables(first, last):
        for f in range(first, last):
            for k in range(2):
                g = total_r[k, to + EMB * f : to + EMB * f + EMB, :]
                update(0, (f, everything, slice(128 * k, 128 * k + 128)), g)

    def update_rest():
        update(4, (everything,), total_r[hid, to + UPB_AT : to + UPB_AT + 4, :])
        for k in range(4):
            at = to + GATE_AT + 8 * (k % 2)
            for s in range(TASKS):
                g = total_r[k // 2, at + 4 * s : at + 4 * s + 4, :]
                update(5, (s, everything, slice(128 * k, 128 * k + 128)), g)
        for s in range(TASKS):
            update(6, (s,), total_r[s, to + TOWER_AT : to + TOWER_AT + TH, :])
        at = to + MISC_AT
        g = total_r[0, at + 5 : at + 6, :]
        for s in range(TASKS):
            update(7, (slice(s, s + 1), everything), g[:, TH * s : TH * s + TH])
        for k in range(4):
            r = 432 * (k % 2) + IN_ROWS
            brow[0:1, 128 * k : 128 * k + 128] = total_r[k // 2, r : r + 1, :]
            brow[0:1, D + 128 * k : D + 128 * k + 128] = total_r[0, at + k : at + k + 1, :]
        brow[0:1, 1024:1032] = total_r[0, at + 6 : at + 7, 0:8]
        brow[0:1, 1032:1160] = total_r[0, at + 4 : at + 5, :]
        brow[0:1, 1160:1162] = total_r[0, at + 6 : at + 7, 8:10]
        update(8, (everything,), brow[0, 0:NB])
        lane = lax.broadcasted_iota(jnp.int32, (1, 128), 1)
        inverse = jnp.zeros((1, 128), F32)
        for k, count in enumerate(counts):
            inverse = jnp.where(lane == k, 1.0 / count, inverse)
        brow[1:2, 0:128] = jnp.sqrt(total_r[0, at + 7 : at + 8, :] * inverse + 1e-06)
        rms_ref[...] = brow[1, 0:4]

    updates = {f"u{e}": functools.partial(update_expert, e) for e in range(EXPERTS)}
    table_split = FIELDS if len(chunks[5]) == 1 else min(FIELDS, sum(part[1] for part in chunks[5][:-1]) // EMB)
    updates["ui"] = update_inputs
    updates["ut"] = functools.partial(update_tables, 0, table_split)
    updates["ur"] = lambda: (update_tables(table_split, FIELDS), update_rest())

    done = set()

    def run(*steps):
        for name in steps:
            if name in updates:
                if not done:
                    for load in loads[13:]:
                        load.wait()
                done.add(name)
                updates[name]()
            elif name in pieces:
                pieces[name].advance()

    def first_gradients(e):
        c, base = 256 * e, e_base[e]
        g = mm((x[0], x[1]), (bpu[0, c : c + 256, :], bpu[1, c : c + 256, :]), NT)
        grads[0, base : base + D, :] = g[0:D, 0:128]
        grads[1, base : base + D, :] = g[0:D, 128:256]
        upb = t_base + UPB_AT + e
        grads[0, upb : upb + 1, :] = g[D : D + 1, 0:128]
        grads[1, upb : upb + 1, :] = g[D : D + 1, 128:256]

    def second_gradients(e):
        c, o, base = 256 * e, 128 * e, e_base[e]
        hi, lo = bpd[0, o : o + 128, :], bpd[1, o : o + 128, :]
        g = dot(h[0, c : c + 256, :], jnp.concatenate([hi, lo], 0), NT)
        g = (g[:, 0:128] + g[:, 128:256]) + dot(h[1, c : c + 256, :], hi, NT)
        grads[0, base + D : base + E_ROWS, :] = g[0:128]
        grads[1, base + D : base + E_ROWS, :] = g[128:256]
        if e_size > E_ROWS:
            grads[:, base + E_ROWS : base + e_size, :] = jnp.zeros((2, e_size - E_ROWS, 128), F32)

    def inputs_back(k):
        parts = []
        for at in blocks(D):
            b = mm((up_b[0, at, :], up_b[1, at, :]), (bpu[0], bpu[1])) + dot(gate_t[at, :], bgl[...], NN)
            parts.append(split(b))
            bi[0, at, :] = parts[-1][0]
            bi[1, at, :] = parts[-1][1]
        bs = [jnp.concatenate([p[k] for p in parts], 0) for k in range(2)]
        for at in blocks(POOLED):
            ps = split(mm((w_in_b[0, at, :], w_in_b[1, at, :]), bs))
            bp[0, at, :] = ps[0]
            bp[1, at, :] = ps[1]

    def input_gradients(k):
        g = mm((feat[0], feat[1]), (bi[0, 256 * k : 256 * k + 256, :], bi[1, 256 * k : 256 * k + 256, :]), NT)
        grads[owner(k), i_base : i_base + 432, :] = g[:, 0:128]
        grads[owner(k), i_base + 432 : i_base + I_ROWS, :] = g[:, 128:256]
        if t_base - i_base > I_ROWS:
            grads[:, i_base + I_ROWS : t_base, :] = jnp.zeros((2, t_base - i_base - I_ROWS, 128), F32)

    def small_gradients():
        g = dot(x[0], bgl[0:32], NT)
        g = g[0:D, 0:8] + g[0:D, 16:24] + dot(x[1], bgl[0:16], NT)[0:D, 0:8]
        for k in range(4):
            tile = jnp.concatenate([g[128 * k : 128 * k + 128], jnp.zeros((128, 120), F32)], 1).T
            at = t_base + GATE_AT + 8 * (k % 2)
            grads[owner(k // 2), at : at + 8, :] = tile[0:8]
        for t in range(TASKS):
            g = dot(bpt[t], mixed[t], NT)
            g = (g[0:TH, 0:OUT] + g[0:TH, OUT : 2 * OUT]) + g[TH : 2 * TH, 0:OUT]
            grads[owner(t), t_base + TOWER_AT : t_base + TOWER_AT + TH, :] = g
        lane = lax.broadcasted_iota(jnp.int32, (1, 128), 1)
        m = owner(0)
        grads[m, misc : misc + 8, :] = row_sums[...].T[0:8]
        total = jnp.zeros((1, 128), F32)
        for k in range(4):
            total = jnp.where(lane == k, squares[k], total)
        grads[m, misc + 7 : misc + 8, :] = total

    def tables(first, last):
        for f in range(2 * first, 2 * last):
            at = slice(EMB * f, EMB * f + EMB)
            total = jnp.zeros((2 * EMB, VOCAB), F32)
            for j in range(rows // width):
                here = slice(width * j, width * (j + 1))
                back = jnp.concatenate([bp[0, at, here], bp[1, at, here]], 0)
                total = total + dot(back, bag_counts(part, f, here, width), NT)
            g = (total[0:EMB] + total[EMB : 2 * EMB]) * sixteen
            at = slice(t_base + EMB * f, t_base + EMB * f + EMB)
            grads[owner(0), at, :] = g[:, 0:128]
            grads[owner(1), at, :] = g[:, 128:256]

    work = {
        "b": expert_back,
        "G": first_gradients,
        "D": second_gradients,
        "h": inputs_back,
        "i": input_gradients,
        "s": lambda k: small_gradients(),
    }
    for item in SCHEDULE:
        if item[0:2] == "!j":
            tables(*[int(v) for v in item[2:].split("-")])
        elif item[0] == "!":
            work[item[1]](int(item[2]))
        else:
            run(*item.split())
    while any(piece.step for piece in pieces.values()):
        run(*[name for name in pieces if pieces[name].step])
    run(*[name for name in updates if name not in done])
    for copy in weights:
        copy.wait_send()
    for piece in pieces.values():
        piece.end()


def layout(n):
    unit = 8 * n
    chunks, base = [], 0
    for size, parts in zip([E_ROWS] * EXPERTS + [I_ROWS, T_ROWS], PARTS):
        left = -(-size // unit) * unit
        pieces = []
        for j, (rows, steps) in enumerate(parts):
            take = left if j == len(parts) - 1 else min(left, -(-rows // unit) * unit)
            if take:
                pieces.append((base, take, steps))
            base += take
            left -= take
        chunks.append(pieces)
    return chunks, base


def step(args, shapes, n, total_rows):
    rows = args[0].shape[2] // 2
    chunks, size = layout(n)
    e_all = chunks[EXPERTS][0][0]
    count, places = 0, sum(len(parts) for parts in chunks)
    for parts in chunks:
        for _, _, steps in parts:
            count += 2 + 2 * len(steps)
    vm = pltpu.VMEM
    scratch = [
        vm((FIELDS, 4, rows), jnp.int32),
        vm((FIELDS, rows), jnp.int32),
        vm((13, rows), F32),
        vm((TASKS, rows), jnp.int32),
        vm((EXPERTS, D, 128), F32),
        vm((EXPERTS, 128, OUT), F32),
        vm((EXPERTS, 128), F32),
        vm((8, 1280), F32),
        vm((2, FIELDS, 4, rows), F32),
        vm((512, D), F32),
        vm((2, D, 512), BF),
        vm((2, POOLED, D), BF),
        vm((2, D, EXPERTS * HID), BF),
        vm((2, EXPERTS * HID + 16, D), BF),
        vm((EXPERTS * HID, 2 * OUT), BF),
        vm((2, EXPERTS, OUT, HID), BF),
        vm((TASKS * TH, 2 * OUT), BF),
        vm((D, 48), BF),
        vm((128, 128), F32),
        vm((128, 128), F32),
        vm((2, 432, rows), BF),
        vm((2, D + 16, rows), BF),
        vm((2, EXPERTS * HID, rows), BF),
        vm((2, EXPERTS * OUT, rows), BF),
        vm((2, EXPERTS * HID, rows), BF),
        vm((EXPERTS * HID, rows), F32),
        vm((TASKS, 2 * OUT, rows), BF),
        vm((TASKS, 2 * TH, rows), BF),
        vm((48, rows), BF),
        vm((128, 128), F32),
        vm((2, D, rows), BF),
        vm((2, POOLED, rows), BF),
        vm((2, size, 128), F32),
        vm((e_all, 128), F32),
        vm((2, size - e_all, 128), F32),
        vm((size, 128), F32),
        vm((size, 128), F32),
        pltpu.SemaphoreType.DMA((31,)),
        pltpu.SemaphoreType.DMA((3,)),
        pltpu.SemaphoreType.DMA((3,)),
        pltpu.SemaphoreType.DMA((places,)),
        pltpu.SemaphoreType.DMA((count,)),
    ]
    counts = [float(total_rows * c) for c in (D, EXPERTS * HID, EXPERTS * OUT, TASKS * TH)]
    return pl.pallas_call(
        functools.partial(step_kernel, n, chunks, total_rows, counts),
        out_shape=[pltpu.VMEM(shape, dtype) for shape, dtype in shapes],
        in_specs=[pl.BlockSpec(memory_space=pl.ANY)] * len(args),
        out_specs=[pl.BlockSpec(memory_space=pltpu.VMEM)] * len(shapes),
        scratch_shapes=scratch,
        compiler_params=pltpu.CompilerParams(collective_id=0, has_side_effects=True, vmem_limit_bytes=50 << 20),
        name="step",
    )(*args)


def write_kernel(*refs):
    sems = refs[-1]
    k = (len(refs) - 1) // 2
    copies = [pltpu.make_async_copy(refs[i], refs[k + i], sems.at[i]) for i in range(k)]
    for copy in copies:
        copy.start()
    for copy in copies:
        copy.wait()


def local(*args):
    n = lax.axis_size("dp")
    ids, lengths, dense, labels = args[:4]
    total_rows = ids.shape[0] * n
    params = [list(args[4 + 3 * k : 7 + 3 * k]) for k in range(9)]
    for k in (0, 5, 6):
        params[k] = [v.transpose(0, 2, 1) for v in params[k]]
    shapes = []
    for p in params:
        shapes += [(p[0].shape, F32)] * 3 + [(p[0].shape, BF)]
    shapes.append(((4,), F32))
    flat = [ids.transpose(1, 2, 0), lengths.T, dense.T, labels.T] + [v for p in params for v in p]
    results = step(flat, shapes, n, total_rows)
    results = [pltpu.with_memory_space_constraint(v, pltpu.VMEM) for v in results]
    outs = pl.pallas_call(
        write_kernel,
        out_shape=[jax.ShapeDtypeStruct(shape, dtype) for shape, dtype in shapes],
        in_specs=[pl.BlockSpec(memory_space=pltpu.VMEM)] * len(shapes),
        out_specs=[pl.BlockSpec(memory_space=pl.ANY)] * len(shapes),
        scratch_shapes=[pltpu.SemaphoreType.DMA((len(shapes),))],
        compiler_params=pltpu.CompilerParams(vmem_limit_bytes=1 << 20),
        name="write",
    )(*results)
    outs = list(outs)
    for k in (0, 5, 6):
        outs[4 * k : 4 * k + 4] = [v.transpose(0, 2, 1) for v in outs[4 * k : 4 * k + 4]]
    return tuple(outs)


def solution(mesh):
    up, down, bias = P(None, None, "hid"), P(None, "hid", None), P(None, "hid")
    rep = P()
    return jax.shard_map(
        local,
        mesh=mesh,
        in_specs=(P("dp", None, None), P("dp", None), P("dp", None), P("dp", None))
        + (rep,) * 6
        + (up,) * 3
        + (down,) * 3
        + (bias,) * 3
        + (rep,) * 12,
        out_specs=(rep,) * 8 + (up,) * 4 + (down,) * 4 + (bias,) * 4 + (rep,) * 17,
        check_vma=False,
    )
```

```python
import functools
import math

import jax
import jax.numpy as jnp
from jax import lax
from jax.experimental import pallas as pl
from jax.experimental.pallas import tpu as pltpu
from jax.sharding import PartitionSpec as P

D = 512
HID = 256
OUT = 128
TH = 64
TASKS = 2
EXPERTS = 4
FIELDS = 26
VOCAB = 256
EMB = 16
POOLED = 416
IN_ROWS = 429
NB = 1162

MOMENTUM_RATE = 0.9
LEARN_RATE = 0.3
AVERAGE_RATE = 0.9

BF = jnp.bfloat16
F32 = jnp.float32
NN = (((1,), (0,)), ((), ()))
NT = (((1,), (1,)), ((), ()))
MESH = pl.DeviceIdType.MESH

E_ROWS = 640
I_BASE = EXPERTS * E_ROWS
I_ROWS = 864
GATE_AT = 416
TOWER_AT = 432
MISC_AT = 496
UPB_AT = 504
T_ROWS = 512


PARTS = (
    ((640, "zyx"),),
    ((640, "pz"),),
    ((640, "pz"),),
    ((640, "pz"),),
    ((256, "zp"), (640, "pz"),),
    ((256, "pz"), (256, "pz"),),
)
SCHEDULE = (
    "!b1",
    "!b0",
    "!b2",
    "!D2",
    "!D0",
    "!D1",
    "!G1",
    "e1a",
    "!G0",
    "e0a",
    "!G2",
    "e1a e2a",
    "!b3",
    "e0a",
    "!G3",
    "!D3",
    "e3a e2a",
    "!h0",
    "e1a e3a",
    "!i0",
    "!i1",
    "ib e2a ia",
    "!s0",
    "ib ia",
    "!j0-8",
    "e1a ta e0a e3a",
    "!j8-10",
    "ta",
    "!j10-13",
    "tb e2a ia ib",
    "tb e0a e1a ta",
    "e3a ia e0a tb",
    "e2a ib ta e1a",
    "e0a ia e3a u1",
    "tb ib e0a e2a",
    "u2 ta ia tb",
    "e3a u3 ia ib",
    "ta ib ui ta",
    "tb ut e0a u0",
    "tb ur",
)


def split(v):
    hi = v.astype(BF)
    return hi, (v - hi.astype(F32)).astype(BF)


def dot(a, b, dims):
    return lax.dot_general(a, b, dims, preferred_element_type=F32)


def blocks(size, step=128):
    return [slice(k, min(size, k + step)) for k in range(0, size, step)]


def mm(a, b, dims=NN):
    return dot(a[0], b[0], dims) + (dot(a[1], b[0], dims) + dot(a[0], b[1], dims))


def bag_counts(part_ref, f, here, width):
    row = lax.broadcasted_iota(jnp.int32, (16, width), 0).astype(F32).astype(BF)
    zero = jnp.zeros((16, width), BF)
    weights = [jnp.broadcast_to(part_ref[0, f, s : s + 1, here], (16, width)).astype(BF) for s in range(4)]
    offsets = [jnp.broadcast_to(part_ref[1, f, s : s + 1, here], (16, width)).astype(BF) - row for s in range(4)]
    low, high = [], []
    for t in range(8):
        start = jnp.full((16, width), 16 * t, BF)
        hit = [jnp.where(offsets[s] == start, weights[s], zero) for s in range(4)]
        both = (hit[0] + hit[1]) + (hit[2] + hit[3])
        whole = (both + 128.0) - 128.0
        low.append(both - whole)
        high.append(whole)
    return jnp.concatenate(low + high, 0)


def step_kernel(n, chunks, total_rows, counts, *refs):
    hbm, refs = refs[:31], refs[31:]
    outs, refs = refs[:37], refs[37:]
    ids_hbm, len_hbm, dense_hbm, lab_hbm = hbm[:4]
    up_hbm, dn_hbm, upb_hbm = hbm[10], hbm[13], hbm[16]
    params = [outs[4 * k : 4 * k + 4] for k in range(9)]
    rms_ref = outs[36]
    tab_ref, w_raw, upo_ref, dno_ref, upbo_ref, gate_ref, tw_ref, tout_ref, bias_ref = [p[0] for p in params]
    (
        ids_ref,
        len_ref,
        dense_ref,
        lab_ref,
        upx_ref,
        dnx_ref,
        upbx_ref,
        brow,
        part,
        w_in,
        w_in_t,
        w_in_b,
        up_b,
        up_t,
        dn_b,
        dn_t,
        tw_b,
        gate_t,
        cols,
        bcol,
        feat,
        x,
        h,
        bpd,
        bpu,
        dsu,
        mixed,
        bpt,
        bgl,
        row_sums,
        bi,
        bp,
        grads,
        total_e,
        total_r,
        r_core,
        r_sum,
        in_sem,
        w_send,
        w_recv,
        s_sem,
        v_sem,
    ) = refs
    dp = lax.axis_index("dp")
    hid = lax.axis_index("hid")
    core_peer = (dp, 1 - hid)

    def group(stride, size):
        me = dp // stride % size
        others = [(me + k) % size for k in range(1, size)]
        return me, [(q, (dp + (q - me) * stride, hid)) for q in others]

    groups = {"x": group(1, 2), "y": group(2, 2), "z": group(4, n // 4), "p": group(1, 4), "a": group(1, n)}

    barrier = pltpu.get_barrier_semaphore()
    kinds = {k for parts in chunks for _, _, steps in parts for k in steps}
    kinds = ["a"] if "a" in kinds else ["p", "z"]
    everyone = [core_peer] + [peer for k in kinds for _, peer in groups[k][1]]
    for peer in everyone:
        pl.semaphore_signal(barrier, inc=1, device_id=peer, device_id_type=MESH)

    rows = ids_ref.shape[2]
    lanes = pl.ds(pl.multiple_of(hid * rows, rows), rows)
    order = (0, 1, 2, 3, 4, 5, 6, 7, 8)
    pairs = [(ids_hbm.at[:, :, lanes], ids_ref), (len_hbm.at[:, lanes], len_ref)]
    pairs += [(hbm[4 + 3 * k], params[k][0]) for k in order]
    pairs += [(dense_hbm.at[:, lanes], dense_ref), (lab_hbm.at[:, lanes], lab_ref)]
    for j in (1, 2):
        pairs += [(hbm[4 + 3 * k + j], params[k][j]) for k in order]
    loads = [pltpu.make_async_copy(src, dst, in_sem.at[k]) for k, (src, dst) in enumerate(pairs)]
    for load in loads[:13]:
        load.start()

    def remote(src, dst, send, recv, peer):
        return pltpu.make_async_remote_copy(
            src_ref=src, dst_ref=dst, send_sem=send, recv_sem=recv, device_id=peer, device_id_type=MESH
        )

    pl.semaphore_wait(barrier, len(everyone))
    weights = [
        remote(src, dst, w_send.at[k], w_recv.at[k], core_peer)
        for k, (src, dst) in enumerate(((up_hbm, upx_ref), (dn_hbm, dnx_ref), (upb_hbm, upbx_ref)))
    ]
    for copy in weights:
        copy.start()

    loads[0].wait()
    loads[1].wait()
    slot = lax.broadcasted_iota(jnp.int32, (4, rows), 0)
    for f in range(FIELDS):
        used = jnp.broadcast_to(len_ref[f : f + 1, :], (4, rows)) > slot
        ident = ids_ref[f]
        part[0, f] = jnp.where(used, jnp.where(ident < 128, 0.0625, 1.0), 0.0)
        part[1, f] = jnp.bitwise_and(ident, 127).astype(F32)
    for load in loads[2:13]:
        load.wait()

    sixteen = jnp.where(lax.broadcasted_iota(jnp.int32, (EMB, VOCAB), 1) < 128, 16.0, 1.0)
    width = 256

    for f in range(FIELDS):
        table = jnp.concatenate(split(tab_ref[f] * sixteen), 0)
        at = slice(EMB * f, EMB * f + EMB)
        for j in range(rows // width):
            here = slice(width * j, width * (j + 1))
            both = dot(table, bag_counts(part, f, here, width), NN)
            hi, lo = split(both[0:EMB] + both[EMB : 2 * EMB])
            feat[0, at, here] = hi
            feat[1, at, here] = lo
    for load in loads[13:]:
        load.start()

    brow[0:1, 0:1024] = bias_ref[0:1024].reshape(1, 1024)
    brow[0:1, 1024:NB] = bias_ref[1024:NB].reshape(1, NB - 1024)
    biases = brow[0:1, 0:NB]
    row = lax.broadcasted_iota(jnp.int32, (8, D), 0)
    in_bias = jnp.broadcast_to(biases[:, 0:D], (8, D))
    w_in[0:IN_ROWS, :] = w_raw[...]
    w_in[424:432, :] = jnp.where(row == 5, in_bias, jnp.where(row < 5, w_in[424:432, :], 0.0))
    w_in[432:512, :] = jnp.zeros((80, D), F32)
    for i in range(4):
        hi, lo = split(w_in[128 * i : 128 * (i + 1), :].T)
        w_in_t[0, :, 128 * i : 128 * (i + 1)] = hi
        w_in_t[1, :, 128 * i : 128 * (i + 1)] = lo
    hi, lo = split(w_in[0:POOLED, :])
    w_in_b[0] = hi
    w_in_b[1] = lo

    def expert_weights(k, up_ref, dn_ref):
        for e in range(EXPERTS):
            c = 256 * e + 128 * k
            up, down = up_ref[e], dn_ref[e]
            hi, lo = split(up)
            up_b[0, :, c : c + 128] = hi
            up_b[1, :, c : c + 128] = lo
            hi, lo = split(up.T)
            up_t[0, c : c + 128, :] = hi
            up_t[1, c : c + 128, :] = lo
            hi, lo = split(down)
            dn_b[c : c + 128, 0:128] = hi
            dn_b[c : c + 128, 128:256] = lo
            hi, lo = split(down.T)
            dn_t[0, e, :, 128 * k : 128 * k + 128] = hi
            dn_t[1, e, :, 128 * k : 128 * k + 128] = lo

    expert_weights(0, upo_ref, dno_ref)
    gate8 = jnp.concatenate([gate_ref[0], gate_ref[1]], 0)
    hi, lo = split(jnp.concatenate([gate8, jnp.zeros((8, D), F32)], 0))
    up_t[0, 1024:1040, :] = hi
    up_t[1, 1024:1040, :] = lo
    for i in range(4):
        tile = jnp.concatenate([gate8[:, 128 * i : 128 * (i + 1)], jnp.zeros((120, 128), F32)], 0).T
        hi, lo = split(tile)
        at = slice(128 * i, 128 * (i + 1))
        gate_t[at, 0:16] = hi[:, 0:16]
        gate_t[at, 16:32] = hi[:, 0:16]
        gate_t[at, 32:48] = lo[:, 0:16]
    for t in range(TASKS):
        hi, lo = split(tw_ref[t])
        tw_b[TH * t : TH * t + TH, 0:128] = hi
        tw_b[TH * t : TH * t + TH, 128:256] = lo
    tw_t = split(jnp.concatenate([tw_ref[0], tw_ref[1]], 0).T)
    x[0, D : D + 16, :] = jnp.ones((16, rows), BF)
    x[1, D : D + 16, :] = jnp.zeros((16, rows), BF)
    hi, lo = split(jnp.concatenate([dense_ref[...], jnp.ones((1, rows), F32), jnp.zeros((2, rows), F32)], 0))
    feat[0, POOLED:432, :] = hi
    feat[1, POOLED:432, :] = lo

    scale = float(total_rows) ** -0.5
    fs = (feat[0], feat[1])
    xv = mm((w_in_t[0, :, 0:432], w_in_t[1, :, 0:432]), fs)
    squares = [jnp.sum(xv * xv, keepdims=True)]
    xs = split(xv)
    x[0, 0:D, :] = xs[0]
    x[1, 0:D, :] = xs[1]
    for copy in weights:
        copy.wait_recv()
    expert_weights(1, upx_ref, dnx_ref)
    bcol[...] = jnp.zeros((128, 128), F32)
    bcol[0:4, :] = upbo_ref[...]
    bcol[4:8, :] = upbx_ref[...]
    for e in range(EXPERTS):
        bcol[8 + e : 9 + e, :] = biases[:, 512 + 128 * e : 640 + 128 * e]
    bcol[12:13, :] = biases[:, 1032:1160]
    bcol[13:14, 0:64] = tout_ref[0:1, :]
    bcol[13:14, 64:128] = tout_ref[1:2, :]
    bcol[14:15, 0:8] = biases[:, 1024:1032]
    cols[...] = bcol[...].T
    row_sums[...] = jnp.zeros((128, 128), F32)

    eouts, slopes = [], []
    sums = [0.0, 0.0, 0.0]
    for e in range(EXPERTS):
        c = 256 * e
        end = c + 256 if e < EXPERTS - 1 else c + 272
        pre = mm((up_t[0, c:end, :], up_t[1, c:end, :]), xs)
        gate_logits = pre[256:264] + cols[0:8, 14:15] if e == EXPERTS - 1 else None
        pre = pre[0:256] + jnp.concatenate([cols[:, e : e + 1], cols[:, 4 + e : 5 + e]], 0)
        s = jax.nn.sigmoid(pre)
        hv = pre * s
        dsu[c : c + 256, :] = s + hv * (1.0 - s)
        sums[0] = sums[0] + jnp.sum(hv * hv, keepdims=True)
        hs = split(hv)
        h[0, c : c + 256, :] = hs[0]
        h[1, c : c + 256, :] = hs[1]
        pre = mm((dn_t[0, e], dn_t[1, e]), hs) + cols[:, 8 + e : 9 + e]
        s = jax.nn.sigmoid(pre)
        out = pre * s
        sums[1] = sums[1] + jnp.sum(out * out, keepdims=True)
        eouts.append(out)
        slopes.append(s + out * (1.0 - s))
    gates = []
    for t in range(TASKS):
        r = [gate_logits[4 * t + e : 4 * t + e + 1] for e in range(EXPERTS)]
        top = jnp.maximum(jnp.maximum(r[0], r[1]), jnp.maximum(r[2], r[3]))
        ex = [jnp.exp(v - top) for v in r]
        inv = 1.0 / ((ex[0] + ex[1]) + (ex[2] + ex[3]))
        gates.append([v * inv for v in ex])
    back_mixed, back_logit = [], []
    for t in range(TASKS):
        z = slice(TH * t, TH * t + TH)
        o = slice(OUT * t, OUT * t + OUT)
        g = gates[t]
        ms = split(g[0] * eouts[0] + g[1] * eouts[1] + g[2] * eouts[2] + g[3] * eouts[3])
        mixed[t, 0:OUT, :] = ms[0]
        mixed[t, OUT : 2 * OUT, :] = ms[1]
        w = tw_b[z, :]
        pre = dot(w, jnp.concatenate([ms[0], ms[0]], 0), NN) + dot(w[:, 0:128], ms[1], NN) + cols[z, 12:13]
        s = jax.nn.sigmoid(pre)
        th = pre * s
        sums[2] = sums[2] + jnp.sum(th * th, keepdims=True)
        wo = cols[z, 13:14]
        logit = jnp.sum(th * wo, axis=0, keepdims=True) + biases[:, 1160 + t : 1161 + t]
        back = (jax.nn.sigmoid(logit) - lab_ref[t : t + 1, :].astype(F32)) * scale
        row_sums[z, 5:6] = jnp.sum(back * th, axis=1, keepdims=True)
        row_sums[8 + t : 9 + t, 6:7] = jnp.sum(back, axis=1, keepdims=True)
        back = back * wo * (s + th * (1.0 - s))
        row_sums[z, 4:5] = jnp.sum(back, axis=1, keepdims=True)
        bs = split(back)
        bpt[t, 0:TH, :] = bs[0]
        bpt[t, TH : 2 * TH, :] = bs[1]
        w = [v[:, z] for v in tw_t]
        bm = dot(jnp.concatenate([w[0], w[1], w[0]], 1), jnp.concatenate([bs[0], bs[0], bs[1]], 0), NN)
        back_mixed.append(bm)
        bg = [jnp.sum(bm * eouts[e], axis=0, keepdims=True) for e in range(EXPERTS)]
        mean = g[0] * bg[0] + g[1] * bg[1] + g[2] * bg[2] + g[3] * bg[3]
        back_logit += [g[e] * (bg[e] - mean) for e in range(EXPERTS)]
    back_logit = jnp.concatenate(back_logit, 0)
    row_sums[0:8, 6:7] = jnp.sum(back_logit, axis=1, keepdims=True)
    bs = split(jnp.concatenate([back_logit, jnp.zeros((8, rows), F32)], 0))
    bgl[0:16] = bs[0]
    bgl[16:32] = bs[1]
    bgl[32:48] = bs[0]
    squares += sums

    def expert_back(e):
        c = 256 * e
        back = (gates[0][e] * back_mixed[0] + gates[1][e] * back_mixed[1]) * slopes[e]
        row_sums[:, e : e + 1] = jnp.sum(back, axis=1, keepdims=True)
        bs = split(back)
        bpd[0, OUT * e : OUT * e + OUT, :] = bs[0]
        bpd[1, OUT * e : OUT * e + OUT, :] = bs[1]
        w = dn_b[c : c + 256, :]
        back = dot(w, jnp.concatenate([bs[0], bs[0]], 0), NN) + dot(w[:, 0:128], bs[1], NN)
        bs = split(back * dsu[c : c + 256, :])
        bpu[0, c : c + 256, :] = bs[0]
        bpu[1, c : c + 256, :] = bs[1]

    rep_base = chunks[EXPERTS][0][0]
    used = {"sem": 0, "row": 0}

    def sems(count):
        first = used["sem"]
        used["sem"] += count
        return first

    class Piece:
        def __init__(self, place, base, size, steps, expert):
            self.place, self.base, self.size, self.expert = place, base, size, expert
            self.steps = [groups[k] for k in steps]
            self.sent = 0
            self.plan = self.stages()

        def at(self, start, size):
            return pl.ds(pl.multiple_of(start, 8), size)

        def total(self, start, size):
            if self.expert:
                return total_e.at[self.at(start, size)]
            return total_r.at[hid, self.at(start - rep_base, size)]

        def start(self, copies, rows):
            k = sems(1)
            for src, dst, peer in copies:
                remote(src, dst, s_sem.at[self.place], v_sem.at[k], peer).start()
            self.sent += rows
            return remote(r_core.at[pl.ds(0, rows)], r_core.at[pl.ds(0, rows)], s_sem.at[self.place], v_sem.at[k], core_peer)

        def stages(self):
            rng = self.at(self.base, self.size)
            yield self.start([(grads.at[1, rng], r_core.at[rng], core_peer)], self.size)
            grads[0, rng, :] += r_core[rng, :]
            start, size, held = self.base, self.size, []
            for me, others in self.steps:
                m = len(others) + 1
                held.append((start, size))
                size //= m
                row = used["row"]
                used["row"] += (m - 1) * size
                copies = []
                for j, (q, peer) in enumerate(others):
                    src, dst = self.at(start + q * size, size), self.at(row + (m - 2 - j) * size, size)
                    copies.append((grads.at[0, src], r_sum.at[dst], peer))
                yield self.start(copies, (m - 1) * size)
                start = start + me * size
                mine = self.at(start, size)
                total = grads[0, mine, :]
                for slot in range(m - 1):
                    total = total + r_sum[row + slot * size : row + slot * size + size, :]
                if len(held) < len(self.steps):
                    grads[0, mine, :] = total
                else:
                    self.total(start, size)[...] = total
            for me, others in reversed(self.steps):
                out = self.total(start, size)
                yield self.start([(out, out, peer) for _, peer in others], len(others) * size)
                start, size = held.pop()
            if not self.expert:
                out = self.total(self.base, self.size)
                yield self.start([(out, out, core_peer)], self.size)

        def advance(self):
            if self.step is not None:
                self.step.wait_recv()
            self.step = next(self.plan, None)

        step = None

        def end(self):
            rows = pl.ds(0, self.sent)
            remote(r_sum.at[rows], r_sum.at[rows], s_sem.at[self.place], v_sem.at[0], core_peer).wait_send()

    names = ("e0", "e1", "e2", "e3", "i", "t")
    pieces = {}
    for k, (name, parts) in enumerate(zip(names, chunks)):
        for j, (base, size, steps) in enumerate(parts):
            pieces[name + "abcd"[j]] = Piece(len(pieces), base, size, steps, k < EXPERTS)

    def owner(k):
        return (k + hid) % 2

    e_base = [chunks[e][0][0] for e in range(EXPERTS)]
    e_size = chunks[1][0][0] - chunks[0][0][0]
    i_base, t_base = chunks[EXPERTS][0][0], chunks[EXPERTS + 1][0][0]
    t_size = grads.shape[1] - t_base
    misc = t_base + MISC_AT
    grads[:, misc : t_base + t_size, :] = jnp.zeros((2, t_size - MISC_AT, 128), F32)

    def update(k, at, g):
        w_ref, m_ref, a_ref, r_ref = params[k]
        new_m = MOMENTUM_RATE * m_ref[at] + g
        new_w = w_ref[at] - LEARN_RATE * (g + MOMENTUM_RATE * new_m)
        w_ref[at] = new_w
        m_ref[at] = new_m
        a_ref[at] = AVERAGE_RATE * a_ref[at] + (1.0 - AVERAGE_RATE) * new_w
        r_ref[at] = new_w.astype(BF)

    everything = slice(None)
    to = t_base - rep_base

    def update_expert(e):
        update(2, (e,), total_e[e_base[e] : e_base[e] + D, :])
        update(3, (e,), total_e[e_base[e] + D : e_base[e] + E_ROWS, :])

    def update_inputs():
        for k in range(4):
            at = 432 * (k % 2)
            update(1, (everything, slice(128 * k, 128 * k + 128)), total_r[k // 2, at : at + IN_ROWS, :])

    def update_tables(first, last):
        for f in range(first, last):
            for k in range(2):
                g = total_r[k, to + EMB * f : to + EMB * f + EMB, :]
                update(0, (f, everything, slice(128 * k, 128 * k + 128)), g)

    def update_rest():
        update(4, (everything,), total_r[hid, to + UPB_AT : to + UPB_AT + 4, :])
        for k in range(4):
            at = to + GATE_AT + 8 * (k % 2)
            for s in range(TASKS):
                g = total_r[k // 2, at + 4 * s : at + 4 * s + 4, :]
                update(5, (s, everything, slice(128 * k, 128 * k + 128)), g)
        for s in range(TASKS):
            update(6, (s,), total_r[s, to + TOWER_AT : to + TOWER_AT + TH, :])
        at = to + MISC_AT
        g = total_r[0, at + 5 : at + 6, :]
        for s in range(TASKS):
            update(7, (slice(s, s + 1), everything), g[:, TH * s : TH * s + TH])
        for k in range(4):
            r = 432 * (k % 2) + IN_ROWS
            brow[0:1, 128 * k : 128 * k + 128] = total_r[k // 2, r : r + 1, :]
            brow[0:1, D + 128 * k : D + 128 * k + 128] = total_r[0, at + k : at + k + 1, :]
        brow[0:1, 1024:1032] = total_r[0, at + 6 : at + 7, 0:8]
        brow[0:1, 1032:1160] = total_r[0, at + 4 : at + 5, :]
        brow[0:1, 1160:1162] = total_r[0, at + 6 : at + 7, 8:10]
        update(8, (everything,), brow[0, 0:NB])
        lane = lax.broadcasted_iota(jnp.int32, (1, 128), 1)
        inverse = jnp.zeros((1, 128), F32)
        for k, count in enumerate(counts):
            inverse = jnp.where(lane == k, 1.0 / count, inverse)
        brow[1:2, 0:128] = jnp.sqrt(total_r[0, at + 7 : at + 8, :] * inverse + 1e-06)
        rms_ref[...] = brow[1, 0:4]

    updates = {f"u{e}": functools.partial(update_expert, e) for e in range(EXPERTS)}
    table_split = FIELDS if len(chunks[5]) == 1 else min(FIELDS, sum(part[1] for part in chunks[5][:-1]) // EMB)
    updates["ui"] = update_inputs
    updates["ut"] = functools.partial(update_tables, 0, table_split)
    updates["ur"] = lambda: (update_tables(table_split, FIELDS), update_rest())

    done = set()

    def run(*steps):
        for name in steps:
            if name in updates:
                if not done:
                    for load in loads[13:]:
                        load.wait()
                done.add(name)
                updates[name]()
            elif name in pieces:
                pieces[name].advance()

    def first_gradients(e):
        c, base = 256 * e, e_base[e]
        g = mm((x[0], x[1]), (bpu[0, c : c + 256, :], bpu[1, c : c + 256, :]), NT)
        grads[0, base : base + D, :] = g[0:D, 0:128]
        grads[1, base : base + D, :] = g[0:D, 128:256]
        upb = t_base + UPB_AT + e
        grads[0, upb : upb + 1, :] = g[D : D + 1, 0:128]
        grads[1, upb : upb + 1, :] = g[D : D + 1, 128:256]

    def second_gradients(e):
        c, o, base = 256 * e, 128 * e, e_base[e]
        hi, lo = bpd[0, o : o + 128, :], bpd[1, o : o + 128, :]
        g = dot(h[0, c : c + 256, :], jnp.concatenate([hi, lo], 0), NT)
        g = (g[:, 0:128] + g[:, 128:256]) + dot(h[1, c : c + 256, :], hi, NT)
        grads[0, base + D : base + E_ROWS, :] = g[0:128]
        grads[1, base + D : base + E_ROWS, :] = g[128:256]
        if e_size > E_ROWS:
            grads[:, base + E_ROWS : base + e_size, :] = jnp.zeros((2, e_size - E_ROWS, 128), F32)

    def inputs_back(k):
        parts = []
        for at in blocks(D):
            b = mm((up_b[0, at, :], up_b[1, at, :]), (bpu[0], bpu[1])) + dot(gate_t[at, :], bgl[...], NN)
            parts.append(split(b))
            bi[0, at, :] = parts[-1][0]
            bi[1, at, :] = parts[-1][1]
        bs = [jnp.concatenate([p[k] for p in parts], 0) for k in range(2)]
        for at in blocks(POOLED):
            ps = split(mm((w_in_b[0, at, :], w_in_b[1, at, :]), bs))
            bp[0, at, :] = ps[0]
            bp[1, at, :] = ps[1]

    def input_gradients(k):
        g = mm((feat[0], feat[1]), (bi[0, 256 * k : 256 * k + 256, :], bi[1, 256 * k : 256 * k + 256, :]), NT)
        grads[owner(k), i_base : i_base + 432, :] = g[:, 0:128]
        grads[owner(k), i_base + 432 : i_base + I_ROWS, :] = g[:, 128:256]
        if t_base - i_base > I_ROWS:
            grads[:, i_base + I_ROWS : t_base, :] = jnp.zeros((2, t_base - i_base - I_ROWS, 128), F32)

    def small_gradients():
        g = dot(x[0], bgl[0:32], NT)
        g = g[0:D, 0:8] + g[0:D, 16:24] + dot(x[1], bgl[0:16], NT)[0:D, 0:8]
        for k in range(4):
            tile = jnp.concatenate([g[128 * k : 128 * k + 128], jnp.zeros((128, 120), F32)], 1).T
            at = t_base + GATE_AT + 8 * (k % 2)
            grads[owner(k // 2), at : at + 8, :] = tile[0:8]
        for t in range(TASKS):
            g = dot(bpt[t], mixed[t], NT)
            g = (g[0:TH, 0:OUT] + g[0:TH, OUT : 2 * OUT]) + g[TH : 2 * TH, 0:OUT]
            grads[owner(t), t_base + TOWER_AT : t_base + TOWER_AT + TH, :] = g
        lane = lax.broadcasted_iota(jnp.int32, (1, 128), 1)
        m = owner(0)
        grads[m, misc : misc + 8, :] = row_sums[...].T[0:8]
        total = jnp.zeros((1, 128), F32)
        for k in range(4):
            total = jnp.where(lane == k, squares[k], total)
        grads[m, misc + 7 : misc + 8, :] = total

    def tables(first, last):
        for f in range(2 * first, 2 * last):
            at = slice(EMB * f, EMB * f + EMB)
            total = jnp.zeros((2 * EMB, VOCAB), F32)
            for j in range(rows // width):
                here = slice(width * j, width * (j + 1))
                back = jnp.concatenate([bp[0, at, here], bp[1, at, here]], 0)
                total = total + dot(back, bag_counts(part, f, here, width), NT)
            g = (total[0:EMB] + total[EMB : 2 * EMB]) * sixteen
            at = slice(t_base + EMB * f, t_base + EMB * f + EMB)
            grads[owner(0), at, :] = g[:, 0:128]
            grads[owner(1), at, :] = g[:, 128:256]

    work = {
        "b": expert_back,
        "G": first_gradients,
        "D": second_gradients,
        "h": inputs_back,
        "i": input_gradients,
        "s": lambda k: small_gradients(),
    }
    for item in SCHEDULE:
        if item[0:2] == "!j":
            tables(*[int(v) for v in item[2:].split("-")])
        elif item[0] == "!":
            work[item[1]](int(item[2]))
        else:
            run(*item.split())
    while any(piece.step for piece in pieces.values()):
        run(*[name for name in pieces if pieces[name].step])
    run(*[name for name in updates if name not in done])
    for copy in weights:
        copy.wait_send()
    for piece in pieces.values():
        piece.end()


def layout(n):
    unit = 8 * n
    chunks, base = [], 0
    for size, parts in zip([E_ROWS] * EXPERTS + [I_ROWS, T_ROWS], PARTS):
        left = -(-size // unit) * unit
        pieces = []
        for j, (rows, steps) in enumerate(parts):
            take = left if j == len(parts) - 1 else min(left, -(-rows // unit) * unit)
            if take:
                pieces.append((base, take, steps))
            base += take
            left -= take
        chunks.append(pieces)
    return chunks, base


def step(args, shapes, n, total_rows):
    rows = args[0].shape[2] // 2
    chunks, size = layout(n)
    e_all = chunks[EXPERTS][0][0]
    count, places = 0, sum(len(parts) for parts in chunks)
    for parts in chunks:
        for _, _, steps in parts:
            count += 2 + 2 * len(steps)
    vm = pltpu.VMEM
    scratch = [
        vm((FIELDS, 4, rows), jnp.int32),
        vm((FIELDS, rows), jnp.int32),
        vm((13, rows), F32),
        vm((TASKS, rows), jnp.int32),
        vm((EXPERTS, D, 128), F32),
        vm((EXPERTS, 128, OUT), F32),
        vm((EXPERTS, 128), F32),
        vm((8, 1280), F32),
        vm((2, FIELDS, 4, rows), F32),
        vm((512, D), F32),
        vm((2, D, 512), BF),
        vm((2, POOLED, D), BF),
        vm((2, D, EXPERTS * HID), BF),
        vm((2, EXPERTS * HID + 16, D), BF),
        vm((EXPERTS * HID, 2 * OUT), BF),
        vm((2, EXPERTS, OUT, HID), BF),
        vm((TASKS * TH, 2 * OUT), BF),
        vm((D, 48), BF),
        vm((128, 128), F32),
        vm((128, 128), F32),
        vm((2, 432, rows), BF),
        vm((2, D + 16, rows), BF),
        vm((2, EXPERTS * HID, rows), BF),
        vm((2, EXPERTS * OUT, rows), BF),
        vm((2, EXPERTS * HID, rows), BF),
        vm((EXPERTS * HID, rows), F32),
        vm((TASKS, 2 * OUT, rows), BF),
        vm((TASKS, 2 * TH, rows), BF),
        vm((48, rows), BF),
        vm((128, 128), F32),
        vm((2, D, rows), BF),
        vm((2, POOLED, rows), BF),
        vm((2, size, 128), F32),
        vm((e_all, 128), F32),
        vm((2, size - e_all, 128), F32),
        vm((size, 128), F32),
        vm((size, 128), F32),
        pltpu.SemaphoreType.DMA((31,)),
        pltpu.SemaphoreType.DMA((3,)),
        pltpu.SemaphoreType.DMA((3,)),
        pltpu.SemaphoreType.DMA((places,)),
        pltpu.SemaphoreType.DMA((count,)),
    ]
    counts = [float(total_rows * c) for c in (D, EXPERTS * HID, EXPERTS * OUT, TASKS * TH)]
    return pl.pallas_call(
        functools.partial(step_kernel, n, chunks, total_rows, counts),
        out_shape=[pltpu.VMEM(shape, dtype) for shape, dtype in shapes],
        in_specs=[pl.BlockSpec(memory_space=pl.ANY)] * len(args),
        out_specs=[pl.BlockSpec(memory_space=pltpu.VMEM)] * len(shapes),
        scratch_shapes=scratch,
        compiler_params=pltpu.CompilerParams(collective_id=0, has_side_effects=True, vmem_limit_bytes=50 << 20),
        name="step",
    )(*args)


def write_kernel(*refs):
    sems = refs[-1]
    k = (len(refs) - 1) // 2
    order = sorted(range(k), key=lambda i: -math.prod(refs[i].shape))
    copies = [pltpu.make_async_copy(refs[i], refs[k + i], sems.at[i]) for i in order]
    for copy in copies:
        copy.start()
    for copy in copies:
        copy.wait()


def local(*args):
    n = lax.axis_size("dp")
    ids, lengths, dense, labels = args[:4]
    total_rows = ids.shape[0] * n
    params = [list(args[4 + 3 * k : 7 + 3 * k]) for k in range(9)]
    for k in (0, 5, 6):
        params[k] = [v.transpose(0, 2, 1) for v in params[k]]
    shapes = []
    for p in params:
        shapes += [(p[0].shape, F32)] * 3 + [(p[0].shape, BF)]
    shapes.append(((4,), F32))
    flat = [ids.transpose(1, 2, 0), lengths.T, dense.T, labels.T] + [v for p in params for v in p]
    results = step(flat, shapes, n, total_rows)
    results = [pltpu.with_memory_space_constraint(v, pltpu.VMEM) for v in results]
    outs = pl.pallas_call(
        write_kernel,
        out_shape=[jax.ShapeDtypeStruct(shape, dtype) for shape, dtype in shapes],
        in_specs=[pl.BlockSpec(memory_space=pltpu.VMEM)] * len(shapes),
        out_specs=[pl.BlockSpec(memory_space=pl.ANY)] * len(shapes),
        scratch_shapes=[pltpu.SemaphoreType.DMA((len(shapes),))],
        compiler_params=pltpu.CompilerParams(vmem_limit_bytes=1 << 20),
        name="write",
    )(*results)
    outs = list(outs)
    for k in (0, 5, 6):
        outs[4 * k : 4 * k + 4] = [v.transpose(0, 2, 1) for v in outs[4 * k : 4 * k + 4]]
    return tuple(outs)


def solution(mesh):
    up, down, bias = P(None, None, "hid"), P(None, "hid", None), P(None, "hid")
    rep = P()
    return jax.shard_map(
        local,
        mesh=mesh,
        in_specs=(P("dp", None, None), P("dp", None), P("dp", None), P("dp", None))
        + (rep,) * 6
        + (up,) * 3
        + (down,) * 3
        + (bias,) * 3
        + (rep,) * 12,
        out_specs=(rep,) * 8 + (up,) * 4 + (down,) * 4 + (bias,) * 4 + (rep,) * 17,
        check_vma=False,
    )
```

```python
import functools
import math

import jax
import jax.numpy as jnp
from jax import lax
from jax.experimental import pallas as pl
from jax.experimental.pallas import tpu as pltpu
from jax.sharding import PartitionSpec as P

D = 512
HID = 256
OUT = 128
TH = 64
TASKS = 2
EXPERTS = 4
FIELDS = 26
VOCAB = 256
EMB = 16
POOLED = 416
IN_ROWS = 429
NB = 1162

MOMENTUM_RATE = 0.9
LEARN_RATE = 0.3
AVERAGE_RATE = 0.9

BF = jnp.bfloat16
F32 = jnp.float32
NN = (((1,), (0,)), ((), ()))
NT = (((1,), (1,)), ((), ()))
MESH = pl.DeviceIdType.MESH

E_ROWS = 640
I_BASE = EXPERTS * E_ROWS
I_ROWS = 864
GATE_AT = 416
TOWER_AT = 432
MISC_AT = 496
UPB_AT = 504
T_ROWS = 512


PARTS = (
    ((640, "pz"),),
    ((640, "pz"),),
    ((640, "zxy"),),
    ((640, "xyz"),),
    ((384, "pz"), (512, "pz"),),
    ((256, "pz"), (256, "pz"),),
)
SCHEDULE = (
    "!b1",
    "!b0",
    "!b2",
    "!b3",
    "!G1",
    "!D1",
    "e1a",
    "!G0",
    "!D0",
    "e1a e0a",
    "!G2",
    "!D2",
    "e2a",
    "!G3",
    "e0a",
    "!D3",
    "e3a e2a",
    "!h0",
    "e3a",
    "!h1",
    "!i0",
    "!i1",
    "ib e1a ia",
    "!h2",
    "ib e0a",
    "!s0",
    "e3a",
    "!j0-8",
    "e1a ta e2a ia",
    "e0a",
    "!j8-13",
    "ta tb ib e3a",
    "e2a tb e1a ia",
    "ta e2a e0a ib",
    "tb e3a ia ta",
    "e2a e1a u1 ib",
    "tb e3a e2a e0a",
    "ia u0 ta tb",
    "ib e3a ib ia",
    "ia ta ui ta",
    "tb ut e2a tb",
    "u2 ur e3a u3",
)


def split(v):
    hi = v.astype(BF)
    return hi, (v - hi.astype(F32)).astype(BF)


def dot(a, b, dims):
    return lax.dot_general(a, b, dims, preferred_element_type=F32)


def blocks(size, step=128):
    return [slice(k, min(size, k + step)) for k in range(0, size, step)]


def mm(a, b, dims=NN):
    return dot(a[0], b[0], dims) + (dot(a[1], b[0], dims) + dot(a[0], b[1], dims))


def bag_counts(part_ref, f, here, width):
    row = lax.broadcasted_iota(jnp.int32, (16, width), 0).astype(F32).astype(BF)
    zero = jnp.zeros((16, width), BF)
    weights = [jnp.broadcast_to(part_ref[0, f, s : s + 1, here], (16, width)).astype(BF) for s in range(4)]
    offsets = [jnp.broadcast_to(part_ref[1, f, s : s + 1, here], (16, width)).astype(BF) - row for s in range(4)]
    low, high = [], []
    for t in range(8):
        start = jnp.full((16, width), 16 * t, BF)
        hit = [jnp.where(offsets[s] == start, weights[s], zero) for s in range(4)]
        both = (hit[0] + hit[1]) + (hit[2] + hit[3])
        whole = (both + 128.0) - 128.0
        low.append(both - whole)
        high.append(whole)
    return jnp.concatenate(low + high, 0)


def step_kernel(n, chunks, total_rows, counts, *refs):
    hbm, refs = refs[:31], refs[31:]
    outs, refs = refs[:37], refs[37:]
    ids_hbm, len_hbm, dense_hbm, lab_hbm = hbm[:4]
    up_hbm, dn_hbm, upb_hbm = hbm[10], hbm[13], hbm[16]
    params = [outs[4 * k : 4 * k + 4] for k in range(9)]
    rms_ref = outs[36]
    tab_ref, w_raw, upo_ref, dno_ref, upbo_ref, gate_ref, tw_ref, tout_ref, bias_ref = [p[0] for p in params]
    (
        ids_ref,
        len_ref,
        dense_ref,
        lab_ref,
        upx_ref,
        dnx_ref,
        upbx_ref,
        brow,
        part,
        w_in,
        w_in_t,
        w_in_b,
        up_b,
        up_t,
        dn_b,
        dn_t,
        tw_b,
        gate_t,
        cols,
        bcol,
        feat,
        x,
        h,
        bpd,
        bpu,
        dsu,
        mixed,
        bpt,
        bgl,
        row_sums,
        bi,
        bp,
        grads,
        total_e,
        total_r,
        r_core,
        r_sum,
        in_sem,
        w_send,
        w_recv,
        s_sem,
        v_sem,
    ) = refs
    dp = lax.axis_index("dp")
    hid = lax.axis_index("hid")
    core_peer = (dp, 1 - hid)

    def group(stride, size):
        me = dp // stride % size
        others = [(me + k) % size for k in range(1, size)]
        return me, [(q, (dp + (q - me) * stride, hid)) for q in others]

    groups = {"x": group(1, 2), "y": group(2, 2), "z": group(4, n // 4), "p": group(1, 4), "a": group(1, n)}

    barrier = pltpu.get_barrier_semaphore()
    kinds = {k for parts in chunks for _, _, steps in parts for k in steps}
    kinds = ["a"] if "a" in kinds else ["p", "z"]
    everyone = [core_peer] + [peer for k in kinds for _, peer in groups[k][1]]
    for peer in everyone:
        pl.semaphore_signal(barrier, inc=1, device_id=peer, device_id_type=MESH)

    rows = ids_ref.shape[2]
    lanes = pl.ds(pl.multiple_of(hid * rows, rows), rows)
    order = (0, 1, 2, 3, 4, 5, 6, 7, 8)
    pairs = [(ids_hbm.at[:, :, lanes], ids_ref), (len_hbm.at[:, lanes], len_ref)]
    pairs += [(hbm[4 + 3 * k], params[k][0]) for k in order]
    pairs += [(dense_hbm.at[:, lanes], dense_ref), (lab_hbm.at[:, lanes], lab_ref)]
    for j in (1, 2):
        pairs += [(hbm[4 + 3 * k + j], params[k][j]) for k in order]
    loads = [pltpu.make_async_copy(src, dst, in_sem.at[k]) for k, (src, dst) in enumerate(pairs)]
    for load in loads[:13]:
        load.start()

    def remote(src, dst, send, recv, peer):
        return pltpu.make_async_remote_copy(
            src_ref=src, dst_ref=dst, send_sem=send, recv_sem=recv, device_id=peer, device_id_type=MESH
        )

    loads[0].wait()
    loads[1].wait()
    slot = lax.broadcasted_iota(jnp.int32, (4, rows), 0)
    for f in range(FIELDS):
        used = jnp.broadcast_to(len_ref[f : f + 1, :], (4, rows)) > slot
        ident = ids_ref[f]
        part[0, f] = jnp.where(used, jnp.where(ident < 128, 0.0625, 1.0), 0.0)
        part[1, f] = jnp.bitwise_and(ident, 127).astype(F32)
    loads[2].wait()

    sixteen = jnp.where(lax.broadcasted_iota(jnp.int32, (EMB, VOCAB), 1) < 128, 16.0, 1.0)
    width = 256

    def pool_field(f):
        table = jnp.concatenate(split(tab_ref[f] * sixteen), 0)
        at = slice(EMB * f, EMB * f + EMB)
        for j in range(rows // width):
            here = slice(width * j, width * (j + 1))
            both = dot(table, bag_counts(part, f, here, width), NN)
            hi, lo = split(both[0:EMB] + both[EMB : 2 * EMB])
            feat[0, at, here] = hi
            feat[1, at, here] = lo

    for f in range(13):
        pool_field(f)
    pl.semaphore_wait(barrier, len(everyone))
    weights = [
        remote(src, dst, w_send.at[k], w_recv.at[k], core_peer)
        for k, (src, dst) in enumerate(((up_hbm, upx_ref), (dn_hbm, dnx_ref), (upb_hbm, upbx_ref)))
    ]
    for copy in weights:
        copy.start()
    for f in range(13, FIELDS):
        pool_field(f)
    for load in loads[13:]:
        load.start()
    for load in loads[3:13]:
        load.wait()

    brow[0:1, 0:1024] = bias_ref[0:1024].reshape(1, 1024)
    brow[0:1, 1024:NB] = bias_ref[1024:NB].reshape(1, NB - 1024)
    biases = brow[0:1, 0:NB]
    row = lax.broadcasted_iota(jnp.int32, (8, D), 0)
    in_bias = jnp.broadcast_to(biases[:, 0:D], (8, D))
    w_in[0:IN_ROWS, :] = w_raw[...]
    w_in[424:432, :] = jnp.where(row == 5, in_bias, jnp.where(row < 5, w_in[424:432, :], 0.0))
    w_in[432:512, :] = jnp.zeros((80, D), F32)
    for i in range(4):
        hi, lo = split(w_in[128 * i : 128 * (i + 1), :].T)
        w_in_t[0, :, 128 * i : 128 * (i + 1)] = hi
        w_in_t[1, :, 128 * i : 128 * (i + 1)] = lo
    hi, lo = split(w_in[0:POOLED, :])
    w_in_b[0] = hi
    w_in_b[1] = lo

    def expert_weights(k, up_ref, dn_ref):
        for e in range(EXPERTS):
            c = 256 * e + 128 * k
            up, down = up_ref[e], dn_ref[e]
            hi, lo = split(up)
            up_b[0, :, c : c + 128] = hi
            up_b[1, :, c : c + 128] = lo
            hi, lo = split(up.T)
            up_t[0, c : c + 128, :] = hi
            up_t[1, c : c + 128, :] = lo
            hi, lo = split(down)
            dn_b[c : c + 128, 0:128] = hi
            dn_b[c : c + 128, 128:256] = lo
            hi, lo = split(down.T)
            dn_t[0, e, :, 128 * k : 128 * k + 128] = hi
            dn_t[1, e, :, 128 * k : 128 * k + 128] = lo

    expert_weights(0, upo_ref, dno_ref)
    gate8 = jnp.concatenate([gate_ref[0], gate_ref[1]], 0)
    hi, lo = split(jnp.concatenate([gate8, jnp.zeros((8, D), F32)], 0))
    up_t[0, 1024:1040, :] = hi
    up_t[1, 1024:1040, :] = lo
    for i in range(4):
        tile = jnp.concatenate([gate8[:, 128 * i : 128 * (i + 1)], jnp.zeros((120, 128), F32)], 0).T
        hi, lo = split(tile)
        at = slice(128 * i, 128 * (i + 1))
        gate_t[at, 0:16] = hi[:, 0:16]
        gate_t[at, 16:32] = hi[:, 0:16]
        gate_t[at, 32:48] = lo[:, 0:16]
    for t in range(TASKS):
        hi, lo = split(tw_ref[t])
        tw_b[TH * t : TH * t + TH, 0:128] = hi
        tw_b[TH * t : TH * t + TH, 128:256] = lo
    tw_t = split(jnp.concatenate([tw_ref[0], tw_ref[1]], 0).T)
    x[0, D : D + 16, :] = jnp.ones((16, rows), BF)
    x[1, D : D + 16, :] = jnp.zeros((16, rows), BF)
    hi, lo = split(jnp.concatenate([dense_ref[...], jnp.ones((1, rows), F32), jnp.zeros((2, rows), F32)], 0))
    feat[0, POOLED:432, :] = hi
    feat[1, POOLED:432, :] = lo

    scale = float(total_rows) ** -0.5
    fs = (feat[0], feat[1])
    xv = mm((w_in_t[0, :, 0:432], w_in_t[1, :, 0:432]), fs)
    squares = [jnp.sum(xv * xv, keepdims=True)]
    xs = split(xv)
    x[0, 0:D, :] = xs[0]
    x[1, 0:D, :] = xs[1]
    for copy in weights:
        copy.wait_recv()
    expert_weights(1, upx_ref, dnx_ref)
    bcol[...] = jnp.zeros((128, 128), F32)
    bcol[0:4, :] = upbo_ref[...]
    bcol[4:8, :] = upbx_ref[...]
    for e in range(EXPERTS):
        bcol[8 + e : 9 + e, :] = biases[:, 512 + 128 * e : 640 + 128 * e]
    bcol[12:13, :] = biases[:, 1032:1160]
    bcol[13:14, 0:64] = tout_ref[0:1, :]
    bcol[13:14, 64:128] = tout_ref[1:2, :]
    bcol[14:15, 0:8] = biases[:, 1024:1032]
    cols[...] = bcol[...].T
    row_sums[...] = jnp.zeros((128, 128), F32)

    eouts, slopes = [], []
    sums = [0.0, 0.0, 0.0]
    for e in range(EXPERTS):
        c = 256 * e
        end = c + 256 if e < EXPERTS - 1 else c + 272
        pre = mm((up_t[0, c:end, :], up_t[1, c:end, :]), xs)
        gate_logits = pre[256:264] + cols[0:8, 14:15] if e == EXPERTS - 1 else None
        pre = pre[0:256] + jnp.concatenate([cols[:, e : e + 1], cols[:, 4 + e : 5 + e]], 0)
        s = jax.nn.sigmoid(pre)
        hv = pre * s
        dsu[c : c + 256, :] = s + hv * (1.0 - s)
        sums[0] = sums[0] + jnp.sum(hv * hv, keepdims=True)
        hs = split(hv)
        h[0, c : c + 256, :] = hs[0]
        h[1, c : c + 256, :] = hs[1]
        pre = mm((dn_t[0, e], dn_t[1, e]), hs) + cols[:, 8 + e : 9 + e]
        s = jax.nn.sigmoid(pre)
        out = pre * s
        sums[1] = sums[1] + jnp.sum(out * out, keepdims=True)
        eouts.append(out)
        slopes.append(s + out * (1.0 - s))
    gates = []
    for t in range(TASKS):
        r = [gate_logits[4 * t + e : 4 * t + e + 1] for e in range(EXPERTS)]
        top = jnp.maximum(jnp.maximum(r[0], r[1]), jnp.maximum(r[2], r[3]))
        ex = [jnp.exp(v - top) for v in r]
        inv = 1.0 / ((ex[0] + ex[1]) + (ex[2] + ex[3]))
        gates.append([v * inv for v in ex])
    back_mixed, back_logit = [], []
    for t in range(TASKS):
        z = slice(TH * t, TH * t + TH)
        o = slice(OUT * t, OUT * t + OUT)
        g = gates[t]
        ms = split(g[0] * eouts[0] + g[1] * eouts[1] + g[2] * eouts[2] + g[3] * eouts[3])
        mixed[t, 0:OUT, :] = ms[0]
        mixed[t, OUT : 2 * OUT, :] = ms[1]
        w = tw_b[z, :]
        pre = dot(w, jnp.concatenate([ms[0], ms[0]], 0), NN) + dot(w[:, 0:128], ms[1], NN) + cols[z, 12:13]
        s = jax.nn.sigmoid(pre)
        th = pre * s
        sums[2] = sums[2] + jnp.sum(th * th, keepdims=True)
        wo = cols[z, 13:14]
        logit = jnp.sum(th * wo, axis=0, keepdims=True) + biases[:, 1160 + t : 1161 + t]
        back = (jax.nn.sigmoid(logit) - lab_ref[t : t + 1, :].astype(F32)) * scale
        row_sums[z, 5:6] = jnp.sum(back * th, axis=1, keepdims=True)
        row_sums[8 + t : 9 + t, 6:7] = jnp.sum(back, axis=1, keepdims=True)
        back = back * wo * (s + th * (1.0 - s))
        row_sums[z, 4:5] = jnp.sum(back, axis=1, keepdims=True)
        bs = split(back)
        bpt[t, 0:TH, :] = bs[0]
        bpt[t, TH : 2 * TH, :] = bs[1]
        w = [v[:, z] for v in tw_t]
        bm = dot(jnp.concatenate([w[0], w[1], w[0]], 1), jnp.concatenate([bs[0], bs[0], bs[1]], 0), NN)
        back_mixed.append(bm)
        bg = [jnp.sum(bm * eouts[e], axis=0, keepdims=True) for e in range(EXPERTS)]
        mean = g[0] * bg[0] + g[1] * bg[1] + g[2] * bg[2] + g[3] * bg[3]
        back_logit += [g[e] * (bg[e] - mean) for e in range(EXPERTS)]
    back_logit = jnp.concatenate(back_logit, 0)
    row_sums[0:8, 6:7] = jnp.sum(back_logit, axis=1, keepdims=True)
    bs = split(jnp.concatenate([back_logit, jnp.zeros((8, rows), F32)], 0))
    bgl[0:16] = bs[0]
    bgl[16:32] = bs[1]
    bgl[32:48] = bs[0]
    squares += sums

    def expert_back(e):
        c = 256 * e
        back = (gates[0][e] * back_mixed[0] + gates[1][e] * back_mixed[1]) * slopes[e]
        row_sums[:, e : e + 1] = jnp.sum(back, axis=1, keepdims=True)
        bs = split(back)
        bpd[0, OUT * e : OUT * e + OUT, :] = bs[0]
        bpd[1, OUT * e : OUT * e + OUT, :] = bs[1]
        w = dn_b[c : c + 256, :]
        back = dot(w, jnp.concatenate([bs[0], bs[0]], 0), NN) + dot(w[:, 0:128], bs[1], NN)
        bs = split(back * dsu[c : c + 256, :])
        bpu[0, c : c + 256, :] = bs[0]
        bpu[1, c : c + 256, :] = bs[1]

    rep_base = chunks[EXPERTS][0][0]
    used = {"sem": 0, "row": 0}

    def sems(count):
        first = used["sem"]
        used["sem"] += count
        return first

    class Piece:
        def __init__(self, place, base, size, steps, expert):
            self.place, self.base, self.size, self.expert = place, base, size, expert
            self.steps = [groups[k] for k in steps]
            self.sent = 0
            self.plan = self.stages()

        def at(self, start, size):
            return pl.ds(pl.multiple_of(start, 8), size)

        def total(self, start, size):
            if self.expert:
                return total_e.at[self.at(start, size)]
            return total_r.at[hid, self.at(start - rep_base, size)]

        def start(self, copies, rows):
            k = sems(1)
            for src, dst, peer in copies:
                remote(src, dst, s_sem.at[self.place], v_sem.at[k], peer).start()
            self.sent += rows
            return remote(r_core.at[pl.ds(0, rows)], r_core.at[pl.ds(0, rows)], s_sem.at[self.place], v_sem.at[k], core_peer)

        def stages(self):
            rng = self.at(self.base, self.size)
            yield self.start([(grads.at[1, rng], r_core.at[rng], core_peer)], self.size)
            grads[0, rng, :] += r_core[rng, :]
            start, size, held = self.base, self.size, []
            for me, others in self.steps:
                m = len(others) + 1
                held.append((start, size))
                size //= m
                row = used["row"]
                used["row"] += (m - 1) * size
                copies = []
                for j, (q, peer) in enumerate(others):
                    src, dst = self.at(start + q * size, size), self.at(row + (m - 2 - j) * size, size)
                    copies.append((grads.at[0, src], r_sum.at[dst], peer))
                yield self.start(copies, (m - 1) * size)
                start = start + me * size
                mine = self.at(start, size)
                total = grads[0, mine, :]
                for slot in range(m - 1):
                    total = total + r_sum[row + slot * size : row + slot * size + size, :]
                if len(held) < len(self.steps):
                    grads[0, mine, :] = total
                else:
                    self.total(start, size)[...] = total
            for me, others in reversed(self.steps):
                out = self.total(start, size)
                yield self.start([(out, out, peer) for _, peer in others], len(others) * size)
                start, size = held.pop()
            if not self.expert:
                out = self.total(self.base, self.size)
                yield self.start([(out, out, core_peer)], self.size)

        def advance(self):
            if self.step is not None:
                self.step.wait_recv()
            self.step = next(self.plan, None)

        step = None

        def end(self):
            rows = pl.ds(0, self.sent)
            remote(r_sum.at[rows], r_sum.at[rows], s_sem.at[self.place], v_sem.at[0], core_peer).wait_send()

    names = ("e0", "e1", "e2", "e3", "i", "t")
    pieces = {}
    for k, (name, parts) in enumerate(zip(names, chunks)):
        for j, (base, size, steps) in enumerate(parts):
            pieces[name + "abcd"[j]] = Piece(len(pieces), base, size, steps, k < EXPERTS)

    def owner(k):
        return (k + hid) % 2

    e_base = [chunks[e][0][0] for e in range(EXPERTS)]
    e_size = chunks[1][0][0] - chunks[0][0][0]
    i_base, t_base = chunks[EXPERTS][0][0], chunks[EXPERTS + 1][0][0]
    t_size = grads.shape[1] - t_base
    misc = t_base + MISC_AT
    grads[:, misc : t_base + t_size, :] = jnp.zeros((2, t_size - MISC_AT, 128), F32)

    def update(k, at, g):
        w_ref, m_ref, a_ref, r_ref = params[k]
        new_m = MOMENTUM_RATE * m_ref[at] + g
        new_w = w_ref[at] - LEARN_RATE * (g + MOMENTUM_RATE * new_m)
        w_ref[at] = new_w
        m_ref[at] = new_m
        a_ref[at] = AVERAGE_RATE * a_ref[at] + (1.0 - AVERAGE_RATE) * new_w
        r_ref[at] = new_w.astype(BF)

    everything = slice(None)
    to = t_base - rep_base

    def update_expert(e):
        update(2, (e,), total_e[e_base[e] : e_base[e] + D, :])
        update(3, (e,), total_e[e_base[e] + D : e_base[e] + E_ROWS, :])

    def update_inputs():
        for k in range(4):
            at = 432 * (k % 2)
            update(1, (everything, slice(128 * k, 128 * k + 128)), total_r[k // 2, at : at + IN_ROWS, :])

    def update_tables(first, last):
        for f in range(first, last):
            for k in range(2):
                g = total_r[k, to + EMB * f : to + EMB * f + EMB, :]
                update(0, (f, everything, slice(128 * k, 128 * k + 128)), g)

    def update_rest():
        update(4, (everything,), total_r[hid, to + UPB_AT : to + UPB_AT + 4, :])
        for k in range(4):
            at = to + GATE_AT + 8 * (k % 2)
            for s in range(TASKS):
                g = total_r[k // 2, at + 4 * s : at + 4 * s + 4, :]
                update(5, (s, everything, slice(128 * k, 128 * k + 128)), g)
        for s in range(TASKS):
            update(6, (s,), total_r[s, to + TOWER_AT : to + TOWER_AT + TH, :])
        at = to + MISC_AT
        g = total_r[0, at + 5 : at + 6, :]
        for s in range(TASKS):
            update(7, (slice(s, s + 1), everything), g[:, TH * s : TH * s + TH])
        for k in range(4):
            r = 432 * (k % 2) + IN_ROWS
            brow[0:1, 128 * k : 128 * k + 128] = total_r[k // 2, r : r + 1, :]
            brow[0:1, D + 128 * k : D + 128 * k + 128] = total_r[0, at + k : at + k + 1, :]
        brow[0:1, 1024:1032] = total_r[0, at + 6 : at + 7, 0:8]
        brow[0:1, 1032:1160] = total_r[0, at + 4 : at + 5, :]
        brow[0:1, 1160:1162] = total_r[0, at + 6 : at + 7, 8:10]
        update(8, (everything,), brow[0, 0:NB])
        lane = lax.broadcasted_iota(jnp.int32, (1, 128), 1)
        inverse = jnp.zeros((1, 128), F32)
        for k, count in enumerate(counts):
            inverse = jnp.where(lane == k, 1.0 / count, inverse)
        brow[1:2, 0:128] = jnp.sqrt(total_r[0, at + 7 : at + 8, :] * inverse + 1e-06)
        rms_ref[...] = brow[1, 0:4]

    updates = {f"u{e}": functools.partial(update_expert, e) for e in range(EXPERTS)}
    table_split = FIELDS if len(chunks[5]) == 1 else min(FIELDS, sum(part[1] for part in chunks[5][:-1]) // EMB)
    updates["ui"] = update_inputs
    updates["ut"] = functools.partial(update_tables, 0, table_split)
    updates["ur"] = lambda: (update_tables(table_split, FIELDS), update_rest())

    done = set()

    def run(*steps):
        for name in steps:
            if name in updates:
                if not done:
                    for load in loads[13:]:
                        load.wait()
                done.add(name)
                updates[name]()
            elif name in pieces:
                pieces[name].advance()

    def first_gradients(e):
        c, base = 256 * e, e_base[e]
        g = mm((x[0], x[1]), (bpu[0, c : c + 256, :], bpu[1, c : c + 256, :]), NT)
        grads[0, base : base + D, :] = g[0:D, 0:128]
        grads[1, base : base + D, :] = g[0:D, 128:256]
        upb = t_base + UPB_AT + e
        grads[0, upb : upb + 1, :] = g[D : D + 1, 0:128]
        grads[1, upb : upb + 1, :] = g[D : D + 1, 128:256]

    def second_gradients(e):
        c, o, base = 256 * e, 128 * e, e_base[e]
        hi, lo = bpd[0, o : o + 128, :], bpd[1, o : o + 128, :]
        g = dot(h[0, c : c + 256, :], jnp.concatenate([hi, lo], 0), NT)
        g = (g[:, 0:128] + g[:, 128:256]) + dot(h[1, c : c + 256, :], hi, NT)
        grads[0, base + D : base + E_ROWS, :] = g[0:128]
        grads[1, base + D : base + E_ROWS, :] = g[128:256]
        if e_size > E_ROWS:
            grads[:, base + E_ROWS : base + e_size, :] = jnp.zeros((2, e_size - E_ROWS, 128), F32)

    inputs_parts = []

    def inputs_back(k):
        if k < 2:
            for at in blocks(D)[2 * k : 2 * k + 2]:
                b = mm((up_b[0, at, :], up_b[1, at, :]), (bpu[0], bpu[1])) + dot(gate_t[at, :], bgl[...], NN)
                inputs_parts.append(split(b))
                bi[0, at, :] = inputs_parts[-1][0]
                bi[1, at, :] = inputs_parts[-1][1]
            return
        bs = [jnp.concatenate([p[j] for p in inputs_parts], 0) for j in range(2)]
        for at in blocks(POOLED):
            ps = split(mm((w_in_b[0, at, :], w_in_b[1, at, :]), bs))
            bp[0, at, :] = ps[0]
            bp[1, at, :] = ps[1]

    def input_gradients(k):
        g = mm((feat[0], feat[1]), (bi[0, 256 * k : 256 * k + 256, :], bi[1, 256 * k : 256 * k + 256, :]), NT)
        grads[owner(k), i_base : i_base + 432, :] = g[:, 0:128]
        grads[owner(k), i_base + 432 : i_base + I_ROWS, :] = g[:, 128:256]
        if t_base - i_base > I_ROWS:
            grads[:, i_base + I_ROWS : t_base, :] = jnp.zeros((2, t_base - i_base - I_ROWS, 128), F32)

    def small_gradients():
        g = dot(x[0], bgl[0:32], NT)
        g = g[0:D, 0:8] + g[0:D, 16:24] + dot(x[1], bgl[0:16], NT)[0:D, 0:8]
        for k in range(4):
            tile = jnp.concatenate([g[128 * k : 128 * k + 128], jnp.zeros((128, 120), F32)], 1).T
            at = t_base + GATE_AT + 8 * (k % 2)
            grads[owner(k // 2), at : at + 8, :] = tile[0:8]
        for t in range(TASKS):
            g = dot(bpt[t], mixed[t], NT)
            g = (g[0:TH, 0:OUT] + g[0:TH, OUT : 2 * OUT]) + g[TH : 2 * TH, 0:OUT]
            grads[owner(t), t_base + TOWER_AT : t_base + TOWER_AT + TH, :] = g
        lane = lax.broadcasted_iota(jnp.int32, (1, 128), 1)
        m = owner(0)
        grads[m, misc : misc + 8, :] = row_sums[...].T[0:8]
        total = jnp.zeros((1, 128), F32)
        for k in range(4):
            total = jnp.where(lane == k, squares[k], total)
        grads[m, misc + 7 : misc + 8, :] = total

    def tables(first, last):
        for f in range(2 * first, 2 * last):
            at = slice(EMB * f, EMB * f + EMB)
            total = jnp.zeros((2 * EMB, VOCAB), F32)
            for j in range(rows // width):
                here = slice(width * j, width * (j + 1))
                back = jnp.concatenate([bp[0, at, here], bp[1, at, here]], 0)
                total = total + dot(back, bag_counts(part, f, here, width), NT)
            g = (total[0:EMB] + total[EMB : 2 * EMB]) * sixteen
            at = slice(t_base + EMB * f, t_base + EMB * f + EMB)
            grads[owner(0), at, :] = g[:, 0:128]
            grads[owner(1), at, :] = g[:, 128:256]

    work = {
        "b": expert_back,
        "G": first_gradients,
        "D": second_gradients,
        "h": inputs_back,
        "i": input_gradients,
        "s": lambda k: small_gradients(),
    }
    for item in SCHEDULE:
        if item[0:2] == "!j":
            tables(*[int(v) for v in item[2:].split("-")])
        elif item[0] == "!":
            work[item[1]](int(item[2]))
        else:
            run(*item.split())
    while any(piece.step for piece in pieces.values()):
        run(*[name for name in pieces if pieces[name].step])
    run(*[name for name in updates if name not in done])
    for copy in weights:
        copy.wait_send()
    for piece in pieces.values():
        piece.end()


def layout(n):
    unit = 8 * n
    chunks, base = [], 0
    for size, parts in zip([E_ROWS] * EXPERTS + [I_ROWS, T_ROWS], PARTS):
        left = -(-size // unit) * unit
        pieces = []
        for j, (rows, steps) in enumerate(parts):
            take = left if j == len(parts) - 1 else min(left, -(-rows // unit) * unit)
            if take:
                pieces.append((base, take, steps))
            base += take
            left -= take
        chunks.append(pieces)
    return chunks, base


def step(args, shapes, n, total_rows):
    rows = args[0].shape[2] // 2
    chunks, size = layout(n)
    e_all = chunks[EXPERTS][0][0]
    count, places = 0, sum(len(parts) for parts in chunks)
    for parts in chunks:
        for _, _, steps in parts:
            count += 2 + 2 * len(steps)
    vm = pltpu.VMEM
    scratch = [
        vm((FIELDS, 4, rows), jnp.int32),
        vm((FIELDS, rows), jnp.int32),
        vm((13, rows), F32),
        vm((TASKS, rows), jnp.int32),
        vm((EXPERTS, D, 128), F32),
        vm((EXPERTS, 128, OUT), F32),
        vm((EXPERTS, 128), F32),
        vm((8, 1280), F32),
        vm((2, FIELDS, 4, rows), F32),
        vm((512, D), F32),
        vm((2, D, 512), BF),
        vm((2, POOLED, D), BF),
        vm((2, D, EXPERTS * HID), BF),
        vm((2, EXPERTS * HID + 16, D), BF),
        vm((EXPERTS * HID, 2 * OUT), BF),
        vm((2, EXPERTS, OUT, HID), BF),
        vm((TASKS * TH, 2 * OUT), BF),
        vm((D, 48), BF),
        vm((128, 128), F32),
        vm((128, 128), F32),
        vm((2, 432, rows), BF),
        vm((2, D + 16, rows), BF),
        vm((2, EXPERTS * HID, rows), BF),
        vm((2, EXPERTS * OUT, rows), BF),
        vm((2, EXPERTS * HID, rows), BF),
        vm((EXPERTS * HID, rows), F32),
        vm((TASKS, 2 * OUT, rows), BF),
        vm((TASKS, 2 * TH, rows), BF),
        vm((48, rows), BF),
        vm((128, 128), F32),
        vm((2, D, rows), BF),
        vm((2, POOLED, rows), BF),
        vm((2, size, 128), F32),
        vm((e_all, 128), F32),
        vm((2, size - e_all, 128), F32),
        vm((size, 128), F32),
        vm((size, 128), F32),
        pltpu.SemaphoreType.DMA((31,)),
        pltpu.SemaphoreType.DMA((3,)),
        pltpu.SemaphoreType.DMA((3,)),
        pltpu.SemaphoreType.DMA((places,)),
        pltpu.SemaphoreType.DMA((count,)),
    ]
    counts = [float(total_rows * c) for c in (D, EXPERTS * HID, EXPERTS * OUT, TASKS * TH)]
    return pl.pallas_call(
        functools.partial(step_kernel, n, chunks, total_rows, counts),
        out_shape=[pltpu.VMEM(shape, dtype) for shape, dtype in shapes],
        in_specs=[pl.BlockSpec(memory_space=pl.ANY)] * len(args),
        out_specs=[pl.BlockSpec(memory_space=pltpu.VMEM)] * len(shapes),
        scratch_shapes=scratch,
        compiler_params=pltpu.CompilerParams(collective_id=0, has_side_effects=True, vmem_limit_bytes=50 << 20),
        name="step",
    )(*args)


def write_kernel(*refs):
    sems = refs[-1]
    k = (len(refs) - 1) // 2
    order = sorted(range(k), key=lambda i: -math.prod(refs[i].shape))
    copies = [pltpu.make_async_copy(refs[i], refs[k + i], sems.at[i]) for i in order]
    for copy in copies:
        copy.start()
    for copy in copies:
        copy.wait()


def local(*args):
    n = lax.axis_size("dp")
    ids, lengths, dense, labels = args[:4]
    total_rows = ids.shape[0] * n
    params = [list(args[4 + 3 * k : 7 + 3 * k]) for k in range(9)]
    for k in (0, 5, 6):
        params[k] = [v.transpose(0, 2, 1) for v in params[k]]
    shapes = []
    for p in params:
        shapes += [(p[0].shape, F32)] * 3 + [(p[0].shape, BF)]
    shapes.append(((4,), F32))
    flat = [ids.transpose(1, 2, 0), lengths.T, dense.T, labels.T] + [v for p in params for v in p]
    results = step(flat, shapes, n, total_rows)
    results = [pltpu.with_memory_space_constraint(v, pltpu.VMEM) for v in results]
    outs = pl.pallas_call(
        write_kernel,
        out_shape=[jax.ShapeDtypeStruct(shape, dtype) for shape, dtype in shapes],
        in_specs=[pl.BlockSpec(memory_space=pltpu.VMEM)] * len(shapes),
        out_specs=[pl.BlockSpec(memory_space=pl.ANY)] * len(shapes),
        scratch_shapes=[pltpu.SemaphoreType.DMA((len(shapes),))],
        compiler_params=pltpu.CompilerParams(vmem_limit_bytes=1 << 20),
        name="write",
    )(*results)
    outs = list(outs)
    for k in (0, 5, 6):
        outs[4 * k : 4 * k + 4] = [v.transpose(0, 2, 1) for v in outs[4 * k : 4 * k + 4]]
    return tuple(outs)


def solution(mesh):
    up, down, bias = P(None, None, "hid"), P(None, "hid", None), P(None, "hid")
    rep = P()
    return jax.shard_map(
        local,
        mesh=mesh,
        in_specs=(P("dp", None, None), P("dp", None), P("dp", None), P("dp", None))
        + (rep,) * 6
        + (up,) * 3
        + (down,) * 3
        + (bias,) * 3
        + (rep,) * 12,
        out_specs=(rep,) * 8 + (up,) * 4 + (down,) * 4 + (bias,) * 4 + (rep,) * 17,
        check_vma=False,
    )
```
